32 devices in a mesh: dp: 16 (over z, y, x), task: 2 (over core).
Axes of the slice: x: 2, y: 2, z: 4, core: 2. Of those that a mesh axis runs over, the one named last changes fastest.
Arguments:
- images: bfloat16 [64, 16, 16, 2048], P(('dp', 'task')), may hold values from -14 to 14
- bucket_shape: int32 [64, 2], P(('dp', 'task')), may hold values from 8 to 16, as said below
- pixel_mask: int32 [64, 16, 16], P(('dp', 'task')), may hold values from 0 to 1
- thresholds: int32 [64, 16, 16, 2048], P(('dp', 'task')), may hold values from 0 to 4095
- reduce_weight: bfloat16 [2048, 512], replicated, may hold values from -0.125 to 0.125
- spatial_weight: bfloat16 [9, 512, 512], replicated, may hold values from -0.09375 to 0.09375
- expand_weight: bfloat16 [512, 2048], replicated, may hold values from -0.25 to 0.25
- mid_gains: float32 [2, 512], replicated, may hold values from 0.5 to 2
- mid_biases: float32 [2, 512], replicated, may hold values from -1 to 1
- out_gain: float32 [2048], replicated, may hold values from 0.5 to 2
- out_bias: float32 [2048], replicated, may hold values from -1 to 1
- head_weights: bfloat16 [2048, 3, 2048], P(None, None, 'task'), may hold values from -0.125 to 0.125
- head_cotangent: bfloat16 [64, 16, 16, 3, 2048], P('dp', None, None, None, 'task'), may hold values from -6 to 6
Outputs:
- head_output: bfloat16 [64, 16, 16, 3, 2048], P('dp', None, None, None, 'task')
- images_grad: float32 [64, 16, 16, 2048], P(('dp', 'task'))
- reduce_grad: float32 [2048, 512], P(('dp', 'task'))
- spatial_grad: float32 [9, 512, 512], P(None, ('dp', 'task'))
- expand_grad: float32 [512, 2048], P(('dp', 'task'))
- gains_grad: float32 [2, 512], replicated
- biases_grad: float32 [2, 512], replicated
- outgain_grad: float32 [2048], replicated
- outbias_grad: float32 [2048], replicated
- heads_grad: float32 [2048, 3, 2048], P('dp', None, 'task')
The draws below stay inside these ranges and needn't reach their ends.
Inputs may be any that keep to these rules, and one draw needn't show every extreme that they name: `bucket_shape`: each image's valid rows and columns, from a few aspect buckets; an image's valid region is the top left corner of its grid.
All inputs are finite; a program needn't handle non-finite values.
Results may differ from the reference program's by a relative error of at most 0.015.
Values may be sent and summed in bfloat16 or wider, within the bound.
No kernel may reach another device: no remote copies, remote signals or barrier semaphores. Data moves between devices by JAX's collectives and lax.ppermute only.
A program may use at most 192 MiB of HBM per device.

```python
import math
from functools import partial
import jax
import jax.numpy as jnp
from jax import lax

C = 2048
MID = 512
TASKS = 3
SIDE = 16
IMAGES = 64


def draw_images(key, part):
    key = jax.random.fold_in(key, 11)
    first, second = jax.random.split(key)
    offsets = jnp.clip(0.5 * jax.random.normal(second, (C,), jnp.float32), -1.5, 1.5)
    ramp = jnp.arange(IMAGES, dtype=jnp.float32) / max(IMAGES - 1, 1)
    noise = jnp.clip(jax.random.normal(first, (IMAGES, SIDE, SIDE, C), jnp.float32), -4.0, 4.0)
    scales = 1.0 + 2.0 * ramp
    return (scales[:, None, None, None] * noise + offsets).astype(jnp.bfloat16)


def draw_pixel_mask(key, part):
    key = jax.random.fold_in(key, 23)
    ramp = jnp.arange(IMAGES, dtype=jnp.int32)
    limits = 300 + 600 * ramp // max(IMAGES - 1, 1)
    rolls = jax.random.randint(key, (IMAGES, SIDE, SIDE), 0, 1000)
    return (rolls < limits[:, None, None]).astype(jnp.int32)


def draw_bucket_shape(key, part):
    key = jax.random.fold_in(key, 37)
    first, second, third = jax.random.split(key, 3)
    picks = jax.random.randint(first, (IMAGES,), 0, 6)
    whole_image = jax.random.randint(second, (), 0, IMAGES)
    narrow_image = (whole_image + 1 + jax.random.randint(third, (), 0, IMAGES - 1)) % IMAGES
    picks = picks.at[whole_image].set(0).at[narrow_image].set(3)
    heights = jnp.array([SIDE, SIDE, 3 * SIDE // 4, SIDE, SIDE // 2, 3 * SIDE // 4], jnp.int32)
    widths = jnp.array([SIDE, 3 * SIDE // 4, SIDE, SIDE // 2, SIDE, 3 * SIDE // 4], jnp.int32)
    return jnp.stack([heights[picks], widths[picks]], axis=1)


def plant(drawn, stream_key, smallest, high):
    place = [jax.random.randint(jax.random.fold_in(stream_key, axis), (), 0, length) for axis, length in enumerate(drawn.shape)]
    widest = drawn.shape.index(max(drawn.shape))
    next_to = place[:widest] + [(place[widest] + 1) % drawn.shape[widest]] + place[widest + 1:]
    return drawn.at[tuple(place)].set(smallest).at[tuple(next_to)].set(high)


def shard_levels(key, extent, pieces, smallest, top_value):
    level = 1.0
    for position, parts in pieces:
        steps = jax.random.uniform(jax.random.fold_in(jax.random.fold_in(key, 6), position), (parts,), jnp.float32, smallest / len(pieces), top_value / len(pieces))
        level = level * jnp.repeat(jnp.exp(steps), extent[position] // parts).reshape((-1,) + (1,) * (len(extent) - 1 - position))
    return level


def centred(stream_key, shape, scale, limit, cuts=(), held_as=jnp.bfloat16):
    values = scale * jax.random.normal(stream_key, shape, jnp.float32)
    if cuts:
        values = values * shard_levels(stream_key, shape, cuts, -0.22, 0.18)
    return jnp.clip(values, -limit, limit).astype(held_as)


def setup_inputs(seed: int = 0) -> dict:
    streams_of = jax.random.split(jax.random.key(seed), 14)
    return {
        "images": draw_images(jax.random.fold_in(streams_of[13], 71), 0),
        "bucket_shape": draw_bucket_shape(jax.random.fold_in(streams_of[13], 71), 0),
        "pixel_mask": draw_pixel_mask(jax.random.fold_in(streams_of[13], 71), 0),
        "thresholds": plant(jax.random.randint(streams_of[3], (IMAGES, SIDE, SIDE, C), 0, 4096), jax.random.fold_in(streams_of[3], 1), 0, 4095).astype(jnp.int32),
        "reduce_weight": centred(streams_of[4], (C, MID), C ** -0.5, 0.125),
        "spatial_weight": centred(streams_of[5], (9, MID, MID), (9 * MID) ** -0.5, 0.09375),
        "expand_weight": centred(streams_of[6], (MID, C), MID ** -0.5, 0.25),
        "mid_gains": jnp.clip(jnp.exp(jax.random.uniform(streams_of[7], (2, MID), jnp.float32, math.log(0.5), math.log(2.0))), 0.5, 2.0),
        "mid_biases": jnp.clip(jax.random.uniform(streams_of[8], (2, MID), jnp.float32, -1.0, 1.0), -1.0, 1.0),
        "out_gain": jnp.clip(jnp.exp(jax.random.uniform(streams_of[9], (C,), jnp.float32, math.log(0.5), math.log(2.0))), 0.5, 2.0),
        "out_bias": jnp.clip(jax.random.uniform(streams_of[10], (C,), jnp.float32, -1.0, 1.0), -1.0, 1.0),
        "head_weights": centred(streams_of[11], (C, TASKS, C), C ** -0.5, 0.125, ((2, 2),)),
        "head_cotangent": centred(streams_of[12], (IMAGES, SIDE, SIDE, TASKS, C), 1.0, 6.0, ((0, 16), (4, 2))),
    }


@jax.custom_vjp
def low(v):
    return lax.optimization_barrier(v.astype(jnp.bfloat16)).astype(jnp.float32)

@jax.custom_vjp
def low_back(v):
    return v

def low_keep(v):
    return (low(v), None)

def low_pass(kept, grad):
    return (grad,)

def back_keep(v):
    return (v, None)

def back_low(kept, grad):
    return (low(grad),)
low.defvjp(low_keep, low_pass)
low_back.defvjp(back_keep, back_low)
epsilon = 1e-05
steepness = 6.0
levels = 4096.0
highest = lax.Precision.HIGHEST

def validity(bucket_shape, pixel_mask):
    row_index = lax.broadcasted_iota(jnp.int32, pixel_mask.shape, 1)
    col_index = lax.broadcasted_iota(jnp.int32, pixel_mask.shape, 2)
    inside = (row_index < bucket_shape[:, 0][:, None, None]) & (col_index < bucket_shape[:, 1][:, None, None])
    return jnp.where(inside, pixel_mask, 0).astype(jnp.float32)[..., None]

def batch_norm(values, valid_cells, valid_count, gain, bias):
    center = lax.optimization_barrier(jnp.sum(valid_cells * values, axis=(0, 1, 2))) / valid_count
    deviation = values - center
    variance = lax.optimization_barrier(jnp.sum(valid_cells * deviation * deviation, axis=(0, 1, 2))) / valid_count
    return gain * deviation * lax.rsqrt(variance + epsilon) + bias

def spatial(acts, weight):
    grid_side = acts.shape[1]
    padded = jnp.pad(acts, ((0, 0), (1, 1), (1, 1), (0, 0)))
    result = jnp.zeros(acts.shape[:3] + (weight.shape[2],), jnp.float32)
    for offset in range(9):
        row_shift = offset // 3
        col_shift = offset % 3
        window = padded[:, row_shift:row_shift + grid_side, col_shift:col_shift + grid_side, :]
        result = result + jnp.einsum('ihwc,cd->ihwd', window, weight[offset], precision=highest)
    return result

def trunk_block(valid_cells, valid_count, inputs, reduce_w, spatial_w, expand_w, mid_gains, mid_biases, out_gain, out_bias):
    masked = valid_cells * inputs
    pre_reduce = low_back(jnp.einsum('ihwc,cd->ihwd', masked, reduce_w, precision=highest))
    act_reduce = low(valid_cells * jax.nn.silu(batch_norm(pre_reduce, valid_cells, valid_count, mid_gains[0], mid_biases[0])))
    pre_spatial = low_back(spatial(act_reduce, spatial_w))
    act_spatial = low(valid_cells * jax.nn.silu(batch_norm(pre_spatial, valid_cells, valid_count, mid_gains[1], mid_biases[1])))
    pre_expand = low_back(jnp.einsum('ihwc,cd->ihwd', act_spatial, expand_w, precision=highest))
    residual = inputs + batch_norm(pre_expand, valid_cells, valid_count, out_gain, out_bias)
    return low(valid_cells * jax.nn.silu(residual))

def head_layer(features, weight):
    return jnp.einsum('ihwc,cd->ihwd', features, weight, precision=highest)

def reference(images, bucket_shape, pixel_mask, thresholds, reduce_weight, spatial_weight, expand_weight, mid_gains, mid_biases, out_gain, out_bias, head_weights, head_cotangent):
    valid_cells = validity(bucket_shape, pixel_mask)
    valid_count = jnp.sum(valid_cells)
    block = partial(trunk_block, valid_cells, valid_count)
    features, trunk_back = jax.vjp(block, images.astype(jnp.float32), reduce_weight.astype(jnp.float32), spatial_weight.astype(jnp.float32), expand_weight.astype(jnp.float32), mid_gains, mid_biases, out_gain, out_bias)
    heads_float = head_weights.astype(jnp.float32)
    cotangent = head_cotangent.astype(jnp.float32)
    outputs = []
    task_grads = []
    weight_grads = []
    for task in range(TASKS):
        values, head_back = jax.vjp(head_layer, features, heads_float[:, task, :])
        grad_features, grad_weight = head_back(cotangent[:, :, :, task, :])
        outputs.append(values)
        task_grads.append(grad_features)
        weight_grads.append(grad_weight)
    head_output = jnp.stack(outputs, axis=3).astype(jnp.bfloat16)
    task_grad = jnp.stack(task_grads, axis=3)
    task_total = lax.optimization_barrier(jnp.sum(task_grad, axis=3))
    spread = lax.optimization_barrier(jnp.sum(jnp.sqrt(task_grad * task_grad + 1.0), axis=3))
    purity = 0.5 * (1.0 + task_total / spread)
    threshold_level = (thresholds.astype(jnp.float32) + 0.5) / levels
    kept_share = jax.nn.sigmoid(steepness * jnp.tanh(task_grad) * (purity - threshold_level)[:, :, :, None, :])
    merged = lax.optimization_barrier(jnp.sum(kept_share * task_grad, axis=3))
    images_grad, reduce_grad, spatial_grad, expand_grad, gains_grad, biases_grad, outgain_grad, outbias_grad = trunk_back(merged)
    heads_grad = jnp.stack(weight_grads, axis=1)
    return (head_output, images_grad, reduce_grad, spatial_grad, expand_grad, gains_grad, biases_grad, outgain_grad, outbias_grad, heads_grad)
```

```python
import jax
import jax.numpy as jnp
from jax import lax
from jax.sharding import PartitionSpec as P

epsilon = 1e-05
steepness = 6.0
levels = 4096.0
everyone = ("dp", "task")


def validity(bucket_shape, pixel_mask):
    row_index = lax.broadcasted_iota(jnp.int32, pixel_mask.shape, 1)
    col_index = lax.broadcasted_iota(jnp.int32, pixel_mask.shape, 2)
    inside = (row_index < bucket_shape[:, 0][:, None, None]) & (
        col_index < bucket_shape[:, 1][:, None, None]
    )
    return jnp.where(inside, pixel_mask, 0).astype(jnp.float32)


def inner_rows(left, right):
    return lax.dot_general(
        left, right, (((0,), (0,)), ((), ())), preferred_element_type=jnp.float32
    )


def outer_back(left, right):
    return lax.dot_general(
        left, right, (((1,), (1,)), ((), ())), preferred_element_type=jnp.float32
    )


def silu_slope(values):
    sigma = jax.nn.sigmoid(values)
    return sigma * (1.0 + values * (1.0 - sigma))


def from_everyone(rows):
    count = lax.axis_size("dp") * lax.axis_size("task")
    k, channels = rows.shape
    sent = jnp.broadcast_to(rows.reshape(1, k * channels // 128, 128), (count, k * channels // 128, 128))
    return lax.all_to_all(sent, everyone, 0, 0, tiled=True).reshape(count, k, channels)


def moments(values, valid_cells, local_count, counts):
    channels = values.shape[1]
    first = jnp.sum(valid_cells * values, axis=0)
    local_center = first / jnp.maximum(local_count, 1.0)
    deviation = values - local_center
    second = jnp.sum(valid_cells * deviation * deviation, axis=0)
    rows = [first, second]
    if counts is None:
        rows.append(jnp.full((channels,), local_count))
    table = from_everyone(jnp.stack(rows))
    if counts is None:
        counts = table[:, 2, 0]
    valid_count = jnp.sum(counts)
    center = jnp.sum(table[:, 0], axis=0) / valid_count
    shift = table[:, 0] / jnp.maximum(counts, 1.0)[:, None] - center
    variance = (
        jnp.sum(table[:, 1], axis=0) + jnp.sum(counts[:, None] * shift * shift, axis=0)
    ) / valid_count
    inverse_std = lax.rsqrt(variance + epsilon)
    return (values - center) * inverse_std, inverse_std, counts, valid_count


def norm_back(grad_shifted, normed, inverse_std, gain, valid_cells, valid_count):
    rows = jnp.stack([jnp.sum(grad_shifted, axis=0), jnp.sum(grad_shifted * normed, axis=0)])
    totals = jnp.sum(from_everyone(rows), axis=0)
    bias_grad, gain_grad = totals[0], totals[1]
    grad_values = (
        gain
        * inverse_std
        * (grad_shifted - valid_cells * (bias_grad + normed * gain_grad) / valid_count)
    )
    return (grad_values.astype(jnp.bfloat16), gain_grad, bias_grad)


def patches(acts):
    grid_side = acts.shape[1]
    padded = jnp.pad(acts, ((0, 0), (1, 1), (1, 1), (0, 0)))
    windows = []
    for offset in range(9):
        row_shift = offset // 3
        col_shift = offset % 3
        windows.append(
            padded[:, row_shift : row_shift + grid_side, col_shift : col_shift + grid_side, :]
        )
    return jnp.concatenate(windows, axis=-1).reshape(-1, 9 * acts.shape[-1])


def unpatch(grad_cols, image_count, grid_side, channels):
    blocks = grad_cols.reshape(image_count, grid_side, grid_side, 9, channels)
    result = jnp.zeros((image_count, grid_side + 2, grid_side + 2, channels), jnp.float32)
    for offset in range(9):
        row_shift = offset // 3
        col_shift = offset % 3
        result = result + jnp.pad(
            blocks[:, :, :, offset, :],
            ((0, 0), (row_shift, 2 - row_shift), (col_shift, 2 - col_shift), (0, 0)),
        )
    return result[:, 1 : grid_side + 1, 1 : grid_side + 1, :]


def dp_bit(bit):
    return (lax.axis_index("dp") >> bit) & 1


def swap_dp(value, bit):
    peers = lax.axis_size("dp")
    return lax.ppermute(value, "dp", [(i, i ^ (1 << bit)) for i in range(peers)])


def swap_core(value):
    return lax.ppermute(value, "task", [(0, 1), (1, 0)])


def pick(value, axis, index):
    return lax.dynamic_index_in_dim(value, index, axis, keepdims=False)


def halve(value, dims, order):
    dims = list(dims)
    for bit in order:
        axis = dims.index(bit)
        mine = dp_bit(bit)
        arrived = swap_dp(pick(value, axis, 1 - mine), bit)
        kept = pick(value, axis, mine).astype(jnp.float32)
        dims.pop(axis)
        total = kept + arrived.astype(jnp.float32)
        value = total.astype(jnp.bfloat16) if dims else total
    return value


def on_device(
    images,
    bucket_shape,
    pixel_mask,
    thresholds,
    reduce_weight,
    spatial_weight,
    expand_weight,
    mid_gains,
    mid_biases,
    out_gain,
    out_bias,
    head_weights,
    head_cotangent,
):
    image_count = images.shape[0]
    grid_side = images.shape[1]
    width = images.shape[3]
    middle = reduce_weight.shape[1]
    head_count = head_weights.shape[1]
    pixels = image_count * grid_side * grid_side
    peers = lax.axis_size("dp")
    bits = peers.bit_length() - 1
    core = lax.axis_index("task")
    valid_cells = validity(bucket_shape, pixel_mask).reshape(pixels, 1)
    local_count = jnp.sum(valid_cells)
    inputs = images.reshape(pixels, width)
    masked = inputs * valid_cells.astype(jnp.bfloat16)

    group_images = head_cotangent.shape[0]
    task_part = jnp.einsum(
        "ihwtd,ctd->ihwtc", head_cotangent, head_weights, preferred_element_type=jnp.float32
    ).reshape(2, pixels, head_count, width)
    task_sent = pick(task_part, 0, 1 - core).astype(jnp.bfloat16)
    task_kept = pick(task_part, 0, core).astype(jnp.bfloat16).astype(jnp.float32)
    task_grad = task_kept + swap_core(task_sent).astype(jnp.float32)
    task_total = jnp.sum(task_grad, axis=1)
    spread = jnp.sum(jnp.sqrt(task_grad * task_grad + 1.0), axis=1)
    purity = 0.5 * (1.0 + task_total / spread)
    threshold_level = (thresholds.reshape(pixels, width).astype(jnp.float32) + 0.5) / levels
    kept_share = jax.nn.sigmoid(
        steepness * jnp.tanh(task_grad) * (purity - threshold_level)[:, None, :]
    )
    merged = jnp.sum(kept_share * task_grad, axis=1)

    pre_reduce = jnp.dot(masked, reduce_weight, preferred_element_type=jnp.float32)
    normed_reduce, inverse_reduce, counts, valid_count = moments(
        pre_reduce, valid_cells, local_count, None
    )
    shifted_reduce = mid_gains[0] * normed_reduce + mid_biases[0]
    act_reduce = (valid_cells * jax.nn.silu(shifted_reduce)).astype(jnp.bfloat16)
    patches_flat = patches(act_reduce.reshape(image_count, grid_side, grid_side, middle))
    spatial_flat = spatial_weight.reshape(9 * middle, middle)
    pre_spatial = jnp.dot(patches_flat, spatial_flat, preferred_element_type=jnp.float32)
    normed_spatial, inverse_spatial, _, _ = moments(pre_spatial, valid_cells, local_count, counts)
    shifted_spatial = mid_gains[1] * normed_spatial + mid_biases[1]
    act_spatial = (valid_cells * jax.nn.silu(shifted_spatial)).astype(jnp.bfloat16)
    pre_expand = jnp.dot(act_spatial, expand_weight, preferred_element_type=jnp.float32)
    normed_expand, inverse_expand, _, _ = moments(pre_expand, valid_cells, local_count, counts)
    residual = inputs.astype(jnp.float32) + out_gain * normed_expand + out_bias
    features = (valid_cells * jax.nn.silu(residual)).astype(jnp.bfloat16)
    gathered = lax.all_gather(features, "task", axis=0, tiled=True)

    lanes = head_weights.shape[2]
    orders = ([0, 1] + list(range(2, bits)), [1, 0] + list(range(2, bits)))
    cut = gathered.reshape((gathered.shape[0],) + (2,) * bits + (width // peers,))
    dims = list(range(bits - 1, -1, -1))
    flat_cotangent = head_cotangent.reshape(gathered.shape[0], head_count, lanes)
    heads_parts = []
    for part, order in enumerate(orders):
        part_cot = flat_cotangent[:, :, part * lanes // 2 : (part + 1) * lanes // 2]
        axis = dims.index(order[0])
        mine = dp_bit(order[0])

        def product(index):
            chosen = pick(cut, 1 + axis, index).reshape(gathered.shape[0], width // 2)
            return jnp.einsum("pc,ptd->tcd", chosen, part_cot, preferred_element_type=jnp.float32)

        arrived = swap_dp(product(1 - mine).astype(jnp.bfloat16), order[0])
        kept = (product(mine) + arrived.astype(jnp.float32)).astype(jnp.bfloat16)
        rest = [d for d in dims if d != order[0]]
        kept = kept.reshape((head_count,) + (2,) * (bits - 1) + (width // peers, lanes // 2))
        kept = jnp.moveaxis(kept, 0, bits - 1)
        heads_parts.append(halve(kept, rest, order[1:]))
    heads_grad = jnp.concatenate(heads_parts, axis=-1)
    heads_grad = jnp.moveaxis(heads_grad, 0, 1)

    head_values = jnp.einsum(
        "pc,ctd->ptd", gathered, head_weights, preferred_element_type=jnp.float32
    )
    head_output = head_values.astype(jnp.bfloat16).reshape(
        group_images, grid_side, grid_side, head_count, -1
    )

    grad_residual = merged * valid_cells * silu_slope(residual)
    grad_expand, outgain_grad, outbias_grad = norm_back(
        grad_residual, normed_expand, inverse_expand, out_gain, valid_cells, valid_count
    )
    expand_part = inner_rows(act_spatial, grad_expand)
    grad_act_spatial = outer_back(grad_expand, expand_weight)
    grad_spatial, gain_two, bias_two = norm_back(
        grad_act_spatial * valid_cells * silu_slope(shifted_spatial),
        normed_spatial,
        inverse_spatial,
        mid_gains[1],
        valid_cells,
        valid_count,
    )
    spatial_part = inner_rows(patches_flat, grad_spatial).reshape(9, middle, middle)
    grad_cols = outer_back(grad_spatial, spatial_flat)
    grad_act_reduce = unpatch(grad_cols, image_count, grid_side, middle).reshape(pixels, middle)
    grad_reduce, gain_one, bias_one = norm_back(
        grad_act_reduce * valid_cells * silu_slope(shifted_reduce),
        normed_reduce,
        inverse_reduce,
        mid_gains[0],
        valid_cells,
        valid_count,
    )
    reduce_part = inner_rows(masked, grad_reduce)
    images_grad = grad_residual + valid_cells * outer_back(grad_reduce, reduce_weight)

    devices = peers * 2
    def by_device(value):
        return value.reshape((2,) * bits + (2,) + value.shape[1:])
    def shared(value, order):
        axis = bits
        arrived = swap_core(pick(value, axis, 1 - core).astype(jnp.bfloat16))
        total = pick(value, axis, core) + arrived.astype(jnp.float32)
        return halve(total.astype(jnp.bfloat16), dims, order)
    expand_rows = middle // devices
    expand_cut = jnp.moveaxis(
        expand_part.reshape(devices, expand_rows, width // middle, middle), 2, 1
    ).reshape(devices, expand_rows * width // middle, middle)
    spatial_cut = jnp.moveaxis(
        spatial_part.reshape(9, devices, middle // devices, middle), 1, 0
    ).reshape(devices, 9 * (middle // devices), middle)
    early = shared(by_device(jnp.concatenate([expand_cut, spatial_cut], axis=1)), orders[0])
    late = shared(by_device(reduce_part.reshape(devices, width // devices, middle)), orders[1])
    split = expand_rows * width // middle
    expand_grad = jnp.moveaxis(
        early[:split].reshape(width // middle, expand_rows, middle), 0, 1
    ).reshape(expand_rows, width)
    spatial_grad = early[split:].reshape(9, middle // devices, middle)
    reduce_grad = late
    gains_grad = jnp.stack([gain_one, gain_two], axis=0)
    biases_grad = jnp.stack([bias_one, bias_two], axis=0)
    return (
        head_output,
        images_grad.reshape(image_count, grid_side, grid_side, width),
        reduce_grad,
        spatial_grad,
        expand_grad,
        gains_grad,
        biases_grad,
        outgain_grad,
        outbias_grad,
        heads_grad,
    )


def solution(mesh):
    placed = (
        P(("dp", "task"), None, None, None),
        P(("dp", "task"), None),
        P(("dp", "task"), None, None),
        P(("dp", "task"), None, None, None),
        P(),
        P(),
        P(),
        P(),
        P(),
        P(),
        P(),
        P(None, None, "task"),
        P("dp", None, None, None, "task"),
    )
    return jax.shard_map(
        on_device,
        mesh=mesh,
        in_specs=placed,
        out_specs=(
            P("dp", None, None, None, "task"),
            P(("dp", "task"), None, None, None),
            P(("dp", "task"), None),
            P(None, ("dp", "task"), None),
            P(("dp", "task"), None),
            P(),
            P(),
            P(),
            P(),
            P("dp", None, "task"),
        ),
        check_vma=False,
    )
```

```python
import functools

import jax
import jax.numpy as jnp
from jax import lax
from jax.experimental import pallas as pl
from jax.experimental.pallas import tpu as pltpu
from jax.sharding import PartitionSpec as P

epsilon = 1e-05
steepness = 6.0
levels = 4096.0
everyone = ("dp", "task")
f32 = jnp.float32
bf16 = jnp.bfloat16
lane = 128
MIB = 1 << 20


def dot(left, right, contract):
    return lax.dot_general(
        left, right, ((contract[0:1], contract[1:2]), ((), ())), preferred_element_type=f32
    )


def kernel_call(body, outs, small=(), big=(), scalars=None, scratch=(), copies=0, after=(), fills=False, name=None):
    skipped = len(after)

    def ordered(*refs):
        body(*refs[skipped:])

    big = [pltpu.with_memory_space_constraint(array, pltpu.HBM) for array in big]
    there = pl.BlockSpec(memory_space=pl.ANY)
    here = pl.BlockSpec(memory_space=pltpu.VMEM)
    given = [] if scalars is None else [scalars]
    return pl.pallas_call(
        ordered,
        in_specs=[there] * skipped
        + [pl.BlockSpec(memory_space=pltpu.SMEM)] * len(given)
        + [here] * len(small)
        + [there] * len(big),
        out_specs=[there if streamed else here for _, _, streamed in outs],
        out_shape=[
            pltpu.HBM(shape, dtype) if streamed else jax.ShapeDtypeStruct(shape, dtype)
            for shape, dtype, streamed in outs
        ],
        scratch_shapes=list(scratch) + ([pltpu.SemaphoreType.DMA((copies,))] if copies else []),
        input_output_aliases={0: 0} if fills else {},
        compiler_params=pltpu.CompilerParams(vmem_limit_bytes=48 * MIB),
        name=name,
    )(*after, *given, *small, *big)


def held_until(after, *values):
    def body(*refs):
        pass

    there = pl.BlockSpec(memory_space=pl.ANY)
    return pl.pallas_call(
        body,
        in_specs=[there] * (len(values) + len(after)),
        out_specs=[there] * len(values),
        out_shape=[jax.ShapeDtypeStruct(v.shape, v.dtype) for v in values],
        input_output_aliases={i: i for i in range(len(values))},
        name="held",
    )(*values, *after)


class Copies:
    def __init__(self, sems):
        self.sems = sems
        self.used = 0
        self.open = []

    def start(self, source, target):
        copy = pltpu.make_async_copy(source, target, self.sems.at[self.used])
        self.used += 1
        copy.start()
        return copy

    def out(self, source, target):
        self.open.append(self.start(source, target))

    def finish(self):
        for copy in self.open:
            copy.wait()


def columns(ref, index, size):
    return ref.at[:, index * size : (index + 1) * size]


def sigmoid(value):
    return 0.5 + 0.5 * jnp.tanh(0.5 * value)


def combined(table, counts):
    counts = counts[:, 0:1]
    total = jnp.sum(counts)
    center = jnp.sum(table[:, 0, :], axis=0, keepdims=True) / total
    shift = table[:, 0, :] / jnp.maximum(counts, 1.0) - center
    variance = (
        jnp.sum(table[:, 1, :] + counts * shift * shift, axis=0, keepdims=True) / total
    )
    return center, lax.rsqrt(variance + epsilon)


def store_rows(stats_ref, rows, at=slice(None)):
    table = jnp.concatenate(rows, axis=0)
    stats_ref[:, :, at] = jnp.broadcast_to(table[None], (stats_ref.shape[0],) + table.shape)


def store_moments(stats_ref, values_ref, valid_ref, at=slice(None)):
    valid, values = valid_ref[...], values_ref[...]
    count = jnp.sum(valid)
    first = jnp.sum(values * valid, axis=0, keepdims=True)
    deviation = (values - first / jnp.maximum(count, 1.0)) * valid
    rows = [first, jnp.sum(deviation * deviation, axis=0, keepdims=True)]
    if stats_ref.shape[1] > 2:
        rows.append(jnp.broadcast_to(count, first.shape))
    store_rows(stats_ref, rows, at)


def store_sums(stats_ref, grad, normed, at=slice(None)):
    rows = [jnp.sum(grad, axis=0, keepdims=True), jnp.sum(grad * normed, axis=0, keepdims=True)]
    store_rows(stats_ref, rows, at)


def reduce_kernel(valid_ref, x_ref, w_ref, out_ref, stats_ref, x_buf, w_buf, sems):
    copies = Copies(sems)
    parts = 4
    size = x_ref.shape[1] // parts
    arriving = []
    for k in range(parts):
        arriving.append(
            (
                copies.start(columns(x_ref, k, size), columns(x_buf, k, size)),
                copies.start(w_ref.at[k * size : (k + 1) * size], w_buf.at[k * size : (k + 1) * size]),
            )
        )
    total = None
    for k, pair in enumerate(arriving):
        for copy in pair:
            copy.wait()
        part = dot(x_buf[:, k * size : (k + 1) * size], w_buf[k * size : (k + 1) * size, :], (1, 0))
        total = part if total is None else total + part
    out_ref[...] = total * valid_ref[...]
    store_moments(stats_ref, out_ref, valid_ref)


def pad_edges(acts_ref, side):
    images = acts_ref.shape[1]
    zeros = jnp.zeros((side, acts_ref.shape[3]), bf16)
    for shift in range(3):
        for image in range(images):
            acts_ref[shift, image, 0:side, :] = zeros
            acts_ref[shift, image, (side + 1) * side : (side + 2) * side, :] = zeros


def store_shifted(acts_ref, values, side):
    pixels = values.shape[0]
    column = lax.broadcasted_iota(jnp.int32, (pixels, 1), 0) % side
    before = jnp.where(column == 0, 0.0, pltpu.roll(values, 1, 0))
    after = jnp.where(column == side - 1, 0.0, pltpu.roll(values, pixels - 1, 0))
    for shift, moved in enumerate((before, values, after)):
        for image in range(acts_ref.shape[1]):
            rows = slice(image * side * side, (image + 1) * side * side)
            acts_ref[shift, image, side : side + side * side, :] = moved[rows].astype(bf16)


def window(acts_ref, row_shift, col_shift, side):
    images = acts_ref.shape[1]
    tile = acts_ref[col_shift, :, row_shift * side : row_shift * side + side * side, :]
    return tile.reshape(images * side * side, acts_ref.shape[3])


def spatial_kernel(
    side, pre_ref, table_ref, norm_ref, valid_ref, w_ref, out_ref, consts_ref, stats_ref, acts_out, w_buf, acts_ref, sems
):
    copies = Copies(sems)
    arriving = [copies.start(w_ref.at[k], w_buf.at[k]) for k in range(9)]
    center, inverse = combined(table_ref, table_ref[:, 2, :])
    consts_ref[0:1, :] = center
    consts_ref[1:2, :] = inverse
    gain, bias = norm_ref[0:1, :], norm_ref[1:2, :]
    pad_edges(acts_ref, side)

    shifted = gain * ((pre_ref[...] - center) * inverse) + bias
    store_shifted(acts_ref, valid_ref[...] * shifted * sigmoid(shifted), side)
    copies.out(acts_ref, acts_out)
    total = None
    for tap in range(9):
        arriving[tap].wait()
        part = dot(window(acts_ref, tap // 3, tap % 3, side), w_buf[tap], (1, 0))
        total = part if total is None else total + part
    out_ref[...] = total
    store_moments(stats_ref, out_ref, valid_ref)
    copies.finish()


def expand_kernel(
    pre_ref, table_ref, first_ref, norm_ref, valid_ref, w_ref, act_ref, consts_ref, stats_ref, out, w_buf, out_buf, sems
):
    copies = Copies(sems)
    parts = 4
    size = w_ref.shape[1] // parts
    arriving = [copies.start(columns(w_ref, k, size), columns(w_buf, k, size)) for k in range(parts)]
    center, inverse = combined(table_ref, first_ref[:, 2, :])
    consts_ref[0:1, :] = center
    consts_ref[1:2, :] = inverse
    gain, bias = norm_ref[0:1, :], norm_ref[1:2, :]

    shifted = gain * ((pre_ref[...] - center) * inverse) + bias
    act_ref[...] = (valid_ref[...] * shifted * sigmoid(shifted)).astype(bf16)
    for k in range(parts):
        at = slice(k * size, (k + 1) * size)
        arriving[k].wait()
        out_buf[:, at] = dot(act_ref[...], w_buf[:, at], (1, 0))
        copies.out(columns(out_buf, k, size), columns(out, k, size))
        store_moments(stats_ref, columns(out_buf, k, size), valid_ref, at)
    copies.finish()


def residual_kernel(
    which_ref, table_ref, first_ref, gain_ref, bias_ref, valid_ref, pre_ref, x_ref, merged_ref,
    consts_ref, sums_ref, feat_out, same_out, cross_out, grad_out,
    pre_buf, x_buf, merged_buf, feat_buf, block_buf, grad_buf, sems,
):
    copies = Copies(sems)
    parts = 4
    size = pre_ref.shape[1] // parts
    arriving = []
    for k in range(parts):
        arriving.append(
            [
                copies.start(columns(ref, k, size), columns(buf, k, size))
                for ref, buf in ((pre_ref, pre_buf), (x_ref, x_buf), (merged_ref, merged_buf))
            ]
        )
    for k in range(parts):
        at = slice(k * size, (k + 1) * size)
        center, inverse = combined(table_ref[:, :, at], first_ref[:, 2, :])
        consts_ref[0:1, at] = center
        consts_ref[1:2, at] = inverse
        gain, bias = gain_ref[:, at], bias_ref[:, at]
        for copy in arriving[k]:
            copy.wait()

        valid = valid_ref[...]
        normed = (pre_buf[:, at] - center) * inverse
        value = x_buf[:, at].astype(f32) + gain * normed + bias
        sigma = sigmoid(value)
        features = (valid * (value * sigma)).astype(bf16)
        feat_buf[:, at] = features
        for piece in range(4):
            block_buf[2 * (piece % 2) + piece // 2, :, k * lane : (k + 1) * lane] = features[
                :, piece * lane : (piece + 1) * lane
            ]
        grad = merged_buf[:, at] * valid * (sigma * (1.0 + value * (1.0 - sigma)))
        grad_buf[:, at] = grad
        store_sums(sums_ref, grad, normed, at)
        copies.out(columns(grad_buf, k, size), columns(grad_out, k, size))
        copies.out(columns(feat_buf, k, size), columns(feat_out, k, size))
    for j in range(2):
        copies.out(block_buf.at[which_ref[j]], same_out.at[j])
        copies.out(block_buf.at[which_ref[2 + j]], cross_out.at[j])
    copies.finish()


def slope_rows(grad, pre_ref, consts_ref, norm_ref, valid_ref, out_ref, sums_ref):
    center, inverse = consts_ref[0:1, :], consts_ref[1:2, :]
    gain, bias = norm_ref[0:1, :], norm_ref[1:2, :]
    normed = (pre_ref[...] - center) * inverse
    value = gain * normed + bias
    sigma = sigmoid(value)
    grad = grad * valid_ref[...] * (sigma * (1.0 + value * (1.0 - sigma)))
    out_ref[...] = grad
    store_sums(sums_ref, grad, normed)


def expand_back_kernel(
    which_ref, consts_ref, table_ref, gain_ref, valid_ref, first_ref, mid_pre_ref, mid_consts_ref, mid_norm_ref,
    grad_ref, pre_ref, w_ref,
    totals_ref, shifted_ref, sums_ref, mine_out, sent_out,
    grad_buf, pre_buf, w_buf, out_buf, sems,
):
    copies = Copies(sems)
    parts = 4
    size = pre_ref.shape[1] // parts
    arriving = []
    for k in range(parts):
        arriving.append(
            [
                copies.start(columns(ref, k, size), columns(buf, k, size))
                for ref, buf in ((grad_ref, grad_buf), (pre_ref, pre_buf), (w_ref, w_buf))
            ]
        )
    count = jnp.sum(first_ref[:, 2, 0:1])
    total = None
    for k in range(parts):
        at = slice(k * size, (k + 1) * size)
        totals = jnp.sum(table_ref[:, :, at], axis=0)
        totals_ref[:, at] = totals
        center, inverse = consts_ref[0:1, at], consts_ref[1:2, at]
        plain, scaled = totals[0:1, :] / count, totals[1:2, :] / count
        scale = gain_ref[:, at] * inverse
        for copy in arriving[k]:
            copy.wait()

        normed = (pre_buf[:, at] - center) * inverse
        grad = scale * (grad_buf[:, at] - valid_ref[...] * (plain + normed * scaled))
        out_buf[:, at] = grad.astype(bf16)
        part = dot(out_buf[:, at], w_buf[:, at], (1, 1))
        total = part if total is None else total + part
    half = out_buf.shape[1] // 2
    for place, out in ((which_ref[0], mine_out), (1 - which_ref[0], sent_out)):
        copies.out(out_buf.at[:, pl.ds(pl.multiple_of(place * half, half), half)], out)
    slope_rows(total, mid_pre_ref, mid_consts_ref, mid_norm_ref, valid_ref, shifted_ref, sums_ref)
    copies.finish()


def spatial_back_kernel(
    side, which_ref, grad_ref, pre_ref, consts_ref, table_ref, norm_ref, valid_ref, first_ref,
    low_pre_ref, low_consts_ref, low_norm_ref, w_ref,
    totals_ref, shifted_ref, sums_ref, mine_out, sent_out,
    w_buf, acts_ref, out_ref, sems,
):
    copies = Copies(sems)
    arriving = [copies.start(w_ref.at[k], w_buf.at[k]) for k in range(9)]
    count = jnp.sum(first_ref[:, 2, 0:1])
    totals = jnp.sum(table_ref[...], axis=0)
    totals_ref[...] = totals
    center, inverse = consts_ref[0:1, :], consts_ref[1:2, :]
    plain, scaled = totals[0:1, :] / count, totals[1:2, :] / count
    scale = norm_ref[0:1, :] * inverse
    pad_edges(acts_ref, side)

    normed = (pre_ref[...] - center) * inverse
    grad = scale * (grad_ref[...] - valid_ref[...] * (plain + normed * scaled))
    out_ref[...] = grad.astype(bf16)
    half = out_ref.shape[1] // 2
    for place, out in ((which_ref[0], mine_out), (1 - which_ref[0], sent_out)):
        copies.out(out_ref.at[:, pl.ds(pl.multiple_of(place * half, half), half)], out)
    store_shifted(acts_ref, grad, side)
    total = None
    for tap in range(9):
        arriving[tap].wait()
        part = dot(window(acts_ref, 2 - tap // 3, 2 - tap % 3, side), w_buf[tap], (1, 1))
        total = part if total is None else total + part
    slope_rows(total, low_pre_ref, low_consts_ref, low_norm_ref, valid_ref, shifted_ref, sums_ref)
    copies.finish()


def reduce_back_kernel(
    grad_ref, pre_ref, consts_ref, table_ref, norm_ref, valid_ref, first_ref, w_ref, res_ref, x_ref,
    totals_ref, images_out, part_out,
    low_buf, w_buf, res_buf, x_buf, part_buf, sems,
):
    copies = Copies(sems)
    parts = 4
    size = res_ref.shape[1] // parts
    arriving = []
    for k in range(parts):
        at = slice(k * size, (k + 1) * size)
        arriving.append(
            [
                copies.start(columns(x_ref, k, size), columns(x_buf, k, size)),
                copies.start(w_ref.at[at], w_buf.at[at]),
                copies.start(columns(res_ref, k, size), columns(res_buf, k, size)),
            ]
        )
    count = jnp.sum(first_ref[:, 2, 0:1])
    totals = jnp.sum(table_ref[...], axis=0)
    totals_ref[...] = totals
    center, inverse = consts_ref[0:1, :], consts_ref[1:2, :]
    plain, scaled = totals[0:1, :] / count, totals[1:2, :] / count
    scale = norm_ref[0:1, :] * inverse

    normed = (pre_ref[...] - center) * inverse
    grad = scale * (grad_ref[...] - valid_ref[...] * (plain + normed * scaled))
    low_buf[...] = grad.astype(bf16)
    for k in range(parts):
        at = slice(k * size, (k + 1) * size)
        arriving[k][0].wait()
        part_buf[at, :] = dot(x_buf[:, at], low_buf[...], (0, 0)).astype(bf16)
        copies.out(part_buf.at[at], part_out.at[at])
    for k in range(parts):
        at = slice(k * size, (k + 1) * size)
        arriving[k][1].wait()
        arriving[k][2].wait()
        res_buf[:, at] = res_buf[:, at] + valid_ref[...] * dot(low_buf[...], w_buf[at, :], (1, 1))
        copies.out(columns(res_buf, k, size), columns(images_out, k, size))
    copies.finish()


def trunk_weights_kernel(
    side, act_ref, act_sib, right_ref, right_sib, acts_ref, acts_sib, grad_ref, grad_sib,
    out, acts_buf, grad_buf, out_buf, sems,
):
    copies = Copies(sems)
    size = right_ref.shape[1]
    blocks = grad_ref.shape[1] // size
    grads = [copies.start(ref, grad_buf.at[c]) for c, ref in enumerate((grad_ref, grad_sib))]
    acts = [copies.start(ref, acts_buf.at[c]) for c, ref in enumerate((acts_ref, acts_sib))]
    for copy in grads:
        copy.wait()
    for k in range(blocks):
        at = slice(k * size, (k + 1) * size)
        out_buf[k] = (
            dot(act_ref[...], grad_buf[0, :, at], (0, 0)) + dot(act_sib[...], grad_buf[1, :, at], (0, 0))
        ).astype(bf16)
        copies.out(out_buf.at[k], out.at[k])
    for copy in acts:
        copy.wait()
    for tap in range(9):
        tiles = [window(acts_buf.at[c], tap // 3, tap % 3, side) for c in range(2)]
        out_buf[blocks + tap] = (
            dot(tiles[0], right_ref[...], (0, 0)) + dot(tiles[1], right_sib[...], (0, 0))
        ).astype(bf16)
        copies.out(out_buf.at[blocks + tap], out.at[blocks + tap])
    copies.finish()


def task_kernel(half_ref, cot_ref, w_ref, out, cot_buf, w_buf, out_buf, sems):
    copies = Copies(sems)
    tasks, pixels = out.shape[:2]
    size = w_buf.shape[1]
    parts = w_ref.shape[1] // size
    rows = cot_buf.shape[1]
    start = pl.multiple_of(half_ref[0] * rows, rows)
    cots, arriving = [], []
    for t in range(tasks):
        cots.append(copies.start(cot_ref.at[pl.ds(start, rows), t], cot_buf.at[t]))
        for j in range(parts):
            arriving.append(copies.start(w_ref.at[t, j * size : (j + 1) * size], w_buf.at[t * parts + j]))
    for t in range(tasks):
        cots[t].wait()
        for j in range(parts):
            slot = t * parts + j
            arriving[slot].wait()
            cot = cot_buf[t].reshape(pixels, cot_buf.shape[3])
            out_buf[slot] = dot(cot, w_buf[slot], (1, 1)).astype(bf16)
            copies.out(out_buf.at[slot], out.at[t, :, j * size : (j + 1) * size])
    copies.finish()


def drop_kernel(mine_ref, other_ref, level_ref, out, mine_buf, other_buf, level_buf, out_buf, sems):
    copies = Copies(sems)
    tasks, pixels, _ = mine_ref.shape
    parts = 8
    size = pixels // parts
    arriving = []
    for k in range(parts):
        at = slice(k * size, (k + 1) * size)
        arriving.append(
            [
                copies.start(mine_ref.at[:, at], mine_buf.at[:, at]),
                copies.start(other_ref.at[:, at], other_buf.at[:, at]),
                copies.start(level_ref.at[at], level_buf.at[at]),
            ]
        )
    for k in range(parts):
        for copy in arriving[k]:
            copy.wait()

        rows = slice(k * size, (k + 1) * size)
        grads = [mine_buf[t, rows].astype(f32) + other_buf[t, rows].astype(f32) for t in range(tasks)]
        total, spread = None, None
        for grad in grads:
            squared = grad * grad + 1.0
            root = squared * lax.rsqrt(squared)
            spread = root if spread is None else spread + root
            total = grad if total is None else total + grad
        margin = (0.25 * steepness) * (total / spread) + (
            0.25 * steepness * (1.0 - 1.0 / levels)
            - level_buf[rows].astype(f32) * (0.5 * steepness / levels)
        )
        merged = total
        for grad in grads:
            merged = merged + grad * jnp.tanh(jnp.tanh(grad) * margin)
        out_buf[rows] = 0.5 * merged
        at = slice(k * size, (k + 1) * size)
        copies.out(out_buf.at[at], out.at[at])
    copies.finish()


def heads_kernel(first, which_ref, own_ref, sib_ref, w_ref, out, own_buf, sib_buf, w_buf, out_buf, sems):
    copies = Copies(sems)
    core = which_ref[0]
    tasks = w_buf.shape[0]
    lanes = w_ref.shape[2]
    size = lanes // 2
    rows = out.shape[0] // 2
    arriving = []
    features = []
    for t in range(tasks):
        for j in range(2):
            at = slice(j * size, (j + 1) * size)
            arriving.append(copies.start(w_ref.at[first + t, :, at], w_buf.at[t, :, at]))
            if not features:
                features = [copies.start(own_ref, own_buf), copies.start(sib_ref, sib_buf)]
    for t in range(tasks):
        for j in range(2):
            at = slice(j * size, (j + 1) * size)
            arriving[2 * t + j].wait()
            for s, (source, place) in enumerate(((own_buf, core), (sib_buf, 1 - core))):
                if t + j == 0:
                    features[s].wait()
                value = dot(source[...], w_buf[t, :, at], (1, 0)).astype(bf16)
                out_buf[t, s, :, :, at] = value.reshape(rows, out.shape[2], size)
                copies.out(
                    out_buf.at[t, s, :, :, at],
                    out.at[pl.ds(pl.multiple_of(place * rows, rows), rows), first + t, :, at],
                )
    copies.finish()


def weights_kernel(column, which_ref, own_ref, sib_ref, far_ref, cross_ref, cot_ref, pair_ref, out, feat_buf, flip_buf, cot_buf, out_buf, sems):
    copies = Copies(sems)
    core, far_place = which_ref[0], which_ref[3]
    tasks, width = out.shape[0], own_ref.shape[1]
    pixels, channels = feat_buf.shape[2:]
    pieces = channels // lane
    lanes = cot_buf.shape[4]
    rows = cot_ref.shape[0] // 2
    features = []
    for j in range(2):
        for s, ref in enumerate((own_ref, sib_ref)):
            features.append(
                [
                    copies.start(
                        ref.at[:, pl.ds(pl.multiple_of((4 * piece + which_ref[1 + j]) * lane, lane), lane)],
                        feat_buf.at[j, s, :, piece * lane : (piece + 1) * lane],
                    )
                    for piece in range(pieces)
                ]
            )
        for s, ref in enumerate((far_ref, cross_ref)):
            features.append([copies.start(ref.at[j], feat_buf.at[j, 2 + s])])
    far_start = far_place * (2 * rows)
    starts = [core * rows, (1 - core) * rows, far_start + core * rows, far_start + (1 - core) * rows]
    cots = []
    for t in range(tasks):
        cots.append(
            [
                copies.start(
                    (cot_ref if s < 2 else pair_ref).at[
                        pl.ds(pl.multiple_of(starts[s], rows), rows),
                        t,
                        :,
                        column * lanes : (column + 1) * lanes,
                    ],
                    cot_buf.at[t, s],
                )
                for s in range(4)
            ]
        )
    for t in range(tasks):
        for j in range(2):
            if t == 0:
                for s in range(4):
                    for copy in features[4 * j + s]:
                        copy.wait()
                    flip_buf[j, :, s * pixels : (s + 1) * pixels] = feat_buf[j, s].T
            if j == 0:
                for copy in cots[t]:
                    copy.wait()
            value = dot(flip_buf[j], cot_buf[t].reshape(4 * pixels, lanes), (1, 0))
            out_buf[t, j] = value.astype(bf16)
            copies.out(out_buf.at[t, j], out.at[t, j])
    copies.finish()


def validity(bucket_shape, pixel_mask):
    row_index = lax.broadcasted_iota(jnp.int32, pixel_mask.shape, 1)
    col_index = lax.broadcasted_iota(jnp.int32, pixel_mask.shape, 2)
    inside = (row_index < bucket_shape[:, 0][:, None, None]) & (
        col_index < bucket_shape[:, 1][:, None, None]
    )
    return jnp.where(inside, pixel_mask, 0).astype(f32)


def from_everyone(rows):
    return lax.all_to_all(rows, everyone, 0, 0, tiled=True)


def swap_core(value):
    return lax.ppermute(value, "task", [(0, 1), (1, 0)])


def pick(value, axis, index):
    return lax.dynamic_index_in_dim(value, index, axis, keepdims=False)


def two(value, axis, first, second):
    return jnp.stack([pick(value, axis, first), pick(value, axis, second)], axis)


def on_device(
    images,
    bucket_shape,
    pixel_mask,
    thresholds,
    reduce_weight,
    spatial_weight,
    expand_weight,
    mid_gains,
    mid_biases,
    out_gain,
    out_bias,
    head_weights,
    head_cotangent,
):
    image_count = images.shape[0]
    side = images.shape[1]
    width = images.shape[3]
    middle = reduce_weight.shape[1]
    tasks = head_weights.shape[1]
    lanes = head_weights.shape[2]
    pixels = image_count * side * side
    peers = lax.axis_size("dp")
    devices = 2 * peers
    core = lax.axis_index("task")
    low = max(0, (lane * peers // width).bit_length() - 1)
    bit_x, bit_y = 1 << low, 2 << low
    position = lax.axis_index("dp")
    my_x, my_y = (position >> low) & 1, (position >> (low + 1)) & 1
    def pairing(bit_of, cross):
        pairs = []
        for i in range(peers):
            for c in range(2):
                if cross:
                    pairs.append((2 * i + c, 2 * (i ^ bit_of[1 - c]) + 1 - c))
                else:
                    pairs.append((2 * i + c, 2 * (i ^ bit_of[c]) + c))
        return pairs

    def swap_first(value):
        return lax.ppermute(value, everyone, pairing((bit_x, bit_y), False))

    def swap_second(value):
        return lax.ppermute(value, everyone, pairing((bit_y, bit_x), False))

    def swap_cross(value):
        return lax.ppermute(value, everyone, pairing((bit_x, bit_y), True))

    def by_core(zero, one):
        return jnp.where(core == 0, zero, one)

    eights = {}
    for i in range(peers):
        for c, bit in enumerate((bit_y, bit_x)):
            key = (i & (bit_x | bit_y) & ~bit, c)
            eights.setdefault(key, []).append((1 if i & bit else 0, 2 * i + c))
    eights = [[device for _, device in sorted(eights[key])] for key in sorted(eights)]
    rest_bits = [b for b in range(peers.bit_length() - 1) if not (1 << b) & (bit_x | bit_y)]

    def scattered(value, dim):
        shape = value.shape
        count = len(rest_bits)
        value = value.reshape(shape[:dim] + (2,) * count + (-1,) + shape[dim + 1 :])
        for done, bit in enumerate(rest_bits):
            axis = dim + count - 1 - done
            mine = (position >> bit) & 1
            came = lax.ppermute(
                pick(value, axis, 1 - mine), "dp", [(i, i ^ (1 << bit)) for i in range(peers)]
            )
            value = pick(value, axis, mine).astype(f32) + came.astype(f32)
            if done < count - 1:
                value = value.astype(bf16)
        return value

    inputs = images.reshape(pixels, width)
    valid = validity(bucket_shape, pixel_mask).reshape(pixels, 1)
    norms = jnp.stack([mid_gains, mid_biases], axis=1)
    gain_row, bias_row = out_gain.reshape(1, width), out_bias.reshape(1, width)
    levels_flat = thresholds.reshape(pixels, width)
    cot = head_cotangent.transpose(0, 1, 3, 2, 4).reshape(2 * image_count * side, tasks, side, lanes)
    rows_half = image_count * side
    weights = head_weights.transpose(1, 0, 2)
    half_lanes = lanes // 2
    block = 4 * lane
    blocks = width // block

    pairs = []
    for i in range(peers):
        for c, bit in enumerate((bit_x, bit_y)):
            if not i & bit:
                pairs.append([2 * i + c, 2 * (i ^ bit) + c])
    pair_cot = lax.all_gather(cot, everyone, axis=0, tiled=True, axis_index_groups=pairs)

    mid = (pixels, middle)
    whole = (pixels, width)
    pair = (2, middle)
    stat_two, stat_three = (devices, 2, middle), (devices, 3, middle)

    def scalars(*values):
        return jnp.stack(values).astype(jnp.int32)

    def task_half(half, after):
        return kernel_call(
            task_kernel,
            [((tasks, pixels, width), bf16, True)],
            big=(cot, weights),
            scalars=scalars(half),
            scratch=[
                pltpu.VMEM((tasks, rows_half, side, lanes), bf16),
                pltpu.VMEM((2 * tasks, width // 2, lanes), bf16),
                pltpu.VMEM((2 * tasks, pixels, width // 2), bf16),
            ],
            copies=5 * tasks,
            after=after,
            name="task_grad",
        )[0]

    pre_reduce, stats = kernel_call(
        reduce_kernel,
        [(mid, f32, False), (stat_three, f32, False)],
        small=(valid,),
        big=(inputs, reduce_weight),
        scratch=[pltpu.VMEM(whole, bf16), pltpu.VMEM(reduce_weight.shape, bf16)],
        copies=8,
        after=(norms,),
        name="reduce",
    )
    table_one = from_everyone(stats)
    task_mine = task_half(core, (stats,))

    padded = (3, image_count, (side + 2) * side, middle)
    pre_spatial, consts_one, stats, acts = kernel_call(
        functools.partial(spatial_kernel, side),
        [(mid, f32, False), (pair, f32, False), (stat_two, f32, False), (padded, bf16, True)],
        small=(pre_reduce, table_one, norms[0], valid),
        big=(spatial_weight,),
        scratch=[pltpu.VMEM(spatial_weight.shape, bf16), pltpu.VMEM(padded, bf16)],
        copies=10,
        after=(task_mine,),
        name="spatial",
    )
    table_two = from_everyone(stats)
    task_sent = task_half(1 - core, (stats,))
    task_other = swap_core(held_until((table_two,), task_sent)[0])

    act_spatial, consts_two, stats, pre_expand = kernel_call(
        expand_kernel,
        [(mid, bf16, False), (pair, f32, False), ((devices, 2, width), f32, False), (whole, f32, True)],
        small=(pre_spatial, table_two, table_one, norms[1], valid),
        big=(expand_weight,),
        scratch=[pltpu.VMEM(expand_weight.shape, bf16), pltpu.VMEM(whole, f32)],
        copies=8,
        after=(task_sent,),
        name="expand",
    )
    table_three = from_everyone(stats)
    (merged,) = kernel_call(
        drop_kernel,
        [(whole, f32, True)],
        big=(task_mine, task_other, levels_flat),
        scratch=[
            pltpu.VMEM((tasks,) + whole, bf16),
            pltpu.VMEM((tasks,) + whole, bf16),
            pltpu.VMEM(whole, jnp.int32),
            pltpu.VMEM(whole, f32),
        ],
        copies=32,
        after=(stats,),
        name="graddrop",
    )


    pair_blocks = (2, pixels, width // 4)
    x_send, y_send = 2 * (1 - my_x), 1 - my_y
    consts_three, sums, features, same, cross, grad_residual = kernel_call(
        residual_kernel,
        [
            ((2, width), f32, False),
            ((devices, 2, width), f32, False),
            (whole, bf16, True),
            (pair_blocks, bf16, True),
            (pair_blocks, bf16, True),
            (whole, f32, True),
        ],
        scalars=scalars(
            by_core(x_send, y_send),
            by_core(x_send + 1, y_send + 2),
            by_core(y_send, x_send),
            by_core(y_send + 2, x_send + 1),
        ),
        small=(table_three, table_one, gain_row, bias_row, valid),
        big=(pre_expand, inputs, merged),
        scratch=[
            pltpu.VMEM(whole, f32),
            pltpu.VMEM(whole, bf16),
            pltpu.VMEM(whole, f32),
            pltpu.VMEM(whole, bf16),
            pltpu.VMEM((4, pixels, width // 4), bf16),
            pltpu.VMEM(whole, f32),
        ],
        copies=24,
        name="residual",
    )
    table_four = from_everyone(sums)
    same, cross, features, acts, act_spatial = held_until(
        (table_four,), same, cross, features, acts, act_spatial
    )
    sibling = swap_core(features)
    far = swap_first(same)
    far_cross = swap_cross(cross)
    acts_sib, act_spatial_sib = swap_core(acts), swap_core(act_spatial)

    def heads(first, count, after, fills):
        return kernel_call(
            functools.partial(heads_kernel, first),
            [(cot.shape, bf16, True)],
            big=(features, sibling, weights),
            scalars=scalars(core),
            scratch=[
                pltpu.VMEM(whole, bf16),
                pltpu.VMEM(whole, bf16),
                pltpu.VMEM((count, width, lanes), bf16),
                pltpu.VMEM((count, 2, rows_half, side, lanes), bf16),
            ],
            copies=2 + 6 * count,
            after=after,
            fills=fills,
            name="heads",
        )[0]

    expand_half, spatial_half = (pixels, width // 2), (pixels, middle // 2)
    out_totals, shifted_two, sums, expand_mine, expand_sent = kernel_call(
        expand_back_kernel,
        [
            ((2, width), f32, False),
            (mid, f32, False),
            (stat_two, f32, False),
            (expand_half, bf16, True),
            (expand_half, bf16, True),
        ],
        scalars=scalars(core),
        small=(consts_three, table_four, gain_row, valid, table_one, pre_spatial, consts_two, norms[1]),
        big=(grad_residual, pre_expand, expand_weight),
        scratch=[
            pltpu.VMEM(whole, f32),
            pltpu.VMEM(whole, f32),
            pltpu.VMEM(expand_weight.shape, bf16),
            pltpu.VMEM(whole, bf16),
        ],
        copies=14,
        name="expand_back",
    )
    table_five = from_everyone(sums)
    head_values = heads(0, 1, (sums,), False)

    part_shape = (tasks, 2, width // 4, half_lanes)

    def weight_part(column, after):
        return kernel_call(
            functools.partial(weights_kernel, column),
            [(part_shape, bf16, True)],
            big=(features, sibling, far, far_cross, cot, pair_cot),
            scalars=scalars(
                core,
                by_core(my_x, 2 * my_y),
                by_core(my_x + 2, 2 * my_y + 1),
                1 - by_core(my_x, my_y),
            ),
            scratch=[
                pltpu.VMEM((2, 4, pixels, width // 4), bf16),
                pltpu.VMEM((2, width // 4, 4 * pixels), bf16),
                pltpu.VMEM((tasks, 4, rows_half, side, half_lanes), bf16),
                pltpu.VMEM(part_shape, bf16),
            ],
            copies=4 * blocks + 4 + 6 * tasks,
            after=after,
            name="heads_grad",
        )[0]

    index = by_core(my_y, my_x)

    def paired(part):
        return part, swap_second(pick(part, 1, 1 - index))

    def added(part, came):
        return (pick(part, 1, index).astype(f32) + came.astype(f32)).astype(bf16)

    first_part = weight_part(0, (head_values,))
    first_part, expand_sent = held_until((table_five,), first_part, expand_sent)
    expand_sib = swap_core(expand_sent)
    first_part, first_came = paired(first_part)
    totals_two, shifted_one, sums, spatial_mine, spatial_sent = kernel_call(
        functools.partial(spatial_back_kernel, side),
        [
            (pair, f32, False),
            (mid, f32, False),
            (stat_two, f32, False),
            (spatial_half, bf16, True),
            (spatial_half, bf16, True),
        ],
        scalars=scalars(core),
        small=(
            shifted_two, pre_spatial, consts_two, table_five, norms[1], valid, table_one,
            pre_reduce, consts_one, norms[0],
        ),
        big=(spatial_weight,),
        scratch=[
            pltpu.VMEM(spatial_weight.shape, bf16),
            pltpu.VMEM(padded, bf16),
            pltpu.VMEM(mid, bf16),
        ],
        copies=11,
        after=(first_part,),
        name="spatial_back",
    )
    table_six = from_everyone(sums)
    second_part = weight_part(1, (sums,))
    second_part, spatial_sent = held_until((table_six,), second_part, spatial_sent)
    spatial_sib = swap_core(spatial_sent)
    second_part, second_came = paired(second_part)
    first_grad = added(first_part, first_came)
    early_shape = (blocks + 9, middle, middle // 2)
    (early_part,) = kernel_call(
        functools.partial(trunk_weights_kernel, side),
        [(early_shape, bf16, True)],
        small=(act_spatial, act_spatial_sib, spatial_mine, spatial_sib),
        big=(acts, acts_sib, expand_mine, expand_sib),
        scratch=[
            pltpu.VMEM((2,) + padded, bf16),
            pltpu.VMEM((2,) + expand_half, bf16),
            pltpu.VMEM(early_shape, bf16),
        ],
        copies=4 + early_shape[0],
        after=(first_grad,),
        name="trunk_weights",
    )
    early = lax.psum_scatter(early_part, "dp", scatter_dimension=1, tiled=True)
    totals_one, images_grad, reduce_part = kernel_call(
        reduce_back_kernel,
        [(pair, f32, False), (whole, f32, True), ((width, middle), bf16, True)],
        small=(shifted_one, pre_reduce, consts_one, table_six, norms[0], valid, table_one),
        big=(reduce_weight, grad_residual, inputs),
        scratch=[
            pltpu.VMEM(mid, bf16),
            pltpu.VMEM(reduce_weight.shape, bf16),
            pltpu.VMEM(whole, f32),
            pltpu.VMEM(whole, bf16),
            pltpu.VMEM((width, middle), bf16),
        ],
        copies=20,
        after=(early_part,),
        name="reduce_back",
    )
    second_grad = added(second_part, second_came)
    heads_grad = jnp.concatenate([scattered(first_grad, 1), scattered(second_grad, 1)], axis=2)
    heads_grad = heads_grad.transpose(1, 0, 2)
    head_values = heads(1, tasks - 1, (head_values, reduce_part), True)
    head_output = head_values.reshape(2 * image_count, side, tasks, side, lanes).transpose(0, 1, 3, 2, 4)

    def shared(value):
        lead, _, columns = value.shape
        value = value.reshape(lead, peers >> (low + 2), 4, 1 << low, 2, -1, columns)

        def summed(mine, came):
            return (mine.astype(f32) + came.astype(f32)).astype(bf16)

        value = summed(pick(value, 4, core), swap_core(pick(value, 4, 1 - core)))
        x_out, y_out = 1 - my_x, 2 * (1 - my_y)
        sent = two(value, 2, by_core(x_out, y_out), by_core(x_out + 2, y_out + 1))
        x_in, y_in = my_x, 2 * my_y
        kept = two(value, 2, by_core(x_in, y_in), by_core(x_in + 2, y_in + 1))
        value = summed(kept, swap_first(sent))
        index = by_core(my_y, my_x)
        value = summed(pick(value, 2, index), swap_second(pick(value, 2, 1 - index)))
        value = value.reshape(lead, peers // 4, -1, columns)
        return scattered(value, 1)[:, 0]

    late = shared(reduce_part[None])
    own_rows = early.reshape(early.shape[0], 2, -1, early.shape[2])
    came_rows = swap_core(pick(own_rows, 1, 1 - core))
    own_rows = pick(own_rows, 1, core)
    halves = jnp.stack(
        [jnp.where(core == 0, own_rows, came_rows), jnp.where(core == 0, came_rows, own_rows)]
    ).astype(f32)
    expand_grad = halves[:, :blocks].transpose(2, 0, 1, 3).reshape(middle // devices, width)
    spatial_grad = halves[:, blocks:].transpose(1, 2, 0, 3).reshape(9, middle // devices, middle)
    reduce_grad = late[0]
    gains_grad = jnp.stack([totals_one[1], totals_two[1]], axis=0)
    biases_grad = jnp.stack([totals_one[0], totals_two[0]], axis=0)
    return (
        head_output,
        images_grad.reshape(images.shape),
        reduce_grad,
        spatial_grad,
        expand_grad,
        gains_grad,
        biases_grad,
        out_totals[1],
        out_totals[0],
        heads_grad,
    )


def solution(mesh):
    placed = (
        P(("dp", "task"), None, None, None),
        P(("dp", "task"), None),
        P(("dp", "task"), None, None),
        P(("dp", "task"), None, None, None),
        P(),
        P(),
        P(),
        P(),
        P(),
        P(),
        P(),
        P(None, None, "task"),
        P("dp", None, None, None, "task"),
    )
    return jax.shard_map(
        on_device,
        mesh=mesh,
        in_specs=placed,
        out_specs=(
            P("dp", None, None, None, "task"),
            P(("dp", "task"), None, None, None),
            P(("dp", "task"), None),
            P(None, ("dp", "task"), None),
            P(("dp", "task"), None),
            P(),
            P(),
            P(),
            P(),
            P("dp", None, "task"),
        ),
        check_vma=False,
    )
```

```python
import functools

import jax
import jax.numpy as jnp
from jax import lax
from jax.experimental import pallas as pl
from jax.experimental.pallas import tpu as pltpu
from jax.sharding import PartitionSpec as P

epsilon = 1e-05
steepness = 6.0
levels = 4096.0
everyone = ("dp", "task")
f32 = jnp.float32
bf16 = jnp.bfloat16
lane = 128
MIB = 1 << 20


def dot(left, right, contract):
    return lax.dot_general(
        left, right, ((contract[0:1], contract[1:2]), ((), ())), preferred_element_type=f32
    )


def kernel_call(body, outs, small=(), big=(), scalars=None, scratch=(), copies=0, after=(), fills=False, name=None):
    skipped = len(after)

    def ordered(*refs):
        body(*refs[skipped:])

    big = [pltpu.with_memory_space_constraint(array, pltpu.HBM) for array in big]
    there = pl.BlockSpec(memory_space=pl.ANY)
    here = pl.BlockSpec(memory_space=pltpu.VMEM)
    given = [] if scalars is None else [scalars]
    return pl.pallas_call(
        ordered,
        in_specs=[there] * skipped
        + [pl.BlockSpec(memory_space=pltpu.SMEM)] * len(given)
        + [here] * len(small)
        + [there] * len(big),
        out_specs=[there if streamed else here for _, _, streamed in outs],
        out_shape=[
            pltpu.HBM(shape, dtype) if streamed else jax.ShapeDtypeStruct(shape, dtype)
            for shape, dtype, streamed in outs
        ],
        scratch_shapes=list(scratch) + ([pltpu.SemaphoreType.DMA((copies,))] if copies else []),
        input_output_aliases={0: 0} if fills else {},
        compiler_params=pltpu.CompilerParams(vmem_limit_bytes=48 * MIB),
        name=name,
    )(*after, *given, *small, *big)


def held_until(after, *values):
    def body(*refs):
        pass

    there = pl.BlockSpec(memory_space=pl.ANY)
    return pl.pallas_call(
        body,
        in_specs=[there] * (len(values) + len(after)),
        out_specs=[there] * len(values),
        out_shape=[jax.ShapeDtypeStruct(v.shape, v.dtype) for v in values],
        input_output_aliases={i: i for i in range(len(values))},
        name="held",
    )(*values, *after)


class Copies:
    def __init__(self, sems):
        self.sems = sems
        self.used = 0
        self.open = []

    def start(self, source, target):
        copy = pltpu.make_async_copy(source, target, self.sems.at[self.used])
        self.used += 1
        copy.start()
        return copy

    def out(self, source, target):
        self.open.append(self.start(source, target))

    def finish(self):
        for copy in self.open:
            copy.wait()


def columns(ref, index, size):
    return ref.at[:, index * size : (index + 1) * size]


def sigmoid(value):
    return 0.5 + 0.5 * jnp.tanh(0.5 * value)


def combined(table, counts):
    counts = counts[:, 0:1]
    total = jnp.sum(counts)
    center = jnp.sum(table[:, 0, :], axis=0, keepdims=True) / total
    shift = table[:, 0, :] / jnp.maximum(counts, 1.0) - center
    variance = (
        jnp.sum(table[:, 1, :] + counts * shift * shift, axis=0, keepdims=True) / total
    )
    return center, lax.rsqrt(variance + epsilon)


def store_rows(stats_ref, rows, at=slice(None)):
    table = jnp.concatenate(rows, axis=0)
    stats_ref[:, :, at] = jnp.broadcast_to(table[None], (stats_ref.shape[0],) + table.shape)


def store_moments(stats_ref, values_ref, valid_ref, at=slice(None)):
    valid, values = valid_ref[...], values_ref[...]
    count = jnp.sum(valid)
    first = jnp.sum(values * valid, axis=0, keepdims=True)
    deviation = (values - first / jnp.maximum(count, 1.0)) * valid
    rows = [first, jnp.sum(deviation * deviation, axis=0, keepdims=True)]
    if stats_ref.shape[1] > 2:
        rows.append(jnp.broadcast_to(count, first.shape))
    store_rows(stats_ref, rows, at)


def store_sums(stats_ref, grad, normed, at=slice(None)):
    rows = [jnp.sum(grad, axis=0, keepdims=True), jnp.sum(grad * normed, axis=0, keepdims=True)]
    store_rows(stats_ref, rows, at)


def reduce_kernel(valid_ref, x_ref, w_ref, out_ref, stats_ref, x_buf, w_buf, sems):
    copies = Copies(sems)
    parts = 4
    size = x_ref.shape[1] // parts
    arriving = []
    for k in range(parts):
        arriving.append(
            (
                copies.start(columns(x_ref, k, size), columns(x_buf, k, size)),
                copies.start(w_ref.at[k * size : (k + 1) * size], w_buf.at[k * size : (k + 1) * size]),
            )
        )
    total = None
    for k, pair in enumerate(arriving):
        for copy in pair:
            copy.wait()
        part = dot(x_buf[:, k * size : (k + 1) * size], w_buf[k * size : (k + 1) * size, :], (1, 0))
        total = part if total is None else total + part
    out_ref[...] = total * valid_ref[...]
    store_moments(stats_ref, out_ref, valid_ref)


def pad_edges(acts_ref, side):
    images = acts_ref.shape[1]
    zeros = jnp.zeros((side, acts_ref.shape[3]), bf16)
    for shift in range(3):
        for image in range(images):
            acts_ref[shift, image, 0:side, :] = zeros
            acts_ref[shift, image, (side + 1) * side : (side + 2) * side, :] = zeros


def store_shifted(acts_ref, values, side):
    pixels = values.shape[0]
    column = lax.broadcasted_iota(jnp.int32, (pixels, 1), 0) % side
    before = jnp.where(column == 0, 0.0, pltpu.roll(values, 1, 0))
    after = jnp.where(column == side - 1, 0.0, pltpu.roll(values, pixels - 1, 0))
    for shift, moved in enumerate((before, values, after)):
        for image in range(acts_ref.shape[1]):
            rows = slice(image * side * side, (image + 1) * side * side)
            acts_ref[shift, image, side : side + side * side, :] = moved[rows].astype(bf16)


def window(acts_ref, row_shift, col_shift, side):
    images = acts_ref.shape[1]
    tile = acts_ref[col_shift, :, row_shift * side : row_shift * side + side * side, :]
    return tile.reshape(images * side * side, acts_ref.shape[3])


def spatial_kernel(
    side, pre_ref, table_ref, norm_ref, valid_ref, w_ref, out_ref, consts_ref, stats_ref, acts_out, w_buf, acts_ref, sems
):
    copies = Copies(sems)
    arriving = [copies.start(w_ref.at[k], w_buf.at[k]) for k in range(9)]
    center, inverse = combined(table_ref, table_ref[:, 2, :])
    consts_ref[0:1, :] = center
    consts_ref[1:2, :] = inverse
    gain, bias = norm_ref[0:1, :], norm_ref[1:2, :]
    pad_edges(acts_ref, side)

    shifted = gain * ((pre_ref[...] - center) * inverse) + bias
    store_shifted(acts_ref, valid_ref[...] * shifted * sigmoid(shifted), side)
    copies.out(acts_ref, acts_out)
    total = None
    for tap in range(9):
        arriving[tap].wait()
        part = dot(window(acts_ref, tap // 3, tap % 3, side), w_buf[tap], (1, 0))
        total = part if total is None else total + part
    out_ref[...] = total
    store_moments(stats_ref, out_ref, valid_ref)
    copies.finish()


def expand_kernel(
    pre_ref, table_ref, first_ref, norm_ref, valid_ref, w_ref, act_ref, consts_ref, stats_ref, out, w_buf, out_buf, sems
):
    copies = Copies(sems)
    parts = 4
    size = w_ref.shape[1] // parts
    arriving = [copies.start(columns(w_ref, k, size), columns(w_buf, k, size)) for k in range(parts)]
    center, inverse = combined(table_ref, first_ref[:, 2, :])
    consts_ref[0:1, :] = center
    consts_ref[1:2, :] = inverse
    gain, bias = norm_ref[0:1, :], norm_ref[1:2, :]

    shifted = gain * ((pre_ref[...] - center) * inverse) + bias
    act_ref[...] = (valid_ref[...] * shifted * sigmoid(shifted)).astype(bf16)
    for k in range(parts):
        at = slice(k * size, (k + 1) * size)
        arriving[k].wait()
        out_buf[:, at] = dot(act_ref[...], w_buf[:, at], (1, 0))
        copies.out(columns(out_buf, k, size), columns(out, k, size))
        store_moments(stats_ref, columns(out_buf, k, size), valid_ref, at)
    copies.finish()


def residual_kernel(
    which_ref, table_ref, first_ref, gain_ref, bias_ref, valid_ref, pre_ref, x_ref, merged_ref,
    consts_ref, sums_ref, feat_out, same_out, cross_out, grad_out,
    pre_buf, x_buf, merged_buf, feat_buf, block_buf, grad_buf, sems,
):
    copies = Copies(sems)
    parts = 4
    size = pre_ref.shape[1] // parts
    arriving = []
    for k in range(parts):
        arriving.append(
            [
                copies.start(columns(ref, k, size), columns(buf, k, size))
                for ref, buf in ((pre_ref, pre_buf), (x_ref, x_buf), (merged_ref, merged_buf))
            ]
        )
    for k in range(parts):
        at = slice(k * size, (k + 1) * size)
        center, inverse = combined(table_ref[:, :, at], first_ref[:, 2, :])
        consts_ref[0:1, at] = center
        consts_ref[1:2, at] = inverse
        gain, bias = gain_ref[:, at], bias_ref[:, at]
        for copy in arriving[k]:
            copy.wait()

        valid = valid_ref[...]
        normed = (pre_buf[:, at] - center) * inverse
        value = x_buf[:, at].astype(f32) + gain * normed + bias
        sigma = sigmoid(value)
        features = (valid * (value * sigma)).astype(bf16)
        feat_buf[:, at] = features
        for piece in range(4):
            block_buf[2 * (piece % 2) + piece // 2, :, k * lane : (k + 1) * lane] = features[
                :, piece * lane : (piece + 1) * lane
            ]
        grad = merged_buf[:, at] * valid * (sigma * (1.0 + value * (1.0 - sigma)))
        grad_buf[:, at] = grad
        store_sums(sums_ref, grad, normed, at)
        copies.out(columns(grad_buf, k, size), columns(grad_out, k, size))
        copies.out(columns(feat_buf, k, size), columns(feat_out, k, size))
    for j in range(2):
        copies.out(block_buf.at[which_ref[j]], same_out.at[j])
        copies.out(block_buf.at[which_ref[2 + j]], cross_out.at[j])
    copies.finish()


def slope_rows(grad, pre_ref, consts_ref, norm_ref, valid_ref, out_ref, sums_ref):
    center, inverse = consts_ref[0:1, :], consts_ref[1:2, :]
    gain, bias = norm_ref[0:1, :], norm_ref[1:2, :]
    normed = (pre_ref[...] - center) * inverse
    value = gain * normed + bias
    sigma = sigmoid(value)
    grad = grad * valid_ref[...] * (sigma * (1.0 + value * (1.0 - sigma)))
    out_ref[...] = grad
    store_sums(sums_ref, grad, normed)


def expand_back_kernel(
    which_ref, consts_ref, table_ref, gain_ref, valid_ref, first_ref, mid_pre_ref, mid_consts_ref, mid_norm_ref,
    grad_ref, pre_ref, w_ref,
    totals_ref, shifted_ref, sums_ref, mine_out, sent_out,
    grad_buf, pre_buf, w_buf, out_buf, sems,
):
    copies = Copies(sems)
    parts = 4
    size = pre_ref.shape[1] // parts
    arriving = []
    for k in range(parts):
        arriving.append(
            [
                copies.start(columns(ref, k, size), columns(buf, k, size))
                for ref, buf in ((grad_ref, grad_buf), (pre_ref, pre_buf), (w_ref, w_buf))
            ]
        )
    count = jnp.sum(first_ref[:, 2, 0:1])
    total = None
    for k in range(parts):
        at = slice(k * size, (k + 1) * size)
        totals = jnp.sum(table_ref[:, :, at], axis=0)
        totals_ref[:, at] = totals
        center, inverse = consts_ref[0:1, at], consts_ref[1:2, at]
        plain, scaled = totals[0:1, :] / count, totals[1:2, :] / count
        scale = gain_ref[:, at] * inverse
        for copy in arriving[k]:
            copy.wait()

        normed = (pre_buf[:, at] - center) * inverse
        grad = scale * (grad_buf[:, at] - valid_ref[...] * (plain + normed * scaled))
        out_buf[:, at] = grad.astype(bf16)
        part = dot(out_buf[:, at], w_buf[:, at], (1, 1))
        total = part if total is None else total + part
    half = out_buf.shape[1] // 2
    for place, out in ((which_ref[0], mine_out), (1 - which_ref[0], sent_out)):
        copies.out(out_buf.at[:, pl.ds(pl.multiple_of(place * half, half), half)], out)
    slope_rows(total, mid_pre_ref, mid_consts_ref, mid_norm_ref, valid_ref, shifted_ref, sums_ref)
    copies.finish()


def spatial_back_kernel(
    side, which_ref, grad_ref, pre_ref, consts_ref, table_ref, norm_ref, valid_ref, first_ref,
    low_pre_ref, low_consts_ref, low_norm_ref, w_ref,
    totals_ref, shifted_ref, sums_ref, mine_out, sent_out,
    w_buf, acts_ref, out_ref, sems,
):
    copies = Copies(sems)
    arriving = [copies.start(w_ref.at[k], w_buf.at[k]) for k in range(9)]
    count = jnp.sum(first_ref[:, 2, 0:1])
    totals = jnp.sum(table_ref[...], axis=0)
    totals_ref[...] = totals
    center, inverse = consts_ref[0:1, :], consts_ref[1:2, :]
    plain, scaled = totals[0:1, :] / count, totals[1:2, :] / count
    scale = norm_ref[0:1, :] * inverse
    pad_edges(acts_ref, side)

    normed = (pre_ref[...] - center) * inverse
    grad = scale * (grad_ref[...] - valid_ref[...] * (plain + normed * scaled))
    out_ref[...] = grad.astype(bf16)
    half = out_ref.shape[1] // 2
    for place, out in ((which_ref[0], mine_out), (1 - which_ref[0], sent_out)):
        copies.out(out_ref.at[:, pl.ds(pl.multiple_of(place * half, half), half)], out)
    store_shifted(acts_ref, grad, side)
    total = None
    for tap in range(9):
        arriving[tap].wait()
        part = dot(window(acts_ref, 2 - tap // 3, 2 - tap % 3, side), w_buf[tap], (1, 1))
        total = part if total is None else total + part
    slope_rows(total, low_pre_ref, low_consts_ref, low_norm_ref, valid_ref, shifted_ref, sums_ref)
    copies.finish()


def reduce_back_kernel(
    which_ref, grad_ref, pre_ref, consts_ref, table_ref, norm_ref, valid_ref, first_ref, w_ref, res_ref, x_ref,
    totals_ref, images_out, sent_out, kept_out,
    low_buf, w_buf, res_buf, x_buf, part_buf, sems,
):
    copies = Copies(sems)
    parts = 4
    size = res_ref.shape[1] // parts
    arriving = []
    for k in range(parts):
        at = slice(k * size, (k + 1) * size)
        arriving.append(
            [
                copies.start(columns(x_ref, k, size), columns(x_buf, k, size)),
                copies.start(w_ref.at[at], w_buf.at[at]),
                copies.start(columns(res_ref, k, size), columns(res_buf, k, size)),
            ]
        )
    count = jnp.sum(first_ref[:, 2, 0:1])
    totals = jnp.sum(table_ref[...], axis=0)
    totals_ref[...] = totals
    center, inverse = consts_ref[0:1, :], consts_ref[1:2, :]
    plain, scaled = totals[0:1, :] / count, totals[1:2, :] / count
    scale = norm_ref[0:1, :] * inverse

    normed = (pre_ref[...] - center) * inverse
    grad = scale * (grad_ref[...] - valid_ref[...] * (plain + normed * scaled))
    low_buf[...] = grad.astype(bf16)
    for k in range(parts):
        at = slice(k * size, (k + 1) * size)
        arriving[k][0].wait()
        value = dot(x_buf[:, at], low_buf[...], (0, 0)).astype(bf16)
        peers = part_buf.shape[0] // parts
        dp = slice(k * peers, (k + 1) * peers)
        part_buf[dp] = value.reshape((peers,) + part_buf.shape[1:])
        copies.out(part_buf.at[dp, 1 - which_ref[0]], sent_out.at[dp])
        copies.out(part_buf.at[dp, which_ref[0]], kept_out.at[dp])
    for k in range(parts):
        at = slice(k * size, (k + 1) * size)
        arriving[k][1].wait()
        arriving[k][2].wait()
        res_buf[:, at] = res_buf[:, at] + valid_ref[...] * dot(low_buf[...], w_buf[at, :], (1, 1))
        copies.out(columns(res_buf, k, size), columns(images_out, k, size))
    copies.finish()


def trunk_weights_kernel(
    side, which_ref, act_ref, act_sib, right_ref, right_sib, acts_ref, acts_sib, grad_ref, grad_sib,
    sent_out, kept_out, acts_buf, grad_buf, out_buf, sems,
):
    copies = Copies(sems)
    size = right_ref.shape[1]
    blocks = grad_ref.shape[1] // size
    grads = [copies.start(ref, grad_buf.at[c]) for c, ref in enumerate((grad_ref, grad_sib))]
    acts = [copies.start(ref, acts_buf.at[c]) for c, ref in enumerate((acts_ref, acts_sib))]

    def store(place, value):
        out_buf[place] = value.astype(bf16).reshape(out_buf.shape[1:])
        for q in range(2):
            copies.out(out_buf.at[place, :, which_ref[q]], sent_out.at[q, place])
            copies.out(out_buf.at[place, :, which_ref[2 + q]], kept_out.at[q, place])

    for copy in grads:
        copy.wait()
    for b in range(blocks):
        at = slice(b * size, (b + 1) * size)
        store(b, dot(act_ref[...], grad_buf[0, :, at], (0, 0)) + dot(act_sib[...], grad_buf[1, :, at], (0, 0)))
    for copy in acts:
        copy.wait()
    for tap in range(9):
        tiles = [window(acts_buf.at[c], tap // 3, tap % 3, side) for c in range(2)]
        store(blocks + tap, dot(tiles[0], right_ref[...], (0, 0)) + dot(tiles[1], right_sib[...], (0, 0)))
    copies.finish()


def halve_kernel(axes, which_ref, *refs):
    n = len(axes)
    ins, outs, bufs, sems = refs[: 2 * n], refs[2 * n : 4 * n], refs[4 * n : 6 * n], refs[6 * n]
    copies = Copies(sems)
    arriving = [copies.start(ref, buf) for ref, buf in zip(ins, bufs)]
    first = 0
    for p, axis in enumerate(axes):
        kept_buf, came_buf = bufs[2 * p : 2 * p + 2]
        arriving[2 * p].wait()
        arriving[2 * p + 1].wait()
        kept_buf[...] = (kept_buf[...].astype(f32) + came_buf[...].astype(f32)).astype(bf16)
        count = kept_buf.shape[axis] // 2
        lead = (slice(None),) * axis
        for out in outs[2 * p : 2 * p + 2]:
            for i in range(count):
                target = lead + ((i,) if count > 1 else ())
                copies.out(kept_buf.at[lead + (which_ref[first],)], out.at[target] if target else out)
                first = first + 1
    copies.finish()


def task_kernel(half_ref, cot_ref, w_ref, out, cot_buf, w_buf, out_buf, sems):
    copies = Copies(sems)
    tasks, pixels = out.shape[:2]
    size = w_buf.shape[1]
    parts = w_ref.shape[1] // size
    rows = cot_buf.shape[1]
    start = pl.multiple_of(half_ref[0] * rows, rows)
    cots, arriving = [], []
    for t in range(tasks):
        cots.append(copies.start(cot_ref.at[pl.ds(start, rows), t], cot_buf.at[t]))
        for j in range(parts):
            arriving.append(copies.start(w_ref.at[t, j * size : (j + 1) * size], w_buf.at[t * parts + j]))
    for t in range(tasks):
        cots[t].wait()
        for j in range(parts):
            slot = t * parts + j
            arriving[slot].wait()
            cot = cot_buf[t].reshape(pixels, cot_buf.shape[3])
            out_buf[slot] = dot(cot, w_buf[slot], (1, 1)).astype(bf16)
            copies.out(out_buf.at[slot], out.at[t, :, j * size : (j + 1) * size])
    copies.finish()


def drop_kernel(mine_ref, other_ref, level_ref, out, mine_buf, other_buf, level_buf, out_buf, sems):
    copies = Copies(sems)
    tasks, pixels, _ = mine_ref.shape
    parts = 8
    size = pixels // parts
    arriving = []
    for k in range(parts):
        at = slice(k * size, (k + 1) * size)
        arriving.append(
            [
                copies.start(mine_ref.at[:, at], mine_buf.at[:, at]),
                copies.start(other_ref.at[:, at], other_buf.at[:, at]),
                copies.start(level_ref.at[at], level_buf.at[at]),
            ]
        )
    for k in range(parts):
        for copy in arriving[k]:
            copy.wait()

        rows = slice(k * size, (k + 1) * size)
        grads = [mine_buf[t, rows].astype(f32) + other_buf[t, rows].astype(f32) for t in range(tasks)]
        total, spread = None, None
        for grad in grads:
            squared = grad * grad + 1.0
            root = squared * lax.rsqrt(squared)
            spread = root if spread is None else spread + root
            total = grad if total is None else total + grad
        margin = (0.25 * steepness) * (total / spread) + (
            0.25 * steepness * (1.0 - 1.0 / levels)
            - level_buf[rows].astype(f32) * (0.5 * steepness / levels)
        )
        merged = total
        for grad in grads:
            merged = merged + grad * jnp.tanh(jnp.tanh(grad) * margin)
        out_buf[rows] = 0.5 * merged
        at = slice(k * size, (k + 1) * size)
        copies.out(out_buf.at[at], out.at[at])
    copies.finish()


def heads_kernel(first, which_ref, own_ref, sib_ref, w_ref, out, own_buf, sib_buf, w_buf, out_buf, sems):
    copies = Copies(sems)
    core = which_ref[0]
    tasks = w_buf.shape[0]
    lanes = w_ref.shape[2]
    size = lanes // 2
    rows = out.shape[0] // 2
    arriving = []
    features = []
    for t in range(tasks):
        for j in range(2):
            at = slice(j * size, (j + 1) * size)
            arriving.append(copies.start(w_ref.at[first + t, :, at], w_buf.at[t, :, at]))
            if not features:
                features = [copies.start(own_ref, own_buf), copies.start(sib_ref, sib_buf)]
    for t in range(tasks):
        for j in range(2):
            at = slice(j * size, (j + 1) * size)
            arriving[2 * t + j].wait()
            for s, (source, place) in enumerate(((own_buf, core), (sib_buf, 1 - core))):
                if t + j == 0:
                    features[s].wait()
                value = dot(source[...], w_buf[t, :, at], (1, 0)).astype(bf16)
                out_buf[t, s, :, :, at] = value.reshape(rows, out.shape[2], size)
                copies.out(
                    out_buf.at[t, s, :, :, at],
                    out.at[pl.ds(pl.multiple_of(place * rows, rows), rows), first + t, :, at],
                )
    copies.finish()


def weights_kernel(near, which_ref, first_ref, second_ref, cot_ref, *refs):
    added_ref, refs = (None, refs) if near else (refs[0], refs[1:])
    out, feat_buf, flip_buf, cot_buf, out_buf, sems = refs
    copies = Copies(sems)
    core = which_ref[0]
    tasks = out.shape[0]
    pixels, channels = feat_buf.shape[2:]
    pieces = channels // lane
    lanes = cot_buf.shape[4]
    rows = cot_buf.shape[2]
    features = []
    for j in range(2):
        for s, ref in enumerate((first_ref, second_ref)):
            if near:
                features.append(
                    [
                        copies.start(
                            ref.at[:, pl.ds(pl.multiple_of((4 * piece + which_ref[1 + j]) * lane, lane), lane)],
                            feat_buf.at[j, s, :, piece * lane : (piece + 1) * lane],
                        )
                        for piece in range(pieces)
                    ]
                )
            else:
                features.append([copies.start(ref.at[j], feat_buf.at[j, s])])
    start = 0 if near else which_ref[3] * (2 * rows)
    cots, more = [], []
    for t in range(tasks):
        cots.append(
            [
                copies.start(
                    cot_ref.at[pl.ds(pl.multiple_of(start + place * rows, rows), rows), t], cot_buf.at[t, s]
                )
                for s, place in enumerate((core, 1 - core))
            ]
        )
        if not near:
            more.append([copies.start(added_ref.at[t, j], out_buf.at[t, j]) for j in range(2)])
    for t in range(tasks):
        for j in range(2):
            if t == 0:
                for s in range(2):
                    for copy in features[2 * j + s]:
                        copy.wait()
                    flip_buf[j, :, s * pixels : (s + 1) * pixels] = feat_buf[j, s].T
            if j == 0:
                for copy in cots[t]:
                    copy.wait()
            value = dot(flip_buf[j], cot_buf[t].reshape(2 * pixels, lanes), (1, 0))
            if not near:
                more[t][j].wait()
                value = value + out_buf[t, j].astype(f32)
            out_buf[t, j] = value.astype(bf16)
            copies.out(out_buf.at[t, j], out.at[t, j])
    copies.finish()


def validity(bucket_shape, pixel_mask):
    row_index = lax.broadcasted_iota(jnp.int32, pixel_mask.shape, 1)
    col_index = lax.broadcasted_iota(jnp.int32, pixel_mask.shape, 2)
    inside = (row_index < bucket_shape[:, 0][:, None, None]) & (
        col_index < bucket_shape[:, 1][:, None, None]
    )
    return jnp.where(inside, pixel_mask, 0).astype(f32)


def from_everyone(rows):
    return lax.all_to_all(rows, everyone, 0, 0, tiled=True)


def swap_core(value):
    return lax.ppermute(value, "task", [(0, 1), (1, 0)])


def pick(value, axis, index):
    return lax.dynamic_index_in_dim(value, index, axis, keepdims=False)


def two(value, axis, first, second):
    return jnp.stack([pick(value, axis, first), pick(value, axis, second)], axis)


def on_device(
    images,
    bucket_shape,
    pixel_mask,
    thresholds,
    reduce_weight,
    spatial_weight,
    expand_weight,
    mid_gains,
    mid_biases,
    out_gain,
    out_bias,
    head_weights,
    head_cotangent,
):
    image_count = images.shape[0]
    side = images.shape[1]
    width = images.shape[3]
    middle = reduce_weight.shape[1]
    tasks = head_weights.shape[1]
    lanes = head_weights.shape[2]
    pixels = image_count * side * side
    peers = lax.axis_size("dp")
    devices = 2 * peers
    core = lax.axis_index("task")
    low = max(0, (lane * peers // width).bit_length() - 1)
    bit_x, bit_y = 1 << low, 2 << low
    position = lax.axis_index("dp")
    my_x, my_y = (position >> low) & 1, (position >> (low + 1)) & 1
    def pairing(bit_of, cross):
        pairs = []
        for i in range(peers):
            for c in range(2):
                if cross:
                    pairs.append((2 * i + c, 2 * (i ^ bit_of[1 - c]) + 1 - c))
                else:
                    pairs.append((2 * i + c, 2 * (i ^ bit_of[c]) + c))
        return pairs

    def swap_first(value):
        return lax.ppermute(value, everyone, pairing((bit_x, bit_y), False))

    def swap_second(value):
        return lax.ppermute(value, everyone, pairing((bit_y, bit_x), False))

    def swap_cross(value):
        return lax.ppermute(value, everyone, pairing((bit_x, bit_y), True))

    def by_core(zero, one):
        return jnp.where(core == 0, zero, one)

    twos = []
    for i in range(peers):
        for c, bit in enumerate((bit_y, bit_x)):
            if not i & bit:
                twos.append([2 * i + c, 2 * (i | bit) + c])
    rest_bits = [b for b in range(peers.bit_length() - 1) if not (1 << b) & (bit_x | bit_y)]

    def swap_rest(value, done):
        bit = rest_bits[done]
        return lax.ppermute(value, "dp", [(i, i ^ (1 << bit)) for i in range(peers)])

    def halved(pairs, after=()):
        outs, scratch, big, which, count = [], [], [], [], 0
        for kept, came, axis, indices in pairs:
            half = kept.shape[axis] // 2
            shape = kept.shape[:axis] + ((half,) if half > 1 else ()) + kept.shape[axis + 1 :]
            outs += [(shape, bf16, True)] * 2
            scratch += [pltpu.VMEM(kept.shape, bf16)] * 2
            big += [kept, came]
            which += list(indices)
            count += 2 + 2 * half
        return kernel_call(
            functools.partial(halve_kernel, tuple(axis for _, _, axis, _ in pairs)),
            outs,
            big=tuple(big),
            scalars=scalars(*which),
            scratch=scratch,
            copies=count,
            after=after,
            name="halve",
        )

    def rest_part(kept, came, dim, done):
        mine = (position >> rest_bits[done]) & 1
        return kept, came, dim + len(rest_bits) - 1 - done, (1 - mine, mine)

    fours, rests = {}, {}
    for i in range(peers):
        fours.setdefault(i & ~(bit_x | bit_y), []).append(i)
        rests.setdefault(i & (bit_x | bit_y), []).append(i)
    fours, rests = list(fours.values()), list(rests.values())

    def exchanged(value, members):
        came = lax.all_to_all(value, "dp", 0, 0, axis_index_groups=members, tiled=True)
        return jnp.sum(came.astype(f32), axis=0)

    inputs = images.reshape(pixels, width)
    valid = validity(bucket_shape, pixel_mask).reshape(pixels, 1)
    norms = jnp.stack([mid_gains, mid_biases], axis=1)
    gain_row, bias_row = out_gain.reshape(1, width), out_bias.reshape(1, width)
    levels_flat = thresholds.reshape(pixels, width)
    cot = head_cotangent.transpose(0, 1, 3, 2, 4).reshape(2 * image_count * side, tasks, side, lanes)
    rows_half = image_count * side
    weights = head_weights.transpose(1, 0, 2)
    half_lanes = lanes // 2
    block = 4 * lane
    blocks = width // block

    pairs = []
    for i in range(peers):
        for c, bit in enumerate((bit_x, bit_y)):
            if not i & bit:
                pairs.append([2 * i + c, 2 * (i ^ bit) + c])
    pair_cot = lax.all_gather(cot, everyone, axis=0, tiled=True, axis_index_groups=pairs)

    mid = (pixels, middle)
    whole = (pixels, width)
    pair = (2, middle)
    stat_two, stat_three = (devices, 2, middle), (devices, 3, middle)

    def scalars(*values):
        return jnp.stack(values).astype(jnp.int32)

    def task_half(half, after):
        return kernel_call(
            task_kernel,
            [((tasks, pixels, width), bf16, True)],
            big=(cot, weights),
            scalars=scalars(half),
            scratch=[
                pltpu.VMEM((tasks, rows_half, side, lanes), bf16),
                pltpu.VMEM((2 * tasks, width // 2, lanes), bf16),
                pltpu.VMEM((2 * tasks, pixels, width // 2), bf16),
            ],
            copies=5 * tasks,
            after=after,
            name="task_grad",
        )[0]

    pre_reduce, stats = kernel_call(
        reduce_kernel,
        [(mid, f32, False), (stat_three, f32, False)],
        small=(valid,),
        big=(inputs, reduce_weight),
        scratch=[pltpu.VMEM(whole, bf16), pltpu.VMEM(reduce_weight.shape, bf16)],
        copies=8,
        after=(norms,),
        name="reduce",
    )
    table_one = from_everyone(stats)
    task_mine = task_half(core, (stats,))

    padded = (3, image_count, (side + 2) * side, middle)
    pre_spatial, consts_one, stats, acts = kernel_call(
        functools.partial(spatial_kernel, side),
        [(mid, f32, False), (pair, f32, False), (stat_two, f32, False), (padded, bf16, True)],
        small=(pre_reduce, table_one, norms[0], valid),
        big=(spatial_weight,),
        scratch=[pltpu.VMEM(spatial_weight.shape, bf16), pltpu.VMEM(padded, bf16)],
        copies=10,
        after=(task_mine,),
        name="spatial",
    )
    table_two = from_everyone(stats)
    task_sent = task_half(1 - core, (stats,))
    task_other = swap_core(held_until((table_two,), task_sent)[0])

    act_spatial, consts_two, stats, pre_expand = kernel_call(
        expand_kernel,
        [(mid, bf16, False), (pair, f32, False), ((devices, 2, width), f32, False), (whole, f32, True)],
        small=(pre_spatial, table_two, table_one, norms[1], valid),
        big=(expand_weight,),
        scratch=[pltpu.VMEM(expand_weight.shape, bf16), pltpu.VMEM(whole, f32)],
        copies=8,
        after=(task_sent,),
        name="expand",
    )
    table_three = from_everyone(stats)
    (merged,) = kernel_call(
        drop_kernel,
        [(whole, f32, True)],
        big=(task_mine, task_other, levels_flat),
        scratch=[
            pltpu.VMEM((tasks,) + whole, bf16),
            pltpu.VMEM((tasks,) + whole, bf16),
            pltpu.VMEM(whole, jnp.int32),
            pltpu.VMEM(whole, f32),
        ],
        copies=32,
        after=(stats,),
        name="graddrop",
    )


    pair_blocks = (2, pixels, width // 4)
    x_send, y_send = 2 * (1 - my_x), 1 - my_y
    consts_three, sums, features, same, cross, grad_residual = kernel_call(
        residual_kernel,
        [
            ((2, width), f32, False),
            ((devices, 2, width), f32, False),
            (whole, bf16, True),
            (pair_blocks, bf16, True),
            (pair_blocks, bf16, True),
            (whole, f32, True),
        ],
        scalars=scalars(
            by_core(x_send, y_send),
            by_core(x_send + 1, y_send + 2),
            by_core(y_send, x_send),
            by_core(y_send + 2, x_send + 1),
        ),
        small=(table_three, table_one, gain_row, bias_row, valid),
        big=(pre_expand, inputs, merged),
        scratch=[
            pltpu.VMEM(whole, f32),
            pltpu.VMEM(whole, bf16),
            pltpu.VMEM(whole, f32),
            pltpu.VMEM(whole, bf16),
            pltpu.VMEM((4, pixels, width // 4), bf16),
            pltpu.VMEM(whole, f32),
        ],
        copies=24,
        name="residual",
    )
    table_four = from_everyone(sums)
    sibling = swap_core(features)
    far = swap_first(same)
    far_cross = swap_cross(cross)
    acts, act_spatial = held_until((features,), acts, act_spatial)
    acts_sib, act_spatial_sib = swap_core(acts), swap_core(act_spatial)

    def heads(first, count, after, fills):
        return kernel_call(
            functools.partial(heads_kernel, first),
            [(cot.shape, bf16, True)],
            big=(features, sibling, weights),
            scalars=scalars(core),
            scratch=[
                pltpu.VMEM(whole, bf16),
                pltpu.VMEM(whole, bf16),
                pltpu.VMEM((count, width, lanes), bf16),
                pltpu.VMEM((count, 2, rows_half, side, lanes), bf16),
            ],
            copies=2 + 6 * count,
            after=after,
            fills=fills,
            name="heads",
        )[0]

    head_values = heads(0, 2, (sums,), False)

    part_shape = (tasks, 2, width // 4, lanes)

    def weight_part(near, first, second, cots, added, after):
        return kernel_call(
            functools.partial(weights_kernel, near),
            [(part_shape, bf16, True)],
            big=(first, second, cots) + added,
            scalars=scalars(
                core,
                by_core(my_x, 2 * my_y),
                by_core(my_x + 2, 2 * my_y + 1),
                1 - by_core(my_x, my_y),
            ),
            scratch=[
                pltpu.VMEM((2, 2, pixels, width // 4), bf16),
                pltpu.VMEM((2, width // 4, 2 * pixels), bf16),
                pltpu.VMEM((tasks, 2, rows_half, side, lanes), bf16),
                pltpu.VMEM(part_shape, bf16),
            ],
            copies=4 * blocks + 10 * tasks,
            after=after,
            name="heads_grad",
        )[0]

    near_part = weight_part(True, features, sibling, cot, (), (head_values,))
    index = by_core(my_y, my_x)

    heads_part = weight_part(False, far, far_cross, pair_cot, (near_part,), (near_part,))
    (heads_part,) = held_until((table_four,), heads_part)
    heads_half = lax.psum_scatter(
        heads_part.reshape(tasks, width // 2, lanes),
        everyone,
        scatter_dimension=1,
        axis_index_groups=twos,
        tiled=True,
    )

    expand_half, spatial_half = (pixels, width // 2), (pixels, middle // 2)
    out_totals, shifted_two, sums, expand_mine, expand_sent = kernel_call(
        expand_back_kernel,
        [
            ((2, width), f32, False),
            (mid, f32, False),
            (stat_two, f32, False),
            (expand_half, bf16, True),
            (expand_half, bf16, True),
        ],
        scalars=scalars(core),
        small=(consts_three, table_four, gain_row, valid, table_one, pre_spatial, consts_two, norms[1]),
        big=(grad_residual, pre_expand, expand_weight),
        scratch=[
            pltpu.VMEM(whole, f32),
            pltpu.VMEM(whole, f32),
            pltpu.VMEM(expand_weight.shape, bf16),
            pltpu.VMEM(whole, bf16),
        ],
        copies=14,
        after=(heads_part,),
        name="expand_back",
    )
    table_five = from_everyone(sums)
    expand_sib = swap_core(expand_sent)
    head_values = heads(2, tasks - 2, (head_values, sums), True)
    head_output = head_values.reshape(2 * image_count, side, tasks, side, lanes).transpose(0, 1, 3, 2, 4)
    totals_two, shifted_one, sums, spatial_mine, spatial_sent = kernel_call(
        functools.partial(spatial_back_kernel, side),
        [
            (pair, f32, False),
            (mid, f32, False),
            (stat_two, f32, False),
            (spatial_half, bf16, True),
            (spatial_half, bf16, True),
        ],
        scalars=scalars(core),
        small=(
            shifted_two, pre_spatial, consts_two, table_five, norms[1], valid, table_one,
            pre_reduce, consts_one, norms[0],
        ),
        big=(spatial_weight,),
        scratch=[
            pltpu.VMEM(spatial_weight.shape, bf16),
            pltpu.VMEM(padded, bf16),
            pltpu.VMEM(mid, bf16),
        ],
        copies=11,
        after=(head_values,),
        name="spatial_back",
    )
    table_six = from_everyone(sums)
    spatial_sib = swap_core(spatial_sent)
    x_out, y_out, x_in, y_in = 1 - my_x, 2 * (1 - my_y), my_x, 2 * my_y
    pair_parts = (
        by_core(x_out, y_out),
        by_core(x_out + 2, y_out + 1),
        by_core(x_in, y_in),
        by_core(x_in + 2, y_in + 1),
    )
    high, rows_of_pair = peers >> (low + 2), (1 << low) * (middle // peers)
    early_shape = (2, blocks + 9, high, rows_of_pair, middle // 2)
    early_sent, early_kept = kernel_call(
        functools.partial(trunk_weights_kernel, side),
        [(early_shape, bf16, True), (early_shape, bf16, True)],
        scalars=scalars(*pair_parts),
        small=(act_spatial, act_spatial_sib, spatial_mine, spatial_sib),
        big=(acts, acts_sib, expand_mine, expand_sib),
        scratch=[
            pltpu.VMEM((2,) + padded, bf16),
            pltpu.VMEM((2,) + expand_half, bf16),
            pltpu.VMEM((blocks + 9, high, 4, rows_of_pair, middle // 2), bf16),
        ],
        copies=4 + 4 * (blocks + 9),
        after=(sums,),
        name="trunk_weights",
    )
    early_sent, heads_half = held_until((table_six,), early_sent, heads_half)
    heads_grad = lax.psum_scatter(
        heads_half, "dp", scatter_dimension=1, axis_index_groups=rests, tiled=True
    )
    heads_grad = heads_grad.astype(f32).transpose(1, 0, 2)
    early_came = swap_first(early_sent)
    dp_rows = (peers, width // devices, middle)
    totals_one, images_grad, reduce_sent, reduce_kept = kernel_call(
        reduce_back_kernel,
        [(pair, f32, False), (whole, f32, True), (dp_rows, bf16, True), (dp_rows, bf16, True)],
        scalars=scalars(core),
        small=(shifted_one, pre_reduce, consts_one, table_six, norms[0], valid, table_one),
        big=(reduce_weight, grad_residual, inputs),
        scratch=[
            pltpu.VMEM(mid, bf16),
            pltpu.VMEM(reduce_weight.shape, bf16),
            pltpu.VMEM(whole, f32),
            pltpu.VMEM(whole, bf16),
            pltpu.VMEM((peers, 2, width // devices, middle), bf16),
        ],
        copies=24,
        after=(early_kept,),
        name="reduce_back",
    )
    reduce_came = swap_core(reduce_sent)
    quarters = (high, 4, (1 << low) * dp_rows[1], middle)
    reduce_sent, reduce_kept = halved(
        [(reduce_kept.reshape(quarters), reduce_came.reshape(quarters), 1, pair_parts)]
    )
    reduce_came = swap_first(reduce_sent)
    early_sent, early_kept, reduce_sent, reduce_kept = halved(
        [
            (early_kept, early_came, 0, (1 - index, index)),
            (reduce_kept, reduce_came, 1, (1 - index, index)),
        ]
    )
    early_came, reduce_came = swap_second(early_sent), swap_second(reduce_sent)
    early_open = (blocks + 9,) + (2,) * len(rest_bits) + (-1, middle // 2)
    reduce_open = (2,) * len(rest_bits) + (-1, middle)
    early_kept, early_came = early_kept.reshape(early_open), early_came.reshape(early_open)
    reduce_kept, reduce_came = reduce_kept.reshape(reduce_open), reduce_came.reshape(reduce_open)
    for done in range(len(rest_bits)):
        early_sent, early_kept, reduce_sent, reduce_kept = halved(
            [rest_part(early_kept, early_came, 1, done), rest_part(reduce_kept, reduce_came, 0, done)]
        )
        early_came, reduce_came = swap_rest(early_sent, done), swap_rest(reduce_sent, done)
    early = early_kept.astype(f32) + early_came.astype(f32)
    reduce_grad = reduce_kept.astype(f32) + reduce_came.astype(f32)

    own_rows = early.reshape(early.shape[0], 2, -1, early.shape[2])
    came_rows = swap_core(pick(own_rows, 1, 1 - core))
    own_rows = pick(own_rows, 1, core)
    halves = jnp.stack(
        [jnp.where(core == 0, own_rows, came_rows), jnp.where(core == 0, came_rows, own_rows)]
    ).astype(f32)
    expand_grad = halves[:, :blocks].transpose(2, 0, 1, 3).reshape(middle // devices, width)
    spatial_grad = halves[:, blocks:].transpose(1, 2, 0, 3).reshape(9, middle // devices, middle)
    gains_grad = jnp.stack([totals_one[1], totals_two[1]], axis=0)
    biases_grad = jnp.stack([totals_one[0], totals_two[0]], axis=0)
    return (
        head_output,
        images_grad.reshape(images.shape),
        reduce_grad,
        spatial_grad,
        expand_grad,
        gains_grad,
        biases_grad,
        out_totals[1],
        out_totals[0],
        heads_grad,
    )


def solution(mesh):
    placed = (
        P(("dp", "task"), None, None, None),
        P(("dp", "task"), None),
        P(("dp", "task"), None, None),
        P(("dp", "task"), None, None, None),
        P(),
        P(),
        P(),
        P(),
        P(),
        P(),
        P(),
        P(None, None, "task"),
        P("dp", None, None, None, "task"),
    )
    return jax.shard_map(
        on_device,
        mesh=mesh,
        in_specs=placed,
        out_specs=(
            P("dp", None, None, None, "task"),
            P(("dp", "task"), None, None, None),
            P(("dp", "task"), None),
            P(None, ("dp", "task"), None),
            P(("dp", "task"), None),
            P(),
            P(),
            P(),
            P(),
            P("dp", None, "task"),
        ),
        check_vma=False,
    )
```

```python
import functools

import jax
import jax.numpy as jnp
from jax import lax
from jax.experimental import pallas as pl
from jax.experimental.pallas import tpu as pltpu
from jax.sharding import PartitionSpec as P

epsilon = 1e-05
steepness = 6.0
levels = 4096.0
everyone = ("dp", "task")
f32 = jnp.float32
bf16 = jnp.bfloat16
lane = 128
MIB = 1 << 20


def dot(left, right, contract):
    return lax.dot_general(
        left, right, ((contract[0:1], contract[1:2]), ((), ())), preferred_element_type=f32
    )


def kernel_call(body, outs, small=(), big=(), scalars=None, scratch=(), copies=0, after=(), fills=False, name=None):
    skipped = len(after)

    def ordered(*refs):
        body(*refs[skipped:])

    big = [pltpu.with_memory_space_constraint(array, pltpu.HBM) for array in big]
    there = pl.BlockSpec(memory_space=pl.ANY)
    here = pl.BlockSpec(memory_space=pltpu.VMEM)
    given = [] if scalars is None else [scalars]
    return pl.pallas_call(
        ordered,
        in_specs=[there] * skipped
        + [pl.BlockSpec(memory_space=pltpu.SMEM)] * len(given)
        + [here] * len(small)
        + [there] * len(big),
        out_specs=[there if streamed else here for _, _, streamed in outs],
        out_shape=[
            pltpu.HBM(shape, dtype) if streamed else jax.ShapeDtypeStruct(shape, dtype)
            for shape, dtype, streamed in outs
        ],
        scratch_shapes=list(scratch) + ([pltpu.SemaphoreType.DMA((copies,))] if copies else []),
        input_output_aliases={0: 0} if fills else {},
        compiler_params=pltpu.CompilerParams(vmem_limit_bytes=48 * MIB),
        name=name,
    )(*after, *given, *small, *big)


def held_until(after, *values):
    def body(*refs):
        pass

    there = pl.BlockSpec(memory_space=pl.ANY)
    return pl.pallas_call(
        body,
        in_specs=[there] * (len(values) + len(after)),
        out_specs=[there] * len(values),
        out_shape=[jax.ShapeDtypeStruct(v.shape, v.dtype) for v in values],
        input_output_aliases={i: i for i in range(len(values))},
        name="held",
    )(*values, *after)


class Copies:
    def __init__(self, sems):
        self.sems = sems
        self.used = 0
        self.open = []

    def start(self, source, target):
        copy = pltpu.make_async_copy(source, target, self.sems.at[self.used])
        self.used += 1
        copy.start()
        return copy

    def out(self, source, target):
        self.open.append(self.start(source, target))

    def finish(self):
        for copy in self.open:
            copy.wait()


def columns(ref, index, size):
    return ref.at[:, index * size : (index + 1) * size]


def sigmoid(value):
    return 0.5 + 0.5 * jnp.tanh(0.5 * value)


def combined(table, counts):
    counts = counts[:, 0:1]
    total = jnp.sum(counts)
    center = jnp.sum(table[:, 0, :], axis=0, keepdims=True) / total
    shift = table[:, 0, :] / jnp.maximum(counts, 1.0) - center
    variance = (
        jnp.sum(table[:, 1, :] + counts * shift * shift, axis=0, keepdims=True) / total
    )
    return center, lax.rsqrt(variance + epsilon)


def store_rows(stats_ref, rows, at=slice(None)):
    table = jnp.concatenate(rows, axis=0)
    stats_ref[:, :, at] = jnp.broadcast_to(table[None], (stats_ref.shape[0],) + table.shape)


def store_moments(stats_ref, values_ref, valid_ref, at=slice(None)):
    valid, values = valid_ref[...], values_ref[...]
    count = jnp.sum(valid)
    first = jnp.sum(values * valid, axis=0, keepdims=True)
    deviation = (values - first / jnp.maximum(count, 1.0)) * valid
    rows = [first, jnp.sum(deviation * deviation, axis=0, keepdims=True)]
    if stats_ref.shape[1] > 2:
        rows.append(jnp.broadcast_to(count, first.shape))
    store_rows(stats_ref, rows, at)


def store_sums(stats_ref, grad, normed, at=slice(None)):
    rows = [jnp.sum(grad, axis=0, keepdims=True), jnp.sum(grad * normed, axis=0, keepdims=True)]
    store_rows(stats_ref, rows, at)


def reduce_kernel(valid_ref, x_ref, w_ref, out_ref, stats_ref, x_buf, w_buf, sems):
    copies = Copies(sems)
    parts = 4
    size = x_ref.shape[1] // parts
    arriving = []
    for k in range(parts):
        arriving.append(
            (
                copies.start(columns(x_ref, k, size), columns(x_buf, k, size)),
                copies.start(w_ref.at[k * size : (k + 1) * size], w_buf.at[k * size : (k + 1) * size]),
            )
        )
    total = None
    for k, pair in enumerate(arriving):
        for copy in pair:
            copy.wait()
        part = dot(x_buf[:, k * size : (k + 1) * size], w_buf[k * size : (k + 1) * size, :], (1, 0))
        total = part if total is None else total + part
    out_ref[...] = total * valid_ref[...]
    store_moments(stats_ref, out_ref, valid_ref)


def pad_edges(acts_ref, side):
    images = acts_ref.shape[1]
    zeros = jnp.zeros((side, acts_ref.shape[3]), bf16)
    for shift in range(3):
        for image in range(images):
            acts_ref[shift, image, 0:side, :] = zeros
            acts_ref[shift, image, (side + 1) * side : (side + 2) * side, :] = zeros


def store_shifted(acts_ref, values, side):
    pixels = values.shape[0]
    column = lax.broadcasted_iota(jnp.int32, (pixels, 1), 0) % side
    before = jnp.where(column == 0, 0.0, pltpu.roll(values, 1, 0))
    after = jnp.where(column == side - 1, 0.0, pltpu.roll(values, pixels - 1, 0))
    for shift, moved in enumerate((before, values, after)):
        for image in range(acts_ref.shape[1]):
            rows = slice(image * side * side, (image + 1) * side * side)
            acts_ref[shift, image, side : side + side * side, :] = moved[rows].astype(bf16)


def window(acts_ref, row_shift, col_shift, side):
    images = acts_ref.shape[1]
    tile = acts_ref[col_shift, :, row_shift * side : row_shift * side + side * side, :]
    return tile.reshape(images * side * side, acts_ref.shape[3])


def spatial_kernel(
    side, pre_ref, table_ref, norm_ref, valid_ref, w_ref, out_ref, consts_ref, stats_ref, acts_out, w_buf, acts_ref, sems
):
    copies = Copies(sems)
    arriving = [copies.start(w_ref.at[k], w_buf.at[k]) for k in range(9)]
    center, inverse = combined(table_ref, table_ref[:, 2, :])
    consts_ref[0:1, :] = center
    consts_ref[1:2, :] = inverse
    gain, bias = norm_ref[0:1, :], norm_ref[1:2, :]
    pad_edges(acts_ref, side)

    shifted = gain * ((pre_ref[...] - center) * inverse) + bias
    store_shifted(acts_ref, valid_ref[...] * shifted * sigmoid(shifted), side)
    copies.out(acts_ref, acts_out)
    total = None
    for tap in range(9):
        arriving[tap].wait()
        part = dot(window(acts_ref, tap // 3, tap % 3, side), w_buf[tap], (1, 0))
        total = part if total is None else total + part
    out_ref[...] = total
    store_moments(stats_ref, out_ref, valid_ref)
    copies.finish()


def expand_kernel(
    pre_ref, table_ref, first_ref, norm_ref, valid_ref, w_ref, act_ref, consts_ref, stats_ref, out, w_buf, out_buf, sems
):
    copies = Copies(sems)
    parts = 4
    size = w_ref.shape[1] // parts
    arriving = [copies.start(columns(w_ref, k, size), columns(w_buf, k, size)) for k in range(parts)]
    center, inverse = combined(table_ref, first_ref[:, 2, :])
    consts_ref[0:1, :] = center
    consts_ref[1:2, :] = inverse
    gain, bias = norm_ref[0:1, :], norm_ref[1:2, :]

    shifted = gain * ((pre_ref[...] - center) * inverse) + bias
    act_ref[...] = (valid_ref[...] * shifted * sigmoid(shifted)).astype(bf16)
    for k in range(parts):
        at = slice(k * size, (k + 1) * size)
        arriving[k].wait()
        out_buf[:, at] = dot(act_ref[...], w_buf[:, at], (1, 0))
        copies.out(columns(out_buf, k, size), columns(out, k, size))
        store_moments(stats_ref, columns(out_buf, k, size), valid_ref, at)
    copies.finish()


def residual_kernel(
    which_ref, table_ref, first_ref, gain_ref, bias_ref, valid_ref, pre_ref, x_ref, merged_ref,
    consts_ref, sums_ref, feat_out, same_out, cross_out, grad_out,
    pre_buf, x_buf, merged_buf, feat_buf, block_buf, grad_buf, sems,
):
    copies = Copies(sems)
    parts = 4
    size = pre_ref.shape[1] // parts
    arriving = []
    for k in range(parts):
        arriving.append(
            [
                copies.start(columns(ref, k, size), columns(buf, k, size))
                for ref, buf in ((pre_ref, pre_buf), (x_ref, x_buf), (merged_ref, merged_buf))
            ]
        )
    for k in range(parts):
        at = slice(k * size, (k + 1) * size)
        center, inverse = combined(table_ref[:, :, at], first_ref[:, 2, :])
        consts_ref[0:1, at] = center
        consts_ref[1:2, at] = inverse
        gain, bias = gain_ref[:, at], bias_ref[:, at]
        for copy in arriving[k]:
            copy.wait()

        valid = valid_ref[...]
        normed = (pre_buf[:, at] - center) * inverse
        value = x_buf[:, at].astype(f32) + gain * normed + bias
        sigma = sigmoid(value)
        features = (valid * (value * sigma)).astype(bf16)
        feat_buf[:, at] = features
        for piece in range(4):
            block_buf[2 * (piece % 2) + piece // 2, :, k * lane : (k + 1) * lane] = features[
                :, piece * lane : (piece + 1) * lane
            ]
        grad = merged_buf[:, at] * valid * (sigma * (1.0 + value * (1.0 - sigma)))
        grad_buf[:, at] = grad
        store_sums(sums_ref, grad, normed, at)
        copies.out(columns(grad_buf, k, size), columns(grad_out, k, size))
        copies.out(columns(feat_buf, k, size), columns(feat_out, k, size))
    for j in range(2):
        copies.out(block_buf.at[which_ref[j]], same_out.at[j])
        copies.out(block_buf.at[which_ref[2 + j]], cross_out.at[j])
    copies.finish()


def slope_rows(grad, pre_ref, consts_ref, norm_ref, valid_ref, out_ref, sums_ref):
    center, inverse = consts_ref[0:1, :], consts_ref[1:2, :]
    gain, bias = norm_ref[0:1, :], norm_ref[1:2, :]
    normed = (pre_ref[...] - center) * inverse
    value = gain * normed + bias
    sigma = sigmoid(value)
    grad = grad * valid_ref[...] * (sigma * (1.0 + value * (1.0 - sigma)))
    out_ref[...] = grad
    store_sums(sums_ref, grad, normed)


def expand_back_kernel(
    which_ref, consts_ref, table_ref, gain_ref, valid_ref, first_ref, mid_pre_ref, mid_consts_ref, mid_norm_ref,
    grad_ref, pre_ref, w_ref,
    totals_ref, shifted_ref, sums_ref, mine_out, sent_out,
    grad_buf, pre_buf, w_buf, out_buf, sems,
):
    copies = Copies(sems)
    parts = 4
    size = pre_ref.shape[1] // parts
    arriving = []
    for k in range(parts):
        arriving.append(
            [
                copies.start(columns(ref, k, size), columns(buf, k, size))
                for ref, buf in ((grad_ref, grad_buf), (pre_ref, pre_buf), (w_ref, w_buf))
            ]
        )
    count = jnp.sum(first_ref[:, 2, 0:1])
    total = None
    for k in range(parts):
        at = slice(k * size, (k + 1) * size)
        totals = jnp.sum(table_ref[:, :, at], axis=0)
        totals_ref[:, at] = totals
        center, inverse = consts_ref[0:1, at], consts_ref[1:2, at]
        plain, scaled = totals[0:1, :] / count, totals[1:2, :] / count
        scale = gain_ref[:, at] * inverse
        for copy in arriving[k]:
            copy.wait()

        normed = (pre_buf[:, at] - center) * inverse
        grad = scale * (grad_buf[:, at] - valid_ref[...] * (plain + normed * scaled))
        out_buf[:, at] = grad.astype(bf16)
        part = dot(out_buf[:, at], w_buf[:, at], (1, 1))
        total = part if total is None else total + part
    half = out_buf.shape[1] // 2
    for place, out in ((which_ref[0], mine_out), (1 - which_ref[0], sent_out)):
        copies.out(out_buf.at[:, pl.ds(pl.multiple_of(place * half, half), half)], out)
    slope_rows(total, mid_pre_ref, mid_consts_ref, mid_norm_ref, valid_ref, shifted_ref, sums_ref)
    copies.finish()


def spatial_back_kernel(
    side, which_ref, grad_ref, pre_ref, consts_ref, table_ref, norm_ref, valid_ref, first_ref,
    low_pre_ref, low_consts_ref, low_norm_ref, w_ref,
    totals_ref, shifted_ref, sums_ref, mine_out, sent_out,
    w_buf, acts_ref, out_ref, sems,
):
    copies = Copies(sems)
    arriving = [copies.start(w_ref.at[k], w_buf.at[k]) for k in range(9)]
    count = jnp.sum(first_ref[:, 2, 0:1])
    totals = jnp.sum(table_ref[...], axis=0)
    totals_ref[...] = totals
    center, inverse = consts_ref[0:1, :], consts_ref[1:2, :]
    plain, scaled = totals[0:1, :] / count, totals[1:2, :] / count
    scale = norm_ref[0:1, :] * inverse
    pad_edges(acts_ref, side)

    normed = (pre_ref[...] - center) * inverse
    grad = scale * (grad_ref[...] - valid_ref[...] * (plain + normed * scaled))
    out_ref[...] = grad.astype(bf16)
    half = out_ref.shape[1] // 2
    for place, out in ((which_ref[0], mine_out), (1 - which_ref[0], sent_out)):
        copies.out(out_ref.at[:, pl.ds(pl.multiple_of(place * half, half), half)], out)
    store_shifted(acts_ref, grad, side)
    total = None
    for tap in range(9):
        arriving[tap].wait()
        part = dot(window(acts_ref, 2 - tap // 3, 2 - tap % 3, side), w_buf[tap], (1, 1))
        total = part if total is None else total + part
    slope_rows(total, low_pre_ref, low_consts_ref, low_norm_ref, valid_ref, shifted_ref, sums_ref)
    copies.finish()


def reduce_back_kernel(
    which_ref, grad_ref, pre_ref, consts_ref, table_ref, norm_ref, valid_ref, first_ref, w_ref, res_ref, x_ref,
    totals_ref, images_out, sent_out, kept_out,
    low_buf, w_buf, res_buf, x_buf, part_buf, sems,
):
    copies = Copies(sems)
    parts = 4
    size = res_ref.shape[1] // parts
    arriving = []
    for k in range(parts):
        at = slice(k * size, (k + 1) * size)
        arriving.append(
            [
                copies.start(columns(x_ref, k, size), columns(x_buf, k, size)),
                copies.start(w_ref.at[at], w_buf.at[at]),
                copies.start(columns(res_ref, k, size), columns(res_buf, k, size)),
            ]
        )
    count = jnp.sum(first_ref[:, 2, 0:1])
    totals = jnp.sum(table_ref[...], axis=0)
    totals_ref[...] = totals
    center, inverse = consts_ref[0:1, :], consts_ref[1:2, :]
    plain, scaled = totals[0:1, :] / count, totals[1:2, :] / count
    scale = norm_ref[0:1, :] * inverse

    normed = (pre_ref[...] - center) * inverse
    grad = scale * (grad_ref[...] - valid_ref[...] * (plain + normed * scaled))
    low_buf[...] = grad.astype(bf16)
    for k in range(parts):
        at = slice(k * size, (k + 1) * size)
        arriving[k][0].wait()
        value = dot(x_buf[:, at], low_buf[...], (0, 0)).astype(bf16)
        peers = part_buf.shape[0] // parts
        dp = slice(k * peers, (k + 1) * peers)
        part_buf[dp] = value.reshape((peers,) + part_buf.shape[1:])
        copies.out(part_buf.at[dp, 1 - which_ref[0]], sent_out.at[dp])
        copies.out(part_buf.at[dp, which_ref[0]], kept_out.at[dp])
    for k in range(parts):
        at = slice(k * size, (k + 1) * size)
        arriving[k][1].wait()
        arriving[k][2].wait()
        res_buf[:, at] = res_buf[:, at] + valid_ref[...] * dot(low_buf[...], w_buf[at, :], (1, 1))
        copies.out(columns(res_buf, k, size), columns(images_out, k, size))
    copies.finish()


def trunk_weights_kernel(
    side, which_ref, act_ref, act_sib, right_ref, right_sib, acts_ref, acts_sib, grad_ref, grad_sib,
    sent_out, kept_out, acts_buf, grad_buf, out_buf, sems,
):
    copies = Copies(sems)
    size = right_ref.shape[1]
    blocks = grad_ref.shape[1] // size
    grads = [copies.start(ref, grad_buf.at[c]) for c, ref in enumerate((grad_ref, grad_sib))]
    acts = [copies.start(ref, acts_buf.at[c]) for c, ref in enumerate((acts_ref, acts_sib))]

    def store(place, value):
        out_buf[place] = value.astype(bf16).reshape(out_buf.shape[1:])
        for q in range(2):
            copies.out(out_buf.at[place, :, which_ref[q]], sent_out.at[q, place])
            copies.out(out_buf.at[place, :, which_ref[2 + q]], kept_out.at[q, place])

    for copy in grads:
        copy.wait()
    for b in range(blocks):
        at = slice(b * size, (b + 1) * size)
        store(b, dot(act_ref[...], grad_buf[0, :, at], (0, 0)) + dot(act_sib[...], grad_buf[1, :, at], (0, 0)))
    for copy in acts:
        copy.wait()
    for tap in range(9):
        tiles = [window(acts_buf.at[c], tap // 3, tap % 3, side) for c in range(2)]
        store(blocks + tap, dot(tiles[0], right_ref[...], (0, 0)) + dot(tiles[1], right_sib[...], (0, 0)))
    copies.finish()


def halve_kernel(axes, which_ref, *refs):
    n = len(axes)
    ins, outs, bufs, sems = refs[: 2 * n], refs[2 * n : 4 * n], refs[4 * n : 6 * n], refs[6 * n]
    copies = Copies(sems)
    arriving = [copies.start(ref, buf) for ref, buf in zip(ins, bufs)]
    first = 0
    for p, axis in enumerate(axes):
        kept_buf, came_buf = bufs[2 * p : 2 * p + 2]
        arriving[2 * p].wait()
        arriving[2 * p + 1].wait()
        kept_buf[...] = (kept_buf[...].astype(f32) + came_buf[...].astype(f32)).astype(bf16)
        count = kept_buf.shape[axis] // 2
        lead = (slice(None),) * axis
        for out in outs[2 * p : 2 * p + 2]:
            for i in range(count):
                target = lead + ((i,) if count > 1 else ())
                copies.out(kept_buf.at[lead + (which_ref[first],)], out.at[target] if target else out)
                first = first + 1
    copies.finish()


def task_kernel(half_ref, cot_ref, w_ref, out, cot_buf, w_buf, out_buf, sems):
    copies = Copies(sems)
    tasks, pixels = out.shape[:2]
    size = w_buf.shape[1]
    parts = w_ref.shape[1] // size
    rows = cot_buf.shape[1]
    start = pl.multiple_of(half_ref[0] * rows, rows)
    cots, arriving = [], []
    for t in range(tasks):
        cots.append(copies.start(cot_ref.at[pl.ds(start, rows), t], cot_buf.at[t]))
        for j in range(parts):
            arriving.append(copies.start(w_ref.at[t, j * size : (j + 1) * size], w_buf.at[t * parts + j]))
    for t in range(tasks):
        cots[t].wait()
        for j in range(parts):
            slot = t * parts + j
            arriving[slot].wait()
            cot = cot_buf[t].reshape(pixels, cot_buf.shape[3])
            out_buf[slot] = dot(cot, w_buf[slot], (1, 1)).astype(bf16)
            copies.out(out_buf.at[slot], out.at[t, :, j * size : (j + 1) * size])
    copies.finish()


def drop_kernel(mine_ref, other_ref, level_ref, out, mine_buf, other_buf, level_buf, out_buf, sems):
    copies = Copies(sems)
    tasks, pixels, _ = mine_ref.shape
    parts = 8
    size = pixels // parts
    arriving = []
    for k in range(parts):
        at = slice(k * size, (k + 1) * size)
        arriving.append(
            [
                copies.start(mine_ref.at[:, at], mine_buf.at[:, at]),
                copies.start(other_ref.at[:, at], other_buf.at[:, at]),
                copies.start(level_ref.at[at], level_buf.at[at]),
            ]
        )
    for k in range(parts):
        for copy in arriving[k]:
            copy.wait()

        rows = slice(k * size, (k + 1) * size)
        grads = [mine_buf[t, rows].astype(f32) + other_buf[t, rows].astype(f32) for t in range(tasks)]
        total, spread = None, None
        for grad in grads:
            squared = grad * grad + 1.0
            root = squared * lax.rsqrt(squared)
            spread = root if spread is None else spread + root
            total = grad if total is None else total + grad
        margin = (0.25 * steepness) * (total / spread) + (
            0.25 * steepness * (1.0 - 1.0 / levels)
            - level_buf[rows].astype(f32) * (0.5 * steepness / levels)
        )
        merged = total
        for grad in grads:
            merged = merged + grad * jnp.tanh(jnp.tanh(grad) * margin)
        out_buf[rows] = 0.5 * merged
        at = slice(k * size, (k + 1) * size)
        copies.out(out_buf.at[at], out.at[at])
    copies.finish()


def heads_kernel(first, which_ref, own_ref, sib_ref, w_ref, out, own_buf, sib_buf, w_buf, out_buf, sems):
    copies = Copies(sems)
    core = which_ref[0]
    tasks = w_buf.shape[0]
    lanes = w_ref.shape[2]
    size = lanes // 2
    rows = out.shape[0] // 2
    arriving = []
    features = []
    for t in range(tasks):
        for j in range(2):
            at = slice(j * size, (j + 1) * size)
            arriving.append(copies.start(w_ref.at[first + t, :, at], w_buf.at[t, :, at]))
            if not features:
                features = [copies.start(own_ref, own_buf), copies.start(sib_ref, sib_buf)]
    for t in range(tasks):
        for j in range(2):
            at = slice(j * size, (j + 1) * size)
            arriving[2 * t + j].wait()
            for s, (source, place) in enumerate(((own_buf, core), (sib_buf, 1 - core))):
                if t + j == 0:
                    features[s].wait()
                value = dot(source[...], w_buf[t, :, at], (1, 0)).astype(bf16)
                out_buf[t, s, :, :, at] = value.reshape(rows, out.shape[2], size)
                copies.out(
                    out_buf.at[t, s, :, :, at],
                    out.at[pl.ds(pl.multiple_of(place * rows, rows), rows), first + t, :, at],
                )
    copies.finish()


def weights_kernel(near, which_ref, first_ref, second_ref, cot_ref, *refs):
    added_ref, refs = (None, refs) if near else (refs[0], refs[1:])
    out, feat_buf, flip_buf, cot_buf, out_buf, sems = refs
    copies = Copies(sems)
    core = which_ref[0]
    tasks = out.shape[0]
    pixels, channels = feat_buf.shape[2:]
    pieces = channels // lane
    lanes = cot_buf.shape[4]
    rows = cot_buf.shape[2]
    features = []
    for j in range(2):
        for s, ref in enumerate((first_ref, second_ref)):
            if near:
                features.append(
                    [
                        copies.start(
                            ref.at[:, pl.ds(pl.multiple_of((4 * piece + which_ref[1 + j]) * lane, lane), lane)],
                            feat_buf.at[j, s, :, piece * lane : (piece + 1) * lane],
                        )
                        for piece in range(pieces)
                    ]
                )
            else:
                features.append([copies.start(ref.at[j], feat_buf.at[j, s])])
    start = 0 if near else which_ref[3] * (2 * rows)
    cots, more = [], []
    for t in range(tasks):
        cots.append(
            [
                copies.start(
                    cot_ref.at[pl.ds(pl.multiple_of(start + place * rows, rows), rows), t], cot_buf.at[t, s]
                )
                for s, place in enumerate((core, 1 - core))
            ]
        )
        if not near:
            more.append([copies.start(added_ref.at[t, j], out_buf.at[t, j]) for j in range(2)])
    for t in range(tasks):
        for j in range(2):
            if t == 0:
                for s in range(2):
                    for copy in features[2 * j + s]:
                        copy.wait()
                    flip_buf[j, :, s * pixels : (s + 1) * pixels] = feat_buf[j, s].T
            if j == 0:
                for copy in cots[t]:
                    copy.wait()
            value = dot(flip_buf[j], cot_buf[t].reshape(2 * pixels, lanes), (1, 0))
            if not near:
                more[t][j].wait()
                value = value + out_buf[t, j].astype(f32)
            out_buf[t, j] = value.astype(bf16)
            copies.out(out_buf.at[t, j], out.at[t, j])
    copies.finish()


def validity(bucket_shape, pixel_mask):
    row_index = lax.broadcasted_iota(jnp.int32, pixel_mask.shape, 1)
    col_index = lax.broadcasted_iota(jnp.int32, pixel_mask.shape, 2)
    inside = (row_index < bucket_shape[:, 0][:, None, None]) & (
        col_index < bucket_shape[:, 1][:, None, None]
    )
    return jnp.where(inside, pixel_mask, 0).astype(f32)


def from_everyone(rows):
    return lax.all_to_all(rows, everyone, 0, 0, tiled=True)


def swap_core(value):
    return lax.ppermute(value, "task", [(0, 1), (1, 0)])


def pick(value, axis, index):
    return lax.dynamic_index_in_dim(value, index, axis, keepdims=False)


def two(value, axis, first, second):
    return jnp.stack([pick(value, axis, first), pick(value, axis, second)], axis)


def on_device(
    images,
    bucket_shape,
    pixel_mask,
    thresholds,
    reduce_weight,
    spatial_weight,
    expand_weight,
    mid_gains,
    mid_biases,
    out_gain,
    out_bias,
    head_weights,
    head_cotangent,
):
    image_count = images.shape[0]
    side = images.shape[1]
    width = images.shape[3]
    middle = reduce_weight.shape[1]
    tasks = head_weights.shape[1]
    lanes = head_weights.shape[2]
    pixels = image_count * side * side
    peers = lax.axis_size("dp")
    devices = 2 * peers
    core = lax.axis_index("task")
    low = max(0, (lane * peers // width).bit_length() - 1)
    bit_x, bit_y = 1 << low, 2 << low
    position = lax.axis_index("dp")
    my_x, my_y = (position >> low) & 1, (position >> (low + 1)) & 1
    def pairing(bit_of, cross):
        pairs = []
        for i in range(peers):
            for c in range(2):
                if cross:
                    pairs.append((2 * i + c, 2 * (i ^ bit_of[1 - c]) + 1 - c))
                else:
                    pairs.append((2 * i + c, 2 * (i ^ bit_of[c]) + c))
        return pairs

    def swap_first(value):
        return lax.ppermute(value, everyone, pairing((bit_x, bit_y), False))

    def swap_second(value):
        return lax.ppermute(value, everyone, pairing((bit_y, bit_x), False))

    def swap_cross(value):
        return lax.ppermute(value, everyone, pairing((bit_x, bit_y), True))

    def by_core(zero, one):
        return jnp.where(core == 0, zero, one)

    twos = []
    for i in range(peers):
        for c, bit in enumerate((bit_y, bit_x)):
            if not i & bit:
                twos.append([2 * i + c, 2 * (i | bit) + c])
    rest_bits = [b for b in range(peers.bit_length() - 1) if not (1 << b) & (bit_x | bit_y)]

    def swap_rest(value, done):
        bit = rest_bits[done]
        return lax.ppermute(value, "dp", [(i, i ^ (1 << bit)) for i in range(peers)])

    def halved(pairs, after=()):
        outs, scratch, big, which, count = [], [], [], [], 0
        for kept, came, axis, indices in pairs:
            half = kept.shape[axis] // 2
            shape = kept.shape[:axis] + ((half,) if half > 1 else ()) + kept.shape[axis + 1 :]
            outs += [(shape, bf16, True)] * 2
            scratch += [pltpu.VMEM(kept.shape, bf16)] * 2
            big += [kept, came]
            which += list(indices)
            count += 2 + 2 * half
        return kernel_call(
            functools.partial(halve_kernel, tuple(axis for _, _, axis, _ in pairs)),
            outs,
            big=tuple(big),
            scalars=scalars(*which),
            scratch=scratch,
            copies=count,
            after=after,
            name="halve",
        )

    def rest_part(kept, came, dim, done):
        mine = (position >> rest_bits[done]) & 1
        return kept, came, dim + len(rest_bits) - 1 - done, (1 - mine, mine)

    fours, rests = {}, {}
    for i in range(peers):
        fours.setdefault(i & ~(bit_x | bit_y), []).append(i)
        rests.setdefault(i & (bit_x | bit_y), []).append(i)
    fours, rests = list(fours.values()), list(rests.values())

    def exchanged(value, members):
        came = lax.all_to_all(value, "dp", 0, 0, axis_index_groups=members, tiled=True)
        return jnp.sum(came.astype(f32), axis=0)

    inputs = images.reshape(pixels, width)
    valid = validity(bucket_shape, pixel_mask).reshape(pixels, 1)
    norms = jnp.stack([mid_gains, mid_biases], axis=1)
    gain_row, bias_row = out_gain.reshape(1, width), out_bias.reshape(1, width)
    levels_flat = thresholds.reshape(pixels, width)
    cot = head_cotangent.transpose(0, 1, 3, 2, 4).reshape(2 * image_count * side, tasks, side, lanes)
    rows_half = image_count * side
    weights = head_weights.transpose(1, 0, 2)
    half_lanes = lanes // 2
    block = 4 * lane
    blocks = width // block

    pairs = []
    for i in range(peers):
        for c, bit in enumerate((bit_x, bit_y)):
            if not i & bit:
                pairs.append([2 * i + c, 2 * (i ^ bit) + c])
    pair_cot = lax.all_gather(cot, everyone, axis=0, tiled=True, axis_index_groups=pairs)

    mid = (pixels, middle)
    whole = (pixels, width)
    pair = (2, middle)
    stat_two, stat_three = (devices, 2, middle), (devices, 3, middle)

    def scalars(*values):
        return jnp.stack(values).astype(jnp.int32)

    def task_half(half, after):
        return kernel_call(
            task_kernel,
            [((tasks, pixels, width), bf16, True)],
            big=(cot, weights),
            scalars=scalars(half),
            scratch=[
                pltpu.VMEM((tasks, rows_half, side, lanes), bf16),
                pltpu.VMEM((2 * tasks, width // 2, lanes), bf16),
                pltpu.VMEM((2 * tasks, pixels, width // 2), bf16),
            ],
            copies=5 * tasks,
            after=after,
            name="task_grad",
        )[0]

    pre_reduce, stats = kernel_call(
        reduce_kernel,
        [(mid, f32, False), (stat_three, f32, False)],
        small=(valid,),
        big=(inputs, reduce_weight),
        scratch=[pltpu.VMEM(whole, bf16), pltpu.VMEM(reduce_weight.shape, bf16)],
        copies=8,
        after=(norms,),
        name="reduce",
    )
    table_one = from_everyone(stats)
    task_mine = task_half(core, (stats,))

    padded = (3, image_count, (side + 2) * side, middle)
    pre_spatial, consts_one, stats, acts = kernel_call(
        functools.partial(spatial_kernel, side),
        [(mid, f32, False), (pair, f32, False), (stat_two, f32, False), (padded, bf16, True)],
        small=(pre_reduce, table_one, norms[0], valid),
        big=(spatial_weight,),
        scratch=[pltpu.VMEM(spatial_weight.shape, bf16), pltpu.VMEM(padded, bf16)],
        copies=10,
        after=(task_mine,),
        name="spatial",
    )
    table_two = from_everyone(stats)
    task_sent = task_half(1 - core, (stats,))
    task_other = swap_core(held_until((table_two,), task_sent)[0])

    act_spatial, consts_two, stats, pre_expand = kernel_call(
        expand_kernel,
        [(mid, bf16, False), (pair, f32, False), ((devices, 2, width), f32, False), (whole, f32, True)],
        small=(pre_spatial, table_two, table_one, norms[1], valid),
        big=(expand_weight,),
        scratch=[pltpu.VMEM(expand_weight.shape, bf16), pltpu.VMEM(whole, f32)],
        copies=8,
        after=(task_sent,),
        name="expand",
    )
    table_three = from_everyone(stats)
    (merged,) = kernel_call(
        drop_kernel,
        [(whole, f32, True)],
        big=(task_mine, task_other, levels_flat),
        scratch=[
            pltpu.VMEM((tasks,) + whole, bf16),
            pltpu.VMEM((tasks,) + whole, bf16),
            pltpu.VMEM(whole, jnp.int32),
            pltpu.VMEM(whole, f32),
        ],
        copies=32,
        after=(stats,),
        name="graddrop",
    )


    pair_blocks = (2, pixels, width // 4)
    x_send, y_send = 2 * (1 - my_x), 1 - my_y
    consts_three, sums, features, same, cross, grad_residual = kernel_call(
        residual_kernel,
        [
            ((2, width), f32, False),
            ((devices, 2, width), f32, False),
            (whole, bf16, True),
            (pair_blocks, bf16, True),
            (pair_blocks, bf16, True),
            (whole, f32, True),
        ],
        scalars=scalars(
            by_core(x_send, y_send),
            by_core(x_send + 1, y_send + 2),
            by_core(y_send, x_send),
            by_core(y_send + 2, x_send + 1),
        ),
        small=(table_three, table_one, gain_row, bias_row, valid),
        big=(pre_expand, inputs, merged),
        scratch=[
            pltpu.VMEM(whole, f32),
            pltpu.VMEM(whole, bf16),
            pltpu.VMEM(whole, f32),
            pltpu.VMEM(whole, bf16),
            pltpu.VMEM((4, pixels, width // 4), bf16),
            pltpu.VMEM(whole, f32),
        ],
        copies=24,
        name="residual",
    )
    table_four = from_everyone(sums)
    sibling = swap_core(features)
    far = swap_first(same)
    far_cross = swap_cross(cross)
    acts, act_spatial = held_until((features,), acts, act_spatial)
    acts_sib, act_spatial_sib = swap_core(acts), swap_core(act_spatial)

    def heads(first, count, after, fills):
        return kernel_call(
            functools.partial(heads_kernel, first),
            [(cot.shape, bf16, True)],
            big=(features, sibling, weights),
            scalars=scalars(core),
            scratch=[
                pltpu.VMEM(whole, bf16),
                pltpu.VMEM(whole, bf16),
                pltpu.VMEM((count, width, lanes), bf16),
                pltpu.VMEM((count, 2, rows_half, side, lanes), bf16),
            ],
            copies=2 + 6 * count,
            after=after,
            fills=fills,
            name="heads",
        )[0]


    part_shape = (tasks, 2, width // 4, lanes)

    def weight_part(near, first, second, cots, added, after):
        return kernel_call(
            functools.partial(weights_kernel, near),
            [(part_shape, bf16, True)],
            big=(first, second, cots) + added,
            scalars=scalars(
                core,
                by_core(my_x, 2 * my_y),
                by_core(my_x + 2, 2 * my_y + 1),
                1 - by_core(my_x, my_y),
            ),
            scratch=[
                pltpu.VMEM((2, 2, pixels, width // 4), bf16),
                pltpu.VMEM((2, width // 4, 2 * pixels), bf16),
                pltpu.VMEM((tasks, 2, rows_half, side, lanes), bf16),
                pltpu.VMEM(part_shape, bf16),
            ],
            copies=4 * blocks + 10 * tasks,
            after=after,
            name="heads_grad",
        )[0]

    near_part = weight_part(True, features, sibling, cot, (), (sums,))
    index = by_core(my_y, my_x)

    heads_part = weight_part(False, far, far_cross, pair_cot, (near_part,), (near_part,))
    (heads_part,) = held_until((table_four,), heads_part)
    heads_half = lax.psum_scatter(
        heads_part.reshape(tasks, width // 2, lanes),
        everyone,
        scatter_dimension=1,
        axis_index_groups=twos,
        tiled=True,
    )

    expand_half, spatial_half = (pixels, width // 2), (pixels, middle // 2)
    out_totals, shifted_two, sums, expand_mine, expand_sent = kernel_call(
        expand_back_kernel,
        [
            ((2, width), f32, False),
            (mid, f32, False),
            (stat_two, f32, False),
            (expand_half, bf16, True),
            (expand_half, bf16, True),
        ],
        scalars=scalars(core),
        small=(consts_three, table_four, gain_row, valid, table_one, pre_spatial, consts_two, norms[1]),
        big=(grad_residual, pre_expand, expand_weight),
        scratch=[
            pltpu.VMEM(whole, f32),
            pltpu.VMEM(whole, f32),
            pltpu.VMEM(expand_weight.shape, bf16),
            pltpu.VMEM(whole, bf16),
        ],
        copies=14,
        after=(heads_part,),
        name="expand_back",
    )
    table_five = from_everyone(sums)
    expand_sib = swap_core(expand_sent)
    totals_two, shifted_one, sums, spatial_mine, spatial_sent = kernel_call(
        functools.partial(spatial_back_kernel, side),
        [
            (pair, f32, False),
            (mid, f32, False),
            (stat_two, f32, False),
            (spatial_half, bf16, True),
            (spatial_half, bf16, True),
        ],
        scalars=scalars(core),
        small=(
            shifted_two, pre_spatial, consts_two, table_five, norms[1], valid, table_one,
            pre_reduce, consts_one, norms[0],
        ),
        big=(spatial_weight,),
        scratch=[
            pltpu.VMEM(spatial_weight.shape, bf16),
            pltpu.VMEM(padded, bf16),
            pltpu.VMEM(mid, bf16),
        ],
        copies=11,
        name="spatial_back",
    )
    table_six = from_everyone(sums)
    spatial_sib = swap_core(spatial_sent)
    x_out, y_out, x_in, y_in = 1 - my_x, 2 * (1 - my_y), my_x, 2 * my_y
    pair_parts = (
        by_core(x_out, y_out),
        by_core(x_out + 2, y_out + 1),
        by_core(x_in, y_in),
        by_core(x_in + 2, y_in + 1),
    )
    high, rows_of_pair = peers >> (low + 2), (1 << low) * (middle // peers)
    early_shape = (2, blocks + 9, high, rows_of_pair, middle // 2)
    early_sent, early_kept = kernel_call(
        functools.partial(trunk_weights_kernel, side),
        [(early_shape, bf16, True), (early_shape, bf16, True)],
        scalars=scalars(*pair_parts),
        small=(act_spatial, act_spatial_sib, spatial_mine, spatial_sib),
        big=(acts, acts_sib, expand_mine, expand_sib),
        scratch=[
            pltpu.VMEM((2,) + padded, bf16),
            pltpu.VMEM((2,) + expand_half, bf16),
            pltpu.VMEM((blocks + 9, high, 4, rows_of_pair, middle // 2), bf16),
        ],
        copies=4 + 4 * (blocks + 9),
        after=(sums,),
        name="trunk_weights",
    )
    (early_sent,) = held_until((table_six,), early_sent)
    early_came = swap_first(early_sent)
    dp_rows = (peers, width // devices, middle)
    totals_one, images_grad, reduce_sent, reduce_kept = kernel_call(
        reduce_back_kernel,
        [(pair, f32, False), (whole, f32, True), (dp_rows, bf16, True), (dp_rows, bf16, True)],
        scalars=scalars(core),
        small=(shifted_one, pre_reduce, consts_one, table_six, norms[0], valid, table_one),
        big=(reduce_weight, grad_residual, inputs),
        scratch=[
            pltpu.VMEM(mid, bf16),
            pltpu.VMEM(reduce_weight.shape, bf16),
            pltpu.VMEM(whole, f32),
            pltpu.VMEM(whole, bf16),
            pltpu.VMEM((peers, 2, width // devices, middle), bf16),
        ],
        copies=24,
        after=(early_kept,),
        name="reduce_back",
    )
    reduce_came = swap_core(reduce_sent)
    (heads_half,) = held_until((reduce_kept,), heads_half)
    heads_grad = lax.psum_scatter(
        heads_half, "dp", scatter_dimension=1, axis_index_groups=rests, tiled=True
    )
    heads_grad = heads_grad.astype(f32)
    quarters = (high, 4, (1 << low) * dp_rows[1], middle)
    reduce_sent, reduce_kept = halved(
        [(reduce_kept.reshape(quarters), reduce_came.reshape(quarters), 1, pair_parts)]
    )
    reduce_came = swap_first(reduce_sent)
    head_values = heads(0, 2, (reduce_kept,), False)
    early_sent, early_kept, reduce_sent, reduce_kept = halved(
        [
            (early_kept, early_came, 0, (1 - index, index)),
            (reduce_kept, reduce_came, 1, (1 - index, index)),
        ],
        (head_values,),
    )
    early_came, reduce_came = swap_second(early_sent), swap_second(reduce_sent)
    head_values = heads(2, tasks - 2, (head_values, reduce_kept), True)
    head_output = head_values.reshape(2 * image_count, side, tasks, side, lanes).transpose(0, 1, 3, 2, 4)
    early_open = (blocks + 9,) + (2,) * len(rest_bits) + (-1, middle // 2)
    reduce_open = (2,) * len(rest_bits) + (-1, middle)
    early_kept, early_came = early_kept.reshape(early_open), early_came.reshape(early_open)
    reduce_kept, reduce_came = reduce_kept.reshape(reduce_open), reduce_came.reshape(reduce_open)
    for done in range(len(rest_bits)):
        early_sent, early_kept, reduce_sent, reduce_kept = halved(
            [rest_part(early_kept, early_came, 1, done), rest_part(reduce_kept, reduce_came, 0, done)],
            (heads_grad if done else head_values,),
        )
        early_came, reduce_came = swap_rest(early_sent, done), swap_rest(reduce_sent, done)
    heads_grad = heads_grad.transpose(1, 0, 2)
    early = early_kept.astype(f32) + early_came.astype(f32)
    reduce_grad = reduce_kept.astype(f32) + reduce_came.astype(f32)

    own_rows = early.reshape(early.shape[0], 2, -1, early.shape[2])
    came_rows = swap_core(pick(own_rows, 1, 1 - core))
    own_rows = pick(own_rows, 1, core)
    halves = jnp.stack(
        [jnp.where(core == 0, own_rows, came_rows), jnp.where(core == 0, came_rows, own_rows)]
    ).astype(f32)
    expand_grad = halves[:, :blocks].transpose(2, 0, 1, 3).reshape(middle // devices, width)
    spatial_grad = halves[:, blocks:].transpose(1, 2, 0, 3).reshape(9, middle // devices, middle)
    gains_grad = jnp.stack([totals_one[1], totals_two[1]], axis=0)
    biases_grad = jnp.stack([totals_one[0], totals_two[0]], axis=0)
    return (
        head_output,
        images_grad.reshape(images.shape),
        reduce_grad,
        spatial_grad,
        expand_grad,
        gains_grad,
        biases_grad,
        out_totals[1],
        out_totals[0],
        heads_grad,
    )


def solution(mesh):
    placed = (
        P(("dp", "task"), None, None, None),
        P(("dp", "task"), None),
        P(("dp", "task"), None, None),
        P(("dp", "task"), None, None, None),
        P(),
        P(),
        P(),
        P(),
        P(),
        P(),
        P(),
        P(None, None, "task"),
        P("dp", None, None, None, "task"),
    )
    return jax.shard_map(
        on_device,
        mesh=mesh,
        in_specs=placed,
        out_specs=(
            P("dp", None, None, None, "task"),
            P(("dp", "task"), None, None, None),
            P(("dp", "task"), None),
            P(None, ("dp", "task"), None),
            P(("dp", "task"), None),
            P(),
            P(),
            P(),
            P(),
            P("dp", None, "task"),
        ),
        check_vma=False,
    )
```

```python
import functools

import jax
import jax.numpy as jnp
from jax import lax
from jax.experimental import pallas as pl
from jax.experimental.pallas import tpu as pltpu
from jax.sharding import PartitionSpec as P

epsilon = 1e-05
steepness = 6.0
levels = 4096.0
everyone = ("dp", "task")
f32 = jnp.float32
bf16 = jnp.bfloat16
lane = 128
MIB = 1 << 20


def dot(left, right, contract):
    return lax.dot_general(
        left, right, ((contract[0:1], contract[1:2]), ((), ())), preferred_element_type=f32
    )


def kernel_call(body, outs, small=(), big=(), scalars=None, scratch=(), copies=0, after=(), fills=False, name=None):
    skipped = len(after)

    def ordered(*refs):
        body(*refs[skipped:])

    big = [pltpu.with_memory_space_constraint(array, pltpu.HBM) for array in big]
    there = pl.BlockSpec(memory_space=pl.ANY)
    here = pl.BlockSpec(memory_space=pltpu.VMEM)
    given = [] if scalars is None else [scalars]
    return pl.pallas_call(
        ordered,
        in_specs=[there] * skipped
        + [pl.BlockSpec(memory_space=pltpu.SMEM)] * len(given)
        + [here] * len(small)
        + [there] * len(big),
        out_specs=[there if streamed else here for _, _, streamed in outs],
        out_shape=[
            pltpu.HBM(shape, dtype) if streamed else jax.ShapeDtypeStruct(shape, dtype)
            for shape, dtype, streamed in outs
        ],
        scratch_shapes=list(scratch) + ([pltpu.SemaphoreType.DMA((copies,))] if copies else []),
        input_output_aliases={0: 0} if fills else {},
        compiler_params=pltpu.CompilerParams(vmem_limit_bytes=48 * MIB),
        name=name,
    )(*after, *given, *small, *big)


def held_until(after, *values):
    def body(*refs):
        pass

    there = pl.BlockSpec(memory_space=pl.ANY)
    return pl.pallas_call(
        body,
        in_specs=[there] * (len(values) + len(after)),
        out_specs=[there] * len(values),
        out_shape=[jax.ShapeDtypeStruct(v.shape, v.dtype) for v in values],
        input_output_aliases={i: i for i in range(len(values))},
        name="held",
    )(*values, *after)


class Copies:
    def __init__(self, sems):
        self.sems = sems
        self.used = 0
        self.open = []

    def start(self, source, target):
        copy = pltpu.make_async_copy(source, target, self.sems.at[self.used])
        self.used += 1
        copy.start()
        return copy

    def out(self, source, target):
        self.open.append(self.start(source, target))

    def finish(self):
        for copy in self.open:
            copy.wait()


def columns(ref, index, size):
    return ref.at[:, index * size : (index + 1) * size]


def sigmoid(value):
    return 0.5 + 0.5 * jnp.tanh(0.5 * value)


def combined(table, counts):
    counts = counts[:, 0:1]
    total = jnp.sum(counts)
    center = jnp.sum(table[:, 0, :], axis=0, keepdims=True) / total
    shift = table[:, 0, :] / jnp.maximum(counts, 1.0) - center
    variance = (
        jnp.sum(table[:, 1, :] + counts * shift * shift, axis=0, keepdims=True) / total
    )
    return center, lax.rsqrt(variance + epsilon)


def store_rows(stats_ref, rows, at=slice(None)):
    table = jnp.concatenate(rows, axis=0)
    stats_ref[:, :, at] = jnp.broadcast_to(table[None], (stats_ref.shape[0],) + table.shape)


def store_moments(stats_ref, values_ref, valid_ref, at=slice(None)):
    valid, values = valid_ref[...], values_ref[...]
    count = jnp.sum(valid)
    first = jnp.sum(values * valid, axis=0, keepdims=True)
    deviation = (values - first / jnp.maximum(count, 1.0)) * valid
    rows = [first, jnp.sum(deviation * deviation, axis=0, keepdims=True)]
    if stats_ref.shape[1] > 2:
        rows.append(jnp.broadcast_to(count, first.shape))
    store_rows(stats_ref, rows, at)


def store_sums(stats_ref, grad, normed, at=slice(None)):
    rows = [jnp.sum(grad, axis=0, keepdims=True), jnp.sum(grad * normed, axis=0, keepdims=True)]
    store_rows(stats_ref, rows, at)


def reduce_kernel(valid_ref, x_ref, w_ref, out_ref, stats_ref, x_buf, w_buf, sems):
    copies = Copies(sems)
    parts = 4
    size = x_ref.shape[1] // parts
    arriving = []
    for k in range(parts):
        arriving.append(
            (
                copies.start(columns(x_ref, k, size), columns(x_buf, k, size)),
                copies.start(w_ref.at[k * size : (k + 1) * size], w_buf.at[k * size : (k + 1) * size]),
            )
        )
    total = None
    for k, pair in enumerate(arriving):
        for copy in pair:
            copy.wait()
        part = dot(x_buf[:, k * size : (k + 1) * size], w_buf[k * size : (k + 1) * size, :], (1, 0))
        total = part if total is None else total + part
    out_ref[...] = total * valid_ref[...]
    store_moments(stats_ref, out_ref, valid_ref)


def pad_edges(acts_ref, side):
    images = acts_ref.shape[1]
    zeros = jnp.zeros((side, acts_ref.shape[3]), bf16)
    for shift in range(3):
        for image in range(images):
            acts_ref[shift, image, 0:side, :] = zeros
            acts_ref[shift, image, (side + 1) * side : (side + 2) * side, :] = zeros


def store_shifted(acts_ref, values, side):
    pixels = values.shape[0]
    column = lax.broadcasted_iota(jnp.int32, (pixels, 1), 0) % side
    before = jnp.where(column == 0, 0.0, pltpu.roll(values, 1, 0))
    after = jnp.where(column == side - 1, 0.0, pltpu.roll(values, pixels - 1, 0))
    for shift, moved in enumerate((before, values, after)):
        for image in range(acts_ref.shape[1]):
            rows = slice(image * side * side, (image + 1) * side * side)
            acts_ref[shift, image, side : side + side * side, :] = moved[rows].astype(bf16)


def window(acts_ref, row_shift, col_shift, side):
    images = acts_ref.shape[1]
    tile = acts_ref[col_shift, :, row_shift * side : row_shift * side + side * side, :]
    return tile.reshape(images * side * side, acts_ref.shape[3])


def spatial_kernel(
    side, pre_ref, table_ref, norm_ref, valid_ref, w_ref, out_ref, consts_ref, stats_ref, acts_out, w_buf, acts_ref, sems
):
    copies = Copies(sems)
    arriving = [copies.start(w_ref.at[k], w_buf.at[k]) for k in range(9)]
    center, inverse = combined(table_ref, table_ref[:, 2, :])
    consts_ref[0:1, :] = center
    consts_ref[1:2, :] = inverse
    gain, bias = norm_ref[0:1, :], norm_ref[1:2, :]
    pad_edges(acts_ref, side)

    shifted = gain * ((pre_ref[...] - center) * inverse) + bias
    store_shifted(acts_ref, valid_ref[...] * shifted * sigmoid(shifted), side)
    copies.out(acts_ref, acts_out)
    total = None
    for tap in range(9):
        arriving[tap].wait()
        part = dot(window(acts_ref, tap // 3, tap % 3, side), w_buf[tap], (1, 0))
        total = part if total is None else total + part
    out_ref[...] = total
    store_moments(stats_ref, out_ref, valid_ref)
    copies.finish()


def expand_kernel(
    pre_ref, table_ref, first_ref, norm_ref, valid_ref, w_ref, act_ref, consts_ref, stats_out, out,
    w_buf, out_buf, stats_ref, sems,
):
    copies = Copies(sems)
    parts = 4
    size = w_ref.shape[1] // parts
    arriving = [copies.start(columns(w_ref, k, size), columns(w_buf, k, size)) for k in range(parts)]
    center, inverse = combined(table_ref, first_ref[:, 2, :])
    consts_ref[0:1, :] = center
    consts_ref[1:2, :] = inverse
    gain, bias = norm_ref[0:1, :], norm_ref[1:2, :]

    shifted = gain * ((pre_ref[...] - center) * inverse) + bias
    act_ref[...] = (valid_ref[...] * shifted * sigmoid(shifted)).astype(bf16)
    for k in range(parts):
        at = slice(k * size, (k + 1) * size)
        arriving[k].wait()
        out_buf[:, at] = dot(act_ref[...], w_buf[:, at], (1, 0))
        copies.out(columns(out_buf, k, size), columns(out, k, size))
        store_moments(stats_ref, columns(out_buf, k, size), valid_ref, at)
        copies.out(stats_ref.at[:, :, at], stats_out.at[:, :, at])
    copies.finish()


def residual_kernel(
    which_ref, table_ref, first_ref, gain_ref, bias_ref, valid_ref, pre_ref, x_ref, merged_ref,
    consts_ref, sums_out, feat_out, same_out, cross_out, grad_out,
    pre_buf, x_buf, merged_buf, feat_buf, block_buf, grad_buf, sums_ref, sems,
):
    copies = Copies(sems)
    parts = 4
    size = pre_ref.shape[1] // parts
    arriving = []
    for k in range(parts):
        arriving.append(
            [
                copies.start(columns(ref, k, size), columns(buf, k, size))
                for ref, buf in ((pre_ref, pre_buf), (x_ref, x_buf), (merged_ref, merged_buf))
            ]
        )
    for k in range(parts):
        at = slice(k * size, (k + 1) * size)
        center, inverse = combined(table_ref[:, :, at], first_ref[:, 2, :])
        consts_ref[0:1, at] = center
        consts_ref[1:2, at] = inverse
        gain, bias = gain_ref[:, at], bias_ref[:, at]
        for copy in arriving[k]:
            copy.wait()

        valid = valid_ref[...]
        normed = (pre_buf[:, at] - center) * inverse
        value = x_buf[:, at].astype(f32) + gain * normed + bias
        sigma = sigmoid(value)
        features = (valid * (value * sigma)).astype(bf16)
        feat_buf[:, at] = features
        for piece in range(4):
            block_buf[2 * (piece % 2) + piece // 2, :, k * lane : (k + 1) * lane] = features[
                :, piece * lane : (piece + 1) * lane
            ]
        grad = merged_buf[:, at] * valid * (sigma * (1.0 + value * (1.0 - sigma)))
        grad_buf[:, at] = grad
        store_sums(sums_ref, grad, normed, at)
        copies.out(sums_ref.at[:, :, at], sums_out.at[:, :, at])
        copies.out(columns(grad_buf, k, size), columns(grad_out, k, size))
        copies.out(columns(feat_buf, k, size), columns(feat_out, k, size))
    for j in range(2):
        copies.out(block_buf.at[which_ref[j]], same_out.at[j])
        copies.out(block_buf.at[which_ref[2 + j]], cross_out.at[j])
    copies.finish()


def slope_rows(grad, pre_ref, consts_ref, norm_ref, valid_ref, out_ref, sums_ref):
    center, inverse = consts_ref[0:1, :], consts_ref[1:2, :]
    gain, bias = norm_ref[0:1, :], norm_ref[1:2, :]
    normed = (pre_ref[...] - center) * inverse
    value = gain * normed + bias
    sigma = sigmoid(value)
    grad = grad * valid_ref[...] * (sigma * (1.0 + value * (1.0 - sigma)))
    out_ref[...] = grad
    store_sums(sums_ref, grad, normed)


def expand_back_kernel(
    which_ref, consts_ref, table_ref, gain_ref, valid_ref, first_ref, mid_pre_ref, mid_consts_ref, mid_norm_ref,
    grad_ref, pre_ref, w_ref,
    totals_ref, shifted_ref, sums_ref, mine_out, sent_out,
    grad_buf, pre_buf, w_buf, out_buf, sems,
):
    copies = Copies(sems)
    parts = 4
    size = pre_ref.shape[1] // parts
    arriving = []
    for k in range(parts):
        arriving.append(
            [
                copies.start(columns(ref, k, size), columns(buf, k, size))
                for ref, buf in ((grad_ref, grad_buf), (pre_ref, pre_buf), (w_ref, w_buf))
            ]
        )
    count = jnp.sum(first_ref[:, 2, 0:1])
    total = None
    for k in range(parts):
        at = slice(k * size, (k + 1) * size)
        totals = jnp.sum(table_ref[:, :, at], axis=0)
        totals_ref[:, at] = totals
        center, inverse = consts_ref[0:1, at], consts_ref[1:2, at]
        plain, scaled = totals[0:1, :] / count, totals[1:2, :] / count
        scale = gain_ref[:, at] * inverse
        for copy in arriving[k]:
            copy.wait()

        normed = (pre_buf[:, at] - center) * inverse
        grad = scale * (grad_buf[:, at] - valid_ref[...] * (plain + normed * scaled))
        out_buf[:, at] = grad.astype(bf16)
        part = dot(out_buf[:, at], w_buf[:, at], (1, 1))
        total = part if total is None else total + part
    half = out_buf.shape[1] // 2
    for place, out in ((which_ref[0], mine_out), (1 - which_ref[0], sent_out)):
        copies.out(out_buf.at[:, pl.ds(pl.multiple_of(place * half, half), half)], out)
    slope_rows(total, mid_pre_ref, mid_consts_ref, mid_norm_ref, valid_ref, shifted_ref, sums_ref)
    copies.finish()


def spatial_back_kernel(
    side, which_ref, grad_ref, pre_ref, consts_ref, table_ref, norm_ref, valid_ref, first_ref,
    low_pre_ref, low_consts_ref, low_norm_ref, w_ref,
    totals_ref, shifted_ref, sums_ref, mine_out, sent_out,
    w_buf, acts_ref, out_ref, sems,
):
    copies = Copies(sems)
    arriving = [copies.start(w_ref.at[k], w_buf.at[k]) for k in range(9)]
    count = jnp.sum(first_ref[:, 2, 0:1])
    totals = jnp.sum(table_ref[...], axis=0)
    totals_ref[...] = totals
    center, inverse = consts_ref[0:1, :], consts_ref[1:2, :]
    plain, scaled = totals[0:1, :] / count, totals[1:2, :] / count
    scale = norm_ref[0:1, :] * inverse
    pad_edges(acts_ref, side)

    normed = (pre_ref[...] - center) * inverse
    grad = scale * (grad_ref[...] - valid_ref[...] * (plain + normed * scaled))
    out_ref[...] = grad.astype(bf16)
    half = out_ref.shape[1] // 2
    for place, out in ((which_ref[0], mine_out), (1 - which_ref[0], sent_out)):
        copies.out(out_ref.at[:, pl.ds(pl.multiple_of(place * half, half), half)], out)
    store_shifted(acts_ref, grad, side)
    total = None
    for tap in range(9):
        arriving[tap].wait()
        part = dot(window(acts_ref, 2 - tap // 3, 2 - tap % 3, side), w_buf[tap], (1, 1))
        total = part if total is None else total + part
    slope_rows(total, low_pre_ref, low_consts_ref, low_norm_ref, valid_ref, shifted_ref, sums_ref)
    copies.finish()


def reduce_back_kernel(
    which_ref, grad_ref, pre_ref, consts_ref, table_ref, norm_ref, valid_ref, first_ref, w_ref, res_ref, x_ref,
    totals_ref, images_out, sent_out, kept_out,
    low_buf, w_buf, res_buf, x_buf, part_buf, sems,
):
    copies = Copies(sems)
    parts = 4
    size = res_ref.shape[1] // parts
    arriving = []
    for k in range(parts):
        at = slice(k * size, (k + 1) * size)
        arriving.append(
            [
                copies.start(columns(x_ref, k, size), columns(x_buf, k, size)),
                copies.start(w_ref.at[at], w_buf.at[at]),
                copies.start(columns(res_ref, k, size), columns(res_buf, k, size)),
            ]
        )
    count = jnp.sum(first_ref[:, 2, 0:1])
    totals = jnp.sum(table_ref[...], axis=0)
    totals_ref[...] = totals
    center, inverse = consts_ref[0:1, :], consts_ref[1:2, :]
    plain, scaled = totals[0:1, :] / count, totals[1:2, :] / count
    scale = norm_ref[0:1, :] * inverse

    normed = (pre_ref[...] - center) * inverse
    grad = scale * (grad_ref[...] - valid_ref[...] * (plain + normed * scaled))
    low_buf[...] = grad.astype(bf16)
    for k in range(parts):
        at = slice(k * size, (k + 1) * size)
        arriving[k][0].wait()
        value = dot(x_buf[:, at], low_buf[...], (0, 0)).astype(bf16)
        peers = part_buf.shape[0] // parts
        dp = slice(k * peers, (k + 1) * peers)
        part_buf[dp] = value.reshape((peers,) + part_buf.shape[1:])
        copies.out(part_buf.at[dp, 1 - which_ref[0]], sent_out.at[dp])
        copies.out(part_buf.at[dp, which_ref[0]], kept_out.at[dp])
    for k in range(parts):
        at = slice(k * size, (k + 1) * size)
        arriving[k][1].wait()
        arriving[k][2].wait()
        res_buf[:, at] = res_buf[:, at] + valid_ref[...] * dot(low_buf[...], w_buf[at, :], (1, 1))
        copies.out(columns(res_buf, k, size), columns(images_out, k, size))
    copies.finish()


def trunk_weights_kernel(
    side, which_ref, act_ref, act_sib, right_ref, right_sib, acts_ref, acts_sib, grad_ref, grad_sib,
    sent_out, kept_out, acts_buf, grad_buf, out_buf, sems,
):
    copies = Copies(sems)
    size = right_ref.shape[1]
    blocks = grad_ref.shape[1] // size
    grads = [copies.start(ref, grad_buf.at[c]) for c, ref in enumerate((grad_ref, grad_sib))]
    acts = [copies.start(ref, acts_buf.at[c]) for c, ref in enumerate((acts_ref, acts_sib))]

    def store(place, value):
        out_buf[place] = value.astype(bf16).reshape(out_buf.shape[1:])
        for q in range(2):
            copies.out(out_buf.at[place, :, which_ref[q]], sent_out.at[q, place])
            copies.out(out_buf.at[place, :, which_ref[2 + q]], kept_out.at[q, place])

    for copy in grads:
        copy.wait()
    for b in range(blocks):
        at = slice(b * size, (b + 1) * size)
        store(b, dot(act_ref[...], grad_buf[0, :, at], (0, 0)) + dot(act_sib[...], grad_buf[1, :, at], (0, 0)))
    for copy in acts:
        copy.wait()
    for tap in range(9):
        tiles = [window(acts_buf.at[c], tap // 3, tap % 3, side) for c in range(2)]
        store(blocks + tap, dot(tiles[0], right_ref[...], (0, 0)) + dot(tiles[1], right_sib[...], (0, 0)))
    copies.finish()


def halve_kernel(axes, which_ref, *refs):
    n = len(axes)
    ins, outs, bufs, sems = refs[: 2 * n], refs[2 * n : 4 * n], refs[4 * n : 6 * n], refs[6 * n]
    copies = Copies(sems)
    arriving = [copies.start(ref, buf) for ref, buf in zip(ins, bufs)]
    first = 0
    for p, axis in enumerate(axes):
        kept_buf, came_buf = bufs[2 * p : 2 * p + 2]
        arriving[2 * p].wait()
        arriving[2 * p + 1].wait()
        kept_buf[...] = (kept_buf[...].astype(f32) + came_buf[...].astype(f32)).astype(bf16)
        count = kept_buf.shape[axis] // 2
        lead = (slice(None),) * axis
        for out in outs[2 * p : 2 * p + 2]:
            for i in range(count):
                target = lead + ((i,) if count > 1 else ())
                copies.out(kept_buf.at[lead + (which_ref[first],)], out.at[target] if target else out)
                first = first + 1
    copies.finish()


def task_kernel(half_ref, cot_ref, w_ref, out, cot_buf, w_buf, out_buf, sems):
    copies = Copies(sems)
    tasks, pixels = out.shape[:2]
    size = w_buf.shape[1]
    parts = w_ref.shape[1] // size
    rows = cot_buf.shape[1]
    start = pl.multiple_of(half_ref[0] * rows, rows)
    cots, arriving = [], []
    for t in range(tasks):
        cots.append(copies.start(cot_ref.at[pl.ds(start, rows), t], cot_buf.at[t]))
        for j in range(parts):
            arriving.append(copies.start(w_ref.at[t, j * size : (j + 1) * size], w_buf.at[t * parts + j]))
    for t in range(tasks):
        cots[t].wait()
        for j in range(parts):
            slot = t * parts + j
            arriving[slot].wait()
            cot = cot_buf[t].reshape(pixels, cot_buf.shape[3])
            out_buf[slot] = dot(cot, w_buf[slot], (1, 1)).astype(bf16)
            copies.out(out_buf.at[slot], out.at[t, :, j * size : (j + 1) * size])
    copies.finish()


def drop_kernel(mine_ref, other_ref, level_ref, out, mine_buf, other_buf, level_buf, out_buf, sems):
    copies = Copies(sems)
    tasks, pixels, _ = mine_ref.shape
    parts = 8
    size = pixels // parts
    arriving = []
    for k in range(parts):
        at = slice(k * size, (k + 1) * size)
        arriving.append(
            [
                copies.start(mine_ref.at[:, at], mine_buf.at[:, at]),
                copies.start(other_ref.at[:, at], other_buf.at[:, at]),
                copies.start(level_ref.at[at], level_buf.at[at]),
            ]
        )
    for k in range(parts):
        for copy in arriving[k]:
            copy.wait()

        rows = slice(k * size, (k + 1) * size)
        grads = [mine_buf[t, rows].astype(f32) + other_buf[t, rows].astype(f32) for t in range(tasks)]
        total, spread = None, None
        for grad in grads:
            squared = grad * grad + 1.0
            root = squared * lax.rsqrt(squared)
            spread = root if spread is None else spread + root
            total = grad if total is None else total + grad
        margin = (0.25 * steepness) * (total / spread) + (
            0.25 * steepness * (1.0 - 1.0 / levels)
            - level_buf[rows].astype(f32) * (0.5 * steepness / levels)
        )
        merged = total
        for grad in grads:
            merged = merged + grad * jnp.tanh(jnp.tanh(grad) * margin)
        out_buf[rows] = 0.5 * merged
        at = slice(k * size, (k + 1) * size)
        copies.out(out_buf.at[at], out.at[at])
    copies.finish()


def heads_kernel(first, which_ref, own_ref, sib_ref, w_ref, out, own_buf, sib_buf, w_buf, out_buf, sems):
    copies = Copies(sems)
    core = which_ref[0]
    tasks = w_buf.shape[0]
    lanes = w_ref.shape[2]
    size = lanes // 2
    rows = out.shape[0] // 2
    arriving = []
    features = []
    for t in range(tasks):
        for j in range(2):
            at = slice(j * size, (j + 1) * size)
            arriving.append(copies.start(w_ref.at[first + t, :, at], w_buf.at[t, :, at]))
            if not features:
                features = [copies.start(own_ref, own_buf), copies.start(sib_ref, sib_buf)]
    for t in range(tasks):
        for j in range(2):
            at = slice(j * size, (j + 1) * size)
            arriving[2 * t + j].wait()
            for s, (source, place) in enumerate(((own_buf, core), (sib_buf, 1 - core))):
                if t + j == 0:
                    features[s].wait()
                value = dot(source[...], w_buf[t, :, at], (1, 0)).astype(bf16)
                out_buf[t, s, :, :, at] = value.reshape(rows, out.shape[2], size)
                copies.out(
                    out_buf.at[t, s, :, :, at],
                    out.at[pl.ds(pl.multiple_of(place * rows, rows), rows), first + t, :, at],
                )
    copies.finish()


def weights_kernel(near, cores, which_ref, *refs):
    sources, cot_ref, refs = refs[: len(cores)], refs[len(cores)], refs[len(cores) + 1 :]
    added_ref, refs = (None, refs) if near else (refs[0], refs[1:])
    out, feat_buf, flip_buf, cot_buf, out_buf, sems = refs
    copies = Copies(sems)
    core = which_ref[0]
    tasks = out.shape[0]
    pixels, channels = feat_buf.shape[2:]
    pieces = channels // lane
    lanes = cot_buf.shape[4]
    rows = cot_buf.shape[2]
    features = []
    for j in range(2):
        for s, ref in enumerate(sources):
            if near:
                features.append(
                    [
                        copies.start(
                            ref.at[:, pl.ds(pl.multiple_of((4 * piece + which_ref[1 + j]) * lane, lane), lane)],
                            feat_buf.at[j, s, :, piece * lane : (piece + 1) * lane],
                        )
                        for piece in range(pieces)
                    ]
                )
            else:
                features.append([copies.start(ref.at[j], feat_buf.at[j, s])])
    start = 0 if near else which_ref[3] * (2 * rows)
    cots, more = [], []
    for t in range(tasks):
        cots.append(
            [
                copies.start(
                    cot_ref.at[pl.ds(pl.multiple_of(start + place * rows, rows), rows), t], cot_buf.at[t, s]
                )
                for s, place in enumerate([core if c == 0 else 1 - core for c in cores])
            ]
        )
        if not near:
            more.append([copies.start(added_ref.at[t, j], out_buf.at[t, j]) for j in range(2)])
    for t in range(tasks):
        for j in range(2):
            if t == 0:
                for s in range(len(cores)):
                    for copy in features[len(cores) * j + s]:
                        copy.wait()
                    flip_buf[j, :, s * pixels : (s + 1) * pixels] = feat_buf[j, s].T
            if j == 0:
                for copy in cots[t]:
                    copy.wait()
            value = dot(flip_buf[j], cot_buf[t].reshape(len(cores) * pixels, lanes), (1, 0))
            if not near:
                more[t][j].wait()
                value = value + out_buf[t, j].astype(f32)
            out_buf[t, j] = value.astype(bf16)
            copies.out(out_buf.at[t, j], out.at[t, j])
    copies.finish()


def validity(bucket_shape, pixel_mask):
    row_index = lax.broadcasted_iota(jnp.int32, pixel_mask.shape, 1)
    col_index = lax.broadcasted_iota(jnp.int32, pixel_mask.shape, 2)
    inside = (row_index < bucket_shape[:, 0][:, None, None]) & (
        col_index < bucket_shape[:, 1][:, None, None]
    )
    return jnp.where(inside, pixel_mask, 0).astype(f32)


def from_everyone(rows):
    return lax.all_to_all(rows, everyone, 0, 0, tiled=True)


def swap_core(value):
    return lax.ppermute(value, "task", [(0, 1), (1, 0)])


def pick(value, axis, index):
    return lax.dynamic_index_in_dim(value, index, axis, keepdims=False)


def two(value, axis, first, second):
    return jnp.stack([pick(value, axis, first), pick(value, axis, second)], axis)


def on_device(
    images,
    bucket_shape,
    pixel_mask,
    thresholds,
    reduce_weight,
    spatial_weight,
    expand_weight,
    mid_gains,
    mid_biases,
    out_gain,
    out_bias,
    head_weights,
    head_cotangent,
):
    image_count = images.shape[0]
    side = images.shape[1]
    width = images.shape[3]
    middle = reduce_weight.shape[1]
    tasks = head_weights.shape[1]
    lanes = head_weights.shape[2]
    pixels = image_count * side * side
    peers = lax.axis_size("dp")
    devices = 2 * peers
    core = lax.axis_index("task")
    low = max(0, (lane * peers // width).bit_length() - 1)
    bit_x, bit_y = 1 << low, 2 << low
    position = lax.axis_index("dp")
    my_x, my_y = (position >> low) & 1, (position >> (low + 1)) & 1
    def pairing(bit_of, cross):
        pairs = []
        for i in range(peers):
            for c in range(2):
                if cross:
                    pairs.append((2 * i + c, 2 * (i ^ bit_of[1 - c]) + 1 - c))
                else:
                    pairs.append((2 * i + c, 2 * (i ^ bit_of[c]) + c))
        return pairs

    def swap_first(value):
        return lax.ppermute(value, everyone, pairing((bit_x, bit_y), False))

    def swap_second(value):
        return lax.ppermute(value, everyone, pairing((bit_y, bit_x), False))

    def swap_cross(value):
        return lax.ppermute(value, everyone, pairing((bit_x, bit_y), True))

    def by_core(zero, one):
        return jnp.where(core == 0, zero, one)

    twos = []
    for i in range(peers):
        for c, bit in enumerate((bit_y, bit_x)):
            if not i & bit:
                twos.append([2 * i + c, 2 * (i | bit) + c])
    rest_bits = [b for b in range(peers.bit_length() - 1) if not (1 << b) & (bit_x | bit_y)]

    def swap_rest(value, done):
        bit = rest_bits[done]
        return lax.ppermute(value, "dp", [(i, i ^ (1 << bit)) for i in range(peers)])

    def halved(pairs, after=()):
        outs, scratch, big, which, count = [], [], [], [], 0
        for kept, came, axis, indices in pairs:
            half = kept.shape[axis] // 2
            shape = kept.shape[:axis] + ((half,) if half > 1 else ()) + kept.shape[axis + 1 :]
            outs += [(shape, bf16, True)] * 2
            scratch += [pltpu.VMEM(kept.shape, bf16)] * 2
            big += [kept, came]
            which += list(indices)
            count += 2 + 2 * half
        return kernel_call(
            functools.partial(halve_kernel, tuple(axis for _, _, axis, _ in pairs)),
            outs,
            big=tuple(big),
            scalars=scalars(*which),
            scratch=scratch,
            copies=count,
            after=after,
            name="halve",
        )

    def rest_part(kept, came, dim, done):
        mine = (position >> rest_bits[done]) & 1
        return kept, came, dim + len(rest_bits) - 1 - done, (1 - mine, mine)

    fours, rests = {}, {}
    for i in range(peers):
        fours.setdefault(i & ~(bit_x | bit_y), []).append(i)
        rests.setdefault(i & (bit_x | bit_y), []).append(i)
    fours, rests = list(fours.values()), list(rests.values())

    def exchanged(value, members):
        came = lax.all_to_all(value, "dp", 0, 0, axis_index_groups=members, tiled=True)
        return jnp.sum(came.astype(f32), axis=0)

    inputs = images.reshape(pixels, width)
    valid = validity(bucket_shape, pixel_mask).reshape(pixels, 1)
    norms = jnp.stack([mid_gains, mid_biases], axis=1)
    gain_row, bias_row = out_gain.reshape(1, width), out_bias.reshape(1, width)
    levels_flat = thresholds.reshape(pixels, width)
    cot = head_cotangent.transpose(0, 1, 3, 2, 4).reshape(2 * image_count * side, tasks, side, lanes)
    rows_half = image_count * side
    weights = head_weights.transpose(1, 0, 2)
    half_lanes = lanes // 2
    block = 4 * lane
    blocks = width // block

    pairs = []
    for i in range(peers):
        for c, bit in enumerate((bit_x, bit_y)):
            if not i & bit:
                pairs.append([2 * i + c, 2 * (i ^ bit) + c])
    pair_cot = lax.all_gather(cot, everyone, axis=0, tiled=True, axis_index_groups=pairs)

    mid = (pixels, middle)
    whole = (pixels, width)
    pair = (2, middle)
    stat_two, stat_three = (devices, 2, middle), (devices, 3, middle)

    def scalars(*values):
        return jnp.stack(values).astype(jnp.int32)

    def task_half(half, after):
        return kernel_call(
            task_kernel,
            [((tasks, pixels, width), bf16, True)],
            big=(cot, weights),
            scalars=scalars(half),
            scratch=[
                pltpu.VMEM((tasks, rows_half, side, lanes), bf16),
                pltpu.VMEM((2 * tasks, width // 2, lanes), bf16),
                pltpu.VMEM((2 * tasks, pixels, width // 2), bf16),
            ],
            copies=5 * tasks,
            after=after,
            name="task_grad",
        )[0]

    pre_reduce, stats = kernel_call(
        reduce_kernel,
        [(mid, f32, False), (stat_three, f32, False)],
        small=(valid,),
        big=(inputs, reduce_weight),
        scratch=[pltpu.VMEM(whole, bf16), pltpu.VMEM(reduce_weight.shape, bf16)],
        copies=8,
        after=(norms,),
        name="reduce",
    )
    table_one = from_everyone(stats)
    task_mine = task_half(core, (stats,))

    padded = (3, image_count, (side + 2) * side, middle)
    pre_spatial, consts_one, stats, acts = kernel_call(
        functools.partial(spatial_kernel, side),
        [(mid, f32, False), (pair, f32, False), (stat_two, f32, False), (padded, bf16, True)],
        small=(pre_reduce, table_one, norms[0], valid),
        big=(spatial_weight,),
        scratch=[pltpu.VMEM(spatial_weight.shape, bf16), pltpu.VMEM(padded, bf16)],
        copies=10,
        after=(task_mine,),
        name="spatial",
    )
    table_two = from_everyone(stats)
    task_sent = task_half(1 - core, (stats,))
    task_other = swap_core(held_until((table_two,), task_sent)[0])

    act_spatial, consts_two, stats, pre_expand = kernel_call(
        expand_kernel,
        [(mid, bf16, False), (pair, f32, False), ((devices, 2, width), f32, True), (whole, f32, True)],
        small=(pre_spatial, table_two, table_one, norms[1], valid),
        big=(expand_weight,),
        scratch=[
            pltpu.VMEM(expand_weight.shape, bf16),
            pltpu.VMEM(whole, f32),
            pltpu.VMEM((devices, 2, width), f32),
        ],
        copies=12,
        after=(task_sent,),
        name="expand",
    )
    table_three = from_everyone(stats)
    (merged,) = kernel_call(
        drop_kernel,
        [(whole, f32, True)],
        big=(task_mine, task_other, levels_flat),
        scratch=[
            pltpu.VMEM((tasks,) + whole, bf16),
            pltpu.VMEM((tasks,) + whole, bf16),
            pltpu.VMEM(whole, jnp.int32),
            pltpu.VMEM(whole, f32),
        ],
        copies=32,
        after=(stats,),
        name="graddrop",
    )


    pair_blocks = (2, pixels, width // 4)
    x_send, y_send = 2 * (1 - my_x), 1 - my_y
    consts_three, sums, features, same, cross, grad_residual = kernel_call(
        residual_kernel,
        [
            ((2, width), f32, False),
            ((devices, 2, width), f32, True),
            (whole, bf16, True),
            (pair_blocks, bf16, True),
            (pair_blocks, bf16, True),
            (whole, f32, True),
        ],
        scalars=scalars(
            by_core(x_send, y_send),
            by_core(x_send + 1, y_send + 2),
            by_core(y_send, x_send),
            by_core(y_send + 2, x_send + 1),
        ),
        small=(table_three, table_one, gain_row, bias_row, valid),
        big=(pre_expand, inputs, merged),
        scratch=[
            pltpu.VMEM(whole, f32),
            pltpu.VMEM(whole, bf16),
            pltpu.VMEM(whole, f32),
            pltpu.VMEM(whole, bf16),
            pltpu.VMEM((4, pixels, width // 4), bf16),
            pltpu.VMEM(whole, f32),
            pltpu.VMEM((devices, 2, width), f32),
        ],
        copies=28,
        name="residual",
    )
    table_four = from_everyone(sums)
    sibling = swap_core(features)
    far = swap_first(same)
    acts, act_spatial = held_until((features,), acts, act_spatial)
    acts_sib, act_spatial_sib = swap_core(acts), swap_core(act_spatial)

    def heads(first, count, after, fills):
        return kernel_call(
            functools.partial(heads_kernel, first),
            [(cot.shape, bf16, True)],
            big=(features, sibling, weights),
            scalars=scalars(core),
            scratch=[
                pltpu.VMEM(whole, bf16),
                pltpu.VMEM(whole, bf16),
                pltpu.VMEM((count, width, lanes), bf16),
                pltpu.VMEM((count, 2, rows_half, side, lanes), bf16),
            ],
            copies=2 + 6 * count,
            after=after,
            fills=fills,
            name="heads",
        )[0]


    part_shape = (tasks, 2, width // 4, lanes)

    def weight_part(near, cores, sources, cots, added, after):
        n = len(cores)
        return kernel_call(
            functools.partial(weights_kernel, near, cores),
            [(part_shape, bf16, True)],
            big=sources + (cots,) + added,
            scalars=scalars(
                core,
                by_core(my_x, 2 * my_y),
                by_core(my_x + 2, 2 * my_y + 1),
                1 - by_core(my_x, my_y),
            ),
            scratch=[
                pltpu.VMEM((2, n, pixels, width // 4), bf16),
                pltpu.VMEM((2, width // 4, n * pixels), bf16),
                pltpu.VMEM((tasks, n, rows_half, side, lanes), bf16),
                pltpu.VMEM(part_shape, bf16),
            ],
            copies=4 * blocks + 10 * tasks,
            after=after,
            name="heads_grad",
        )[0]

    index = by_core(my_y, my_x)
    near_part = weight_part(True, (0, 1), (features, sibling), cot, (), (sums, same))
    (cross,) = held_until((far, near_part), cross)
    far_cross = swap_cross(cross)
    half_part = weight_part(False, (0,), (far,), pair_cot, (near_part,), (cross,))
    heads_part = weight_part(False, (1,), (far_cross,), pair_cot, (half_part,), ())
    (heads_part,) = held_until((table_four,), heads_part)
    heads_half = lax.psum_scatter(
        heads_part.reshape(tasks, width // 2, lanes),
        everyone,
        scatter_dimension=1,
        axis_index_groups=twos,
        tiled=True,
    )

    expand_half, spatial_half = (pixels, width // 2), (pixels, middle // 2)
    out_totals, shifted_two, sums, expand_mine, expand_sent = kernel_call(
        expand_back_kernel,
        [
            ((2, width), f32, False),
            (mid, f32, False),
            (stat_two, f32, False),
            (expand_half, bf16, True),
            (expand_half, bf16, True),
        ],
        scalars=scalars(core),
        small=(consts_three, table_four, gain_row, valid, table_one, pre_spatial, consts_two, norms[1]),
        big=(grad_residual, pre_expand, expand_weight),
        scratch=[
            pltpu.VMEM(whole, f32),
            pltpu.VMEM(whole, f32),
            pltpu.VMEM(expand_weight.shape, bf16),
            pltpu.VMEM(whole, bf16),
        ],
        copies=14,
        after=(heads_part,),
        name="expand_back",
    )
    table_five = from_everyone(sums)
    expand_sib = swap_core(expand_sent)
    totals_two, shifted_one, sums, spatial_mine, spatial_sent = kernel_call(
        functools.partial(spatial_back_kernel, side),
        [
            (pair, f32, False),
            (mid, f32, False),
            (stat_two, f32, False),
            (spatial_half, bf16, True),
            (spatial_half, bf16, True),
        ],
        scalars=scalars(core),
        small=(
            shifted_two, pre_spatial, consts_two, table_five, norms[1], valid, table_one,
            pre_reduce, consts_one, norms[0],
        ),
        big=(spatial_weight,),
        scratch=[
            pltpu.VMEM(spatial_weight.shape, bf16),
            pltpu.VMEM(padded, bf16),
            pltpu.VMEM(mid, bf16),
        ],
        copies=11,
        name="spatial_back",
    )
    table_six = from_everyone(sums)
    spatial_sib = swap_core(spatial_sent)
    x_out, y_out, x_in, y_in = 1 - my_x, 2 * (1 - my_y), my_x, 2 * my_y
    pair_parts = (
        by_core(x_out, y_out),
        by_core(x_out + 2, y_out + 1),
        by_core(x_in, y_in),
        by_core(x_in + 2, y_in + 1),
    )
    high, rows_of_pair = peers >> (low + 2), (1 << low) * (middle // peers)
    early_shape = (2, blocks + 9, high, rows_of_pair, middle // 2)
    early_sent, early_kept = kernel_call(
        functools.partial(trunk_weights_kernel, side),
        [(early_shape, bf16, True), (early_shape, bf16, True)],
        scalars=scalars(*pair_parts),
        small=(act_spatial, act_spatial_sib, spatial_mine, spatial_sib),
        big=(acts, acts_sib, expand_mine, expand_sib),
        scratch=[
            pltpu.VMEM((2,) + padded, bf16),
            pltpu.VMEM((2,) + expand_half, bf16),
            pltpu.VMEM((blocks + 9, high, 4, rows_of_pair, middle // 2), bf16),
        ],
        copies=4 + 4 * (blocks + 9),
        after=(sums,),
        name="trunk_weights",
    )
    (early_sent,) = held_until((table_six,), early_sent)
    early_came = swap_first(early_sent)
    dp_rows = (peers, width // devices, middle)
    totals_one, images_grad, reduce_sent, reduce_kept = kernel_call(
        reduce_back_kernel,
        [(pair, f32, False), (whole, f32, True), (dp_rows, bf16, True), (dp_rows, bf16, True)],
        scalars=scalars(core),
        small=(shifted_one, pre_reduce, consts_one, table_six, norms[0], valid, table_one),
        big=(reduce_weight, grad_residual, inputs),
        scratch=[
            pltpu.VMEM(mid, bf16),
            pltpu.VMEM(reduce_weight.shape, bf16),
            pltpu.VMEM(whole, f32),
            pltpu.VMEM(whole, bf16),
            pltpu.VMEM((peers, 2, width // devices, middle), bf16),
        ],
        copies=24,
        after=(early_kept,),
        name="reduce_back",
    )
    reduce_came = swap_core(reduce_sent)
    (heads_half,) = held_until((reduce_kept,), heads_half)
    heads_grad = lax.psum_scatter(
        heads_half, "dp", scatter_dimension=1, axis_index_groups=rests, tiled=True
    )
    heads_grad = heads_grad.astype(f32)
    quarters = (high, 4, (1 << low) * dp_rows[1], middle)
    reduce_sent, reduce_kept = halved(
        [(reduce_kept.reshape(quarters), reduce_came.reshape(quarters), 1, pair_parts)]
    )
    reduce_came = swap_first(reduce_sent)
    head_values = heads(0, 2, (reduce_kept,), False)
    early_sent, early_kept, reduce_sent, reduce_kept = halved(
        [
            (early_kept, early_came, 0, (1 - index, index)),
            (reduce_kept, reduce_came, 1, (1 - index, index)),
        ],
        (head_values,),
    )
    early_came, reduce_came = swap_second(early_sent), swap_second(reduce_sent)
    head_values = heads(2, tasks - 2, (head_values, reduce_kept), True)
    head_output = head_values.reshape(2 * image_count, side, tasks, side, lanes).transpose(0, 1, 3, 2, 4)
    early = (early_kept.astype(f32) + early_came.astype(f32)).astype(bf16)
    early = early.reshape(blocks + 9, peers // 4, -1, middle // 2).transpose(1, 0, 2, 3)
    late = (reduce_kept.astype(f32) + reduce_came.astype(f32)).astype(bf16)
    both = jnp.concatenate(
        [early.reshape(peers // 4, -1, middle // 2), late.reshape(peers // 4, -1, middle // 2)], axis=1
    )
    came = lax.all_to_all(both, "dp", 0, 0, axis_index_groups=rests, tiled=True)
    (came,) = held_until((head_values, heads_grad), came)
    both = jnp.sum(came.astype(f32), axis=0)
    heads_grad = heads_grad.transpose(1, 0, 2)
    split = (blocks + 9) * (middle // peers)
    early = both[:split].reshape(blocks + 9, -1, middle // 2)
    reduce_grad = both[split:].reshape(-1, middle)

    own_rows = early.reshape(early.shape[0], 2, -1, early.shape[2])
    came_rows = swap_core(pick(own_rows, 1, 1 - core))
    own_rows = pick(own_rows, 1, core)
    halves = jnp.stack(
        [jnp.where(core == 0, own_rows, came_rows), jnp.where(core == 0, came_rows, own_rows)]
    ).astype(f32)
    expand_grad = halves[:, :blocks].transpose(2, 0, 1, 3).reshape(middle // devices, width)
    spatial_grad = halves[:, blocks:].transpose(1, 2, 0, 3).reshape(9, middle // devices, middle)
    gains_grad = jnp.stack([totals_one[1], totals_two[1]], axis=0)
    biases_grad = jnp.stack([totals_one[0], totals_two[0]], axis=0)
    return (
        head_output,
        images_grad.reshape(images.shape),
        reduce_grad,
        spatial_grad,
        expand_grad,
        gains_grad,
        biases_grad,
        out_totals[1],
        out_totals[0],
        heads_grad,
    )


def solution(mesh):
    placed = (
        P(("dp", "task"), None, None, None),
        P(("dp", "task"), None),
        P(("dp", "task"), None, None),
        P(("dp", "task"), None, None, None),
        P(),
        P(),
        P(),
        P(),
        P(),
        P(),
        P(),
        P(None, None, "task"),
        P("dp", None, None, None, "task"),
    )
    return jax.shard_map(
        on_device,
        mesh=mesh,
        in_specs=placed,
        out_specs=(
            P("dp", None, None, None, "task"),
            P(("dp", "task"), None, None, None),
            P(("dp", "task"), None),
            P(None, ("dp", "task"), None),
            P(("dp", "task"), None),
            P(),
            P(),
            P(),
            P(),
            P("dp", None, "task"),
        ),
        check_vma=False,
    )
```

```python
import functools

import jax
import jax.numpy as jnp
from jax import lax
from jax.experimental import pallas as pl
from jax.experimental.pallas import tpu as pltpu
from jax.sharding import PartitionSpec as P

epsilon = 1e-05
steepness = 6.0
levels = 4096.0
everyone = ("dp", "task")
f32 = jnp.float32
bf16 = jnp.bfloat16
lane = 128
MIB = 1 << 20


def dot(left, right, contract):
    return lax.dot_general(
        left, right, ((contract[0:1], contract[1:2]), ((), ())), preferred_element_type=f32
    )


def kernel_call(body, outs, small=(), big=(), scalars=None, scratch=(), copies=0, after=(), fills=False, name=None):
    skipped = len(after)

    def ordered(*refs):
        body(*refs[skipped:])

    big = [pltpu.with_memory_space_constraint(array, pltpu.HBM) for array in big]
    there = pl.BlockSpec(memory_space=pl.ANY)
    here = pl.BlockSpec(memory_space=pltpu.VMEM)
    given = [] if scalars is None else [scalars]
    return pl.pallas_call(
        ordered,
        in_specs=[there] * skipped
        + [pl.BlockSpec(memory_space=pltpu.SMEM)] * len(given)
        + [here] * len(small)
        + [there] * len(big),
        out_specs=[there if streamed else here for _, _, streamed in outs],
        out_shape=[
            pltpu.HBM(shape, dtype) if streamed else jax.ShapeDtypeStruct(shape, dtype)
            for shape, dtype, streamed in outs
        ],
        scratch_shapes=list(scratch) + ([pltpu.SemaphoreType.DMA((copies,))] if copies else []),
        input_output_aliases={0: 0} if fills else {},
        compiler_params=pltpu.CompilerParams(vmem_limit_bytes=48 * MIB),
        name=name,
    )(*after, *given, *small, *big)


def held_until(after, *values):
    def body(*refs):
        pass

    there = pl.BlockSpec(memory_space=pl.ANY)
    return pl.pallas_call(
        body,
        in_specs=[there] * (len(values) + len(after)),
        out_specs=[there] * len(values),
        out_shape=[jax.ShapeDtypeStruct(v.shape, v.dtype) for v in values],
        input_output_aliases={i: i for i in range(len(values))},
        name="held",
    )(*values, *after)


class Copies:
    def __init__(self, sems):
        self.sems = sems
        self.used = 0
        self.open = []

    def start(self, source, target):
        copy = pltpu.make_async_copy(source, target, self.sems.at[self.used])
        self.used += 1
        copy.start()
        return copy

    def out(self, source, target):
        self.open.append(self.start(source, target))

    def finish(self):
        for copy in self.open:
            copy.wait()


def columns(ref, index, size):
    return ref.at[:, index * size : (index + 1) * size]


def sigmoid(value):
    return 0.5 + 0.5 * jnp.tanh(0.5 * value)


def combined(table, counts):
    counts = counts[:, 0:1]
    total = jnp.sum(counts)
    center = jnp.sum(table[:, 0, :], axis=0, keepdims=True) / total
    shift = table[:, 0, :] / jnp.maximum(counts, 1.0) - center
    variance = (
        jnp.sum(table[:, 1, :] + counts * shift * shift, axis=0, keepdims=True) / total
    )
    return center, lax.rsqrt(variance + epsilon)


def store_rows(stats_ref, rows, at=slice(None)):
    table = jnp.concatenate(rows, axis=0)
    stats_ref[:, :, at] = jnp.broadcast_to(table[None], (stats_ref.shape[0],) + table.shape)


def store_moments(stats_ref, values_ref, valid_ref, at=slice(None)):
    valid, values = valid_ref[...], values_ref[...]
    count = jnp.sum(valid)
    first = jnp.sum(values * valid, axis=0, keepdims=True)
    deviation = (values - first / jnp.maximum(count, 1.0)) * valid
    rows = [first, jnp.sum(deviation * deviation, axis=0, keepdims=True)]
    if stats_ref.shape[1] > 2:
        rows.append(jnp.broadcast_to(count, first.shape))
    store_rows(stats_ref, rows, at)


def store_sums(stats_ref, grad, normed, at=slice(None)):
    rows = [jnp.sum(grad, axis=0, keepdims=True), jnp.sum(grad * normed, axis=0, keepdims=True)]
    store_rows(stats_ref, rows, at)


def reduce_kernel(valid_ref, x_ref, w_ref, out_ref, stats_ref, x_buf, w_buf, sems):
    copies = Copies(sems)
    parts = 4
    size = x_ref.shape[1] // parts
    arriving = []
    for k in range(parts):
        arriving.append(
            (
                copies.start(columns(x_ref, k, size), columns(x_buf, k, size)),
                copies.start(w_ref.at[k * size : (k + 1) * size], w_buf.at[k * size : (k + 1) * size]),
            )
        )
    total = None
    for k, pair in enumerate(arriving):
        for copy in pair:
            copy.wait()
        part = dot(x_buf[:, k * size : (k + 1) * size], w_buf[k * size : (k + 1) * size, :], (1, 0))
        total = part if total is None else total + part
    out_ref[...] = total * valid_ref[...]
    store_moments(stats_ref, out_ref, valid_ref)


def pad_edges(acts_ref, side):
    images = acts_ref.shape[1]
    zeros = jnp.zeros((side, acts_ref.shape[3]), bf16)
    for shift in range(3):
        for image in range(images):
            acts_ref[shift, image, 0:side, :] = zeros
            acts_ref[shift, image, (side + 1) * side : (side + 2) * side, :] = zeros


def store_shifted(acts_ref, values, side):
    pixels = values.shape[0]
    column = lax.broadcasted_iota(jnp.int32, (pixels, 1), 0) % side
    before = jnp.where(column == 0, 0.0, pltpu.roll(values, 1, 0))
    after = jnp.where(column == side - 1, 0.0, pltpu.roll(values, pixels - 1, 0))
    for shift, moved in enumerate((before, values, after)):
        for image in range(acts_ref.shape[1]):
            rows = slice(image * side * side, (image + 1) * side * side)
            acts_ref[shift, image, side : side + side * side, :] = moved[rows].astype(bf16)


def window(acts_ref, row_shift, col_shift, side):
    images = acts_ref.shape[1]
    tile = acts_ref[col_shift, :, row_shift * side : row_shift * side + side * side, :]
    return tile.reshape(images * side * side, acts_ref.shape[3])


def spatial_kernel(
    side, pre_ref, table_ref, norm_ref, valid_ref, w_ref, out_ref, consts_ref, stats_ref, acts_out, w_buf, acts_ref, sems
):
    copies = Copies(sems)
    arriving = [copies.start(w_ref.at[k], w_buf.at[k]) for k in range(9)]
    center, inverse = combined(table_ref, table_ref[:, 2, :])
    consts_ref[0:1, :] = center
    consts_ref[1:2, :] = inverse
    gain, bias = norm_ref[0:1, :], norm_ref[1:2, :]
    pad_edges(acts_ref, side)

    shifted = gain * ((pre_ref[...] - center) * inverse) + bias
    store_shifted(acts_ref, valid_ref[...] * shifted * sigmoid(shifted), side)
    copies.out(acts_ref, acts_out)
    total = None
    for tap in range(9):
        arriving[tap].wait()
        part = dot(window(acts_ref, tap // 3, tap % 3, side), w_buf[tap], (1, 0))
        total = part if total is None else total + part
    out_ref[...] = total
    store_moments(stats_ref, out_ref, valid_ref)
    copies.finish()


def expand_kernel(
    pre_ref, table_ref, first_ref, norm_ref, valid_ref, w_ref, act_ref, consts_ref, stats_out, out,
    w_buf, out_buf, stats_ref, sems,
):
    copies = Copies(sems)
    parts = 4
    size = w_ref.shape[1] // parts
    arriving = [copies.start(columns(w_ref, k, size), columns(w_buf, k, size)) for k in range(parts)]
    center, inverse = combined(table_ref, first_ref[:, 2, :])
    consts_ref[0:1, :] = center
    consts_ref[1:2, :] = inverse
    gain, bias = norm_ref[0:1, :], norm_ref[1:2, :]

    shifted = gain * ((pre_ref[...] - center) * inverse) + bias
    act_ref[...] = (valid_ref[...] * shifted * sigmoid(shifted)).astype(bf16)
    for k in range(parts):
        at = slice(k * size, (k + 1) * size)
        arriving[k].wait()
        out_buf[:, at] = dot(act_ref[...], w_buf[:, at], (1, 0))
        copies.out(columns(out_buf, k, size), columns(out, k, size))
        store_moments(stats_ref, columns(out_buf, k, size), valid_ref, at)
        copies.out(stats_ref.at[:, :, at], stats_out.at[:, :, at])
    copies.finish()


def residual_kernel(
    which_ref, table_ref, first_ref, gain_ref, bias_ref, valid_ref, pre_ref, x_ref, merged_ref,
    consts_ref, sums_out, feat_out, same_out, cross_out, grad_out,
    pre_buf, x_buf, merged_buf, feat_buf, block_buf, grad_buf, sums_ref, sems,
):
    copies = Copies(sems)
    parts = 4
    size = pre_ref.shape[1] // parts
    arriving = []
    for k in range(parts):
        arriving.append(
            [
                copies.start(columns(ref, k, size), columns(buf, k, size))
                for ref, buf in ((pre_ref, pre_buf), (x_ref, x_buf), (merged_ref, merged_buf))
            ]
        )
    for k in range(parts):
        at = slice(k * size, (k + 1) * size)
        center, inverse = combined(table_ref[:, :, at], first_ref[:, 2, :])
        consts_ref[0:1, at] = center
        consts_ref[1:2, at] = inverse
        gain, bias = gain_ref[:, at], bias_ref[:, at]
        for copy in arriving[k]:
            copy.wait()

        valid = valid_ref[...]
        normed = (pre_buf[:, at] - center) * inverse
        value = x_buf[:, at].astype(f32) + gain * normed + bias
        sigma = sigmoid(value)
        features = (valid * (value * sigma)).astype(bf16)
        feat_buf[:, at] = features
        for piece in range(4):
            block_buf[2 * (piece % 2) + piece // 2, :, k * lane : (k + 1) * lane] = features[
                :, piece * lane : (piece + 1) * lane
            ]
        grad = merged_buf[:, at] * valid * (sigma * (1.0 + value * (1.0 - sigma)))
        grad_buf[:, at] = grad
        store_sums(sums_ref, grad, normed, at)
        copies.out(sums_ref.at[:, :, at], sums_out.at[:, :, at])
        copies.out(columns(grad_buf, k, size), columns(grad_out, k, size))
        copies.out(columns(feat_buf, k, size), columns(feat_out, k, size))
    for j in range(2):
        copies.out(block_buf.at[which_ref[j]], same_out.at[j])
        copies.out(block_buf.at[which_ref[2 + j]], cross_out.at[j])
    copies.finish()


def slope_rows(grad, pre_ref, consts_ref, norm_ref, valid_ref, out_ref, sums_ref):
    center, inverse = consts_ref[0:1, :], consts_ref[1:2, :]
    gain, bias = norm_ref[0:1, :], norm_ref[1:2, :]
    normed = (pre_ref[...] - center) * inverse
    value = gain * normed + bias
    sigma = sigmoid(value)
    grad = grad * valid_ref[...] * (sigma * (1.0 + value * (1.0 - sigma)))
    out_ref[...] = grad
    store_sums(sums_ref, grad, normed)


def expand_back_kernel(
    which_ref, consts_ref, table_ref, gain_ref, valid_ref, first_ref, mid_pre_ref, mid_consts_ref, mid_norm_ref,
    grad_ref, pre_ref, w_ref,
    totals_ref, shifted_ref, sums_ref, mine_out, sent_out,
    grad_buf, pre_buf, w_buf, out_buf, sems,
):
    copies = Copies(sems)
    parts = 4
    size = pre_ref.shape[1] // parts
    arriving = []
    for k in range(parts):
        arriving.append(
            [
                copies.start(columns(ref, k, size), columns(buf, k, size))
                for ref, buf in ((grad_ref, grad_buf), (pre_ref, pre_buf), (w_ref, w_buf))
            ]
        )
    count = jnp.sum(first_ref[:, 2, 0:1])
    total = None
    for k in range(parts):
        at = slice(k * size, (k + 1) * size)
        totals = jnp.sum(table_ref[:, :, at], axis=0)
        totals_ref[:, at] = totals
        center, inverse = consts_ref[0:1, at], consts_ref[1:2, at]
        plain, scaled = totals[0:1, :] / count, totals[1:2, :] / count
        scale = gain_ref[:, at] * inverse
        for copy in arriving[k]:
            copy.wait()

        normed = (pre_buf[:, at] - center) * inverse
        grad = scale * (grad_buf[:, at] - valid_ref[...] * (plain + normed * scaled))
        out_buf[:, at] = grad.astype(bf16)
        part = dot(out_buf[:, at], w_buf[:, at], (1, 1))
        total = part if total is None else total + part
    half = out_buf.shape[1] // 2
    for place, out in ((which_ref[0], mine_out), (1 - which_ref[0], sent_out)):
        copies.out(out_buf.at[:, pl.ds(pl.multiple_of(place * half, half), half)], out)
    slope_rows(total, mid_pre_ref, mid_consts_ref, mid_norm_ref, valid_ref, shifted_ref, sums_ref)
    copies.finish()


def spatial_back_kernel(
    side, which_ref, grad_ref, pre_ref, consts_ref, table_ref, norm_ref, valid_ref, first_ref,
    low_pre_ref, low_consts_ref, low_norm_ref, w_ref,
    totals_ref, shifted_ref, sums_ref, mine_out, sent_out,
    w_buf, acts_ref, out_ref, sems,
):
    copies = Copies(sems)
    arriving = [copies.start(w_ref.at[k], w_buf.at[k]) for k in range(9)]
    count = jnp.sum(first_ref[:, 2, 0:1])
    totals = jnp.sum(table_ref[...], axis=0)
    totals_ref[...] = totals
    center, inverse = consts_ref[0:1, :], consts_ref[1:2, :]
    plain, scaled = totals[0:1, :] / count, totals[1:2, :] / count
    scale = norm_ref[0:1, :] * inverse
    pad_edges(acts_ref, side)

    normed = (pre_ref[...] - center) * inverse
    grad = scale * (grad_ref[...] - valid_ref[...] * (plain + normed * scaled))
    out_ref[...] = grad.astype(bf16)
    half = out_ref.shape[1] // 2
    for place, out in ((which_ref[0], mine_out), (1 - which_ref[0], sent_out)):
        copies.out(out_ref.at[:, pl.ds(pl.multiple_of(place * half, half), half)], out)
    store_shifted(acts_ref, grad, side)
    total = None
    for tap in range(9):
        arriving[tap].wait()
        part = dot(window(acts_ref, 2 - tap // 3, 2 - tap % 3, side), w_buf[tap], (1, 1))
        total = part if total is None else total + part
    slope_rows(total, low_pre_ref, low_consts_ref, low_norm_ref, valid_ref, shifted_ref, sums_ref)
    copies.finish()


def reduce_back_kernel(
    which_ref, grad_ref, pre_ref, consts_ref, table_ref, norm_ref, valid_ref, first_ref, w_ref, res_ref, x_ref,
    totals_ref, images_out, sent_out, kept_out,
    low_buf, w_buf, res_buf, x_buf, part_buf, sems,
):
    copies = Copies(sems)
    parts = 4
    size = res_ref.shape[1] // parts
    arriving = []
    for k in range(parts):
        at = slice(k * size, (k + 1) * size)
        arriving.append(
            [
                copies.start(columns(x_ref, k, size), columns(x_buf, k, size)),
                copies.start(w_ref.at[at], w_buf.at[at]),
                copies.start(columns(res_ref, k, size), columns(res_buf, k, size)),
            ]
        )
    count = jnp.sum(first_ref[:, 2, 0:1])
    totals = jnp.sum(table_ref[...], axis=0)
    totals_ref[...] = totals
    center, inverse = consts_ref[0:1, :], consts_ref[1:2, :]
    plain, scaled = totals[0:1, :] / count, totals[1:2, :] / count
    scale = norm_ref[0:1, :] * inverse

    normed = (pre_ref[...] - center) * inverse
    grad = scale * (grad_ref[...] - valid_ref[...] * (plain + normed * scaled))
    low_buf[...] = grad.astype(bf16)
    for k in range(parts):
        at = slice(k * size, (k + 1) * size)
        arriving[k][0].wait()
        value = dot(x_buf[:, at], low_buf[...], (0, 0)).astype(bf16)
        peers = part_buf.shape[0] // parts
        dp = slice(k * peers, (k + 1) * peers)
        part_buf[dp] = value.reshape((peers,) + part_buf.shape[1:])
        copies.out(part_buf.at[dp, 1 - which_ref[0]], sent_out.at[dp])
        copies.out(part_buf.at[dp, which_ref[0]], kept_out.at[dp])
    for k in range(parts):
        at = slice(k * size, (k + 1) * size)
        arriving[k][1].wait()
        arriving[k][2].wait()
        res_buf[:, at] = res_buf[:, at] + valid_ref[...] * dot(low_buf[...], w_buf[at, :], (1, 1))
        copies.out(columns(res_buf, k, size), columns(images_out, k, size))
    copies.finish()


def trunk_weights_kernel(
    side, which_ref, act_ref, act_sib, right_ref, right_sib, acts_ref, acts_sib, grad_ref, grad_sib,
    sent_out, kept_out, acts_buf, grad_buf, out_buf, sems,
):
    copies = Copies(sems)
    size = right_ref.shape[1]
    blocks = grad_ref.shape[1] // size
    grads = [copies.start(ref, grad_buf.at[c]) for c, ref in enumerate((grad_ref, grad_sib))]
    acts = [copies.start(ref, acts_buf.at[c]) for c, ref in enumerate((acts_ref, acts_sib))]

    def store(place, value):
        out_buf[place] = value.astype(bf16).reshape(out_buf.shape[1:])
        for q in range(2):
            copies.out(out_buf.at[place, :, which_ref[q]], sent_out.at[q, place])
            copies.out(out_buf.at[place, :, which_ref[2 + q]], kept_out.at[q, place])

    for copy in grads:
        copy.wait()
    for b in range(blocks):
        at = slice(b * size, (b + 1) * size)
        store(b, dot(act_ref[...], grad_buf[0, :, at], (0, 0)) + dot(act_sib[...], grad_buf[1, :, at], (0, 0)))
    for copy in acts:
        copy.wait()
    for tap in range(9):
        tiles = [window(acts_buf.at[c], tap // 3, tap % 3, side) for c in range(2)]
        store(blocks + tap, dot(tiles[0], right_ref[...], (0, 0)) + dot(tiles[1], right_sib[...], (0, 0)))
    copies.finish()


def halve_kernel(axes, which_ref, *refs):
    n = len(axes)
    ins, outs, bufs, sems = refs[: 2 * n], refs[2 * n : 4 * n], refs[4 * n : 6 * n], refs[6 * n]
    copies = Copies(sems)
    arriving = [copies.start(ref, buf) for ref, buf in zip(ins, bufs)]
    first = 0
    for p, axis in enumerate(axes):
        kept_buf, came_buf = bufs[2 * p : 2 * p + 2]
        arriving[2 * p].wait()
        arriving[2 * p + 1].wait()
        kept_buf[...] = (kept_buf[...].astype(f32) + came_buf[...].astype(f32)).astype(bf16)
        count = kept_buf.shape[axis] // 2
        lead = (slice(None),) * axis
        for out in outs[2 * p : 2 * p + 2]:
            for i in range(count):
                target = lead + ((i,) if count > 1 else ())
                copies.out(kept_buf.at[lead + (which_ref[first],)], out.at[target] if target else out)
                first = first + 1
    copies.finish()


def task_kernel(half_ref, cot_ref, w_ref, out, cot_buf, w_buf, out_buf, sems):
    copies = Copies(sems)
    tasks, pixels = out.shape[:2]
    size = w_buf.shape[1]
    parts = w_ref.shape[1] // size
    rows = cot_buf.shape[1]
    start = pl.multiple_of(half_ref[0] * rows, rows)
    cots, arriving = [], []
    for t in range(tasks):
        cots.append(copies.start(cot_ref.at[pl.ds(start, rows), t], cot_buf.at[t]))
        for j in range(parts):
            arriving.append(copies.start(w_ref.at[t, j * size : (j + 1) * size], w_buf.at[t * parts + j]))
    for t in range(tasks):
        cots[t].wait()
        for j in range(parts):
            slot = t * parts + j
            arriving[slot].wait()
            cot = cot_buf[t].reshape(pixels, cot_buf.shape[3])
            out_buf[slot] = dot(cot, w_buf[slot], (1, 1)).astype(bf16)
            copies.out(out_buf.at[slot], out.at[t, :, j * size : (j + 1) * size])
    copies.finish()


def drop_kernel(mine_ref, other_ref, level_ref, out, mine_buf, other_buf, level_buf, out_buf, sems):
    copies = Copies(sems)
    tasks, pixels, _ = mine_ref.shape
    parts = 8
    size = pixels // parts
    arriving = []
    for k in range(parts):
        at = slice(k * size, (k + 1) * size)
        arriving.append(
            [
                copies.start(mine_ref.at[:, at], mine_buf.at[:, at]),
                copies.start(other_ref.at[:, at], other_buf.at[:, at]),
                copies.start(level_ref.at[at], level_buf.at[at]),
            ]
        )
    for k in range(parts):
        for copy in arriving[k]:
            copy.wait()

        rows = slice(k * size, (k + 1) * size)
        grads = [mine_buf[t, rows].astype(f32) + other_buf[t, rows].astype(f32) for t in range(tasks)]
        total, spread = None, None
        for grad in grads:
            squared = grad * grad + 1.0
            root = squared * lax.rsqrt(squared)
            spread = root if spread is None else spread + root
            total = grad if total is None else total + grad
        margin = (0.25 * steepness) * (total / spread) + (
            0.25 * steepness * (1.0 - 1.0 / levels)
            - level_buf[rows].astype(f32) * (0.5 * steepness / levels)
        )
        merged = total
        for grad in grads:
            merged = merged + grad * jnp.tanh(jnp.tanh(grad) * margin)
        out_buf[rows] = 0.5 * merged
        at = slice(k * size, (k + 1) * size)
        copies.out(out_buf.at[at], out.at[at])
    copies.finish()


def heads_kernel(first, which_ref, own_ref, sib_ref, w_ref, out, own_buf, sib_buf, w_buf, out_buf, sems):
    copies = Copies(sems)
    core = which_ref[0]
    tasks = w_buf.shape[0]
    lanes = w_ref.shape[2]
    size = lanes // 2
    rows = out.shape[0] // 2
    arriving = []
    features = []
    for t in range(tasks):
        for j in range(2):
            at = slice(j * size, (j + 1) * size)
            arriving.append(copies.start(w_ref.at[first + t, :, at], w_buf.at[t, :, at]))
            if not features:
                features = [copies.start(own_ref, own_buf), copies.start(sib_ref, sib_buf)]
    for t in range(tasks):
        for j in range(2):
            at = slice(j * size, (j + 1) * size)
            arriving[2 * t + j].wait()
            for s, (source, place) in enumerate(((own_buf, core), (sib_buf, 1 - core))):
                if t + j == 0:
                    features[s].wait()
                value = dot(source[...], w_buf[t, :, at], (1, 0)).astype(bf16)
                out_buf[t, s, :, :, at] = value.reshape(rows, out.shape[2], size)
                copies.out(
                    out_buf.at[t, s, :, :, at],
                    out.at[pl.ds(pl.multiple_of(place * rows, rows), rows), first + t, :, at],
                )
    copies.finish()


def weights_kernel(near, cores, which_ref, *refs):
    sources, cot_ref, refs = refs[: len(cores)], refs[len(cores)], refs[len(cores) + 1 :]
    added_ref, refs = (None, refs) if near else (refs[0], refs[1:])
    out, feat_buf, flip_buf, cot_buf, out_buf, sems = refs
    copies = Copies(sems)
    core = which_ref[0]
    tasks = out.shape[0]
    pixels, channels = feat_buf.shape[2:]
    pieces = channels // lane
    lanes = cot_buf.shape[4]
    rows = cot_buf.shape[2]
    features = []
    for j in range(2):
        for s, ref in enumerate(sources):
            if near:
                features.append(
                    [
                        copies.start(
                            ref.at[:, pl.ds(pl.multiple_of((4 * piece + which_ref[1 + j]) * lane, lane), lane)],
                            feat_buf.at[j, s, :, piece * lane : (piece + 1) * lane],
                        )
                        for piece in range(pieces)
                    ]
                )
            else:
                features.append([copies.start(ref.at[j], feat_buf.at[j, s])])
    start = 0 if near else which_ref[3] * (2 * rows)
    cots, more = [], []
    for t in range(tasks):
        cots.append(
            [
                copies.start(
                    cot_ref.at[pl.ds(pl.multiple_of(start + place * rows, rows), rows), t], cot_buf.at[t, s]
                )
                for s, place in enumerate([core if c == 0 else 1 - core for c in cores])
            ]
        )
        if not near:
            more.append([copies.start(added_ref.at[t, j], out_buf.at[t, j]) for j in range(2)])
    for t in range(tasks):
        for j in range(2):
            if t == 0:
                for s in range(len(cores)):
                    for copy in features[len(cores) * j + s]:
                        copy.wait()
                    flip_buf[j, :, s * pixels : (s + 1) * pixels] = feat_buf[j, s].T
            if j == 0:
                for copy in cots[t]:
                    copy.wait()
            value = dot(flip_buf[j], cot_buf[t].reshape(len(cores) * pixels, lanes), (1, 0))
            if not near:
                more[t][j].wait()
                value = value + out_buf[t, j].astype(f32)
            out_buf[t, j] = value.astype(bf16)
            copies.out(out_buf.at[t, j], out.at[t, j])
    copies.finish()


def validity(bucket_shape, pixel_mask):
    row_index = lax.broadcasted_iota(jnp.int32, pixel_mask.shape, 1)
    col_index = lax.broadcasted_iota(jnp.int32, pixel_mask.shape, 2)
    inside = (row_index < bucket_shape[:, 0][:, None, None]) & (
        col_index < bucket_shape[:, 1][:, None, None]
    )
    return jnp.where(inside, pixel_mask, 0).astype(f32)


def from_everyone(rows):
    return lax.all_to_all(rows, everyone, 0, 0, tiled=True)


def swap_core(value):
    return lax.ppermute(value, "task", [(0, 1), (1, 0)])


def pick(value, axis, index):
    return lax.dynamic_index_in_dim(value, index, axis, keepdims=False)


def two(value, axis, first, second):
    return jnp.stack([pick(value, axis, first), pick(value, axis, second)], axis)


def on_device(
    images,
    bucket_shape,
    pixel_mask,
    thresholds,
    reduce_weight,
    spatial_weight,
    expand_weight,
    mid_gains,
    mid_biases,
    out_gain,
    out_bias,
    head_weights,
    head_cotangent,
):
    image_count = images.shape[0]
    side = images.shape[1]
    width = images.shape[3]
    middle = reduce_weight.shape[1]
    tasks = head_weights.shape[1]
    lanes = head_weights.shape[2]
    pixels = image_count * side * side
    peers = lax.axis_size("dp")
    devices = 2 * peers
    core = lax.axis_index("task")
    low = max(0, (lane * peers // width).bit_length() - 1)
    bit_x, bit_y = 1 << low, 2 << low
    position = lax.axis_index("dp")
    my_x, my_y = (position >> low) & 1, (position >> (low + 1)) & 1
    def pairing(bit_of, cross):
        pairs = []
        for i in range(peers):
            for c in range(2):
                if cross:
                    pairs.append((2 * i + c, 2 * (i ^ bit_of[1 - c]) + 1 - c))
                else:
                    pairs.append((2 * i + c, 2 * (i ^ bit_of[c]) + c))
        return pairs

    def swap_first(value):
        return lax.ppermute(value, everyone, pairing((bit_x, bit_y), False))

    def swap_second(value):
        return lax.ppermute(value, everyone, pairing((bit_y, bit_x), False))

    def swap_cross(value):
        return lax.ppermute(value, everyone, pairing((bit_x, bit_y), True))

    def by_core(zero, one):
        return jnp.where(core == 0, zero, one)

    twos = []
    for i in range(peers):
        for c, bit in enumerate((bit_y, bit_x)):
            if not i & bit:
                twos.append([2 * i + c, 2 * (i | bit) + c])
    rest_bits = [b for b in range(peers.bit_length() - 1) if not (1 << b) & (bit_x | bit_y)]

    def swap_rest(value, done):
        bit = rest_bits[done]
        return lax.ppermute(value, "dp", [(i, i ^ (1 << bit)) for i in range(peers)])

    def halved(pairs, after=()):
        outs, scratch, big, which, count = [], [], [], [], 0
        for kept, came, axis, indices in pairs:
            half = kept.shape[axis] // 2
            shape = kept.shape[:axis] + ((half,) if half > 1 else ()) + kept.shape[axis + 1 :]
            outs += [(shape, bf16, True)] * 2
            scratch += [pltpu.VMEM(kept.shape, bf16)] * 2
            big += [kept, came]
            which += list(indices)
            count += 2 + 2 * half
        return kernel_call(
            functools.partial(halve_kernel, tuple(axis for _, _, axis, _ in pairs)),
            outs,
            big=tuple(big),
            scalars=scalars(*which),
            scratch=scratch,
            copies=count,
            after=after,
            name="halve",
        )

    def rest_part(kept, came, dim, done):
        mine = (position >> rest_bits[done]) & 1
        return kept, came, dim + len(rest_bits) - 1 - done, (1 - mine, mine)

    fours, rests = {}, {}
    for i in range(peers):
        fours.setdefault(i & ~(bit_x | bit_y), []).append(i)
        rests.setdefault(i & (bit_x | bit_y), []).append(i)
    fours, rests = list(fours.values()), list(rests.values())

    def exchanged(value, members):
        came = lax.all_to_all(value, "dp", 0, 0, axis_index_groups=members, tiled=True)
        return jnp.sum(came.astype(f32), axis=0)

    inputs = images.reshape(pixels, width)
    valid = validity(bucket_shape, pixel_mask).reshape(pixels, 1)
    norms = jnp.stack([mid_gains, mid_biases], axis=1)
    gain_row, bias_row = out_gain.reshape(1, width), out_bias.reshape(1, width)
    levels_flat = thresholds.reshape(pixels, width)
    cot = head_cotangent.transpose(0, 1, 3, 2, 4).reshape(2 * image_count * side, tasks, side, lanes)
    rows_half = image_count * side
    weights = head_weights.transpose(1, 0, 2)
    half_lanes = lanes // 2
    block = 4 * lane
    blocks = width // block

    pairs = []
    for i in range(peers):
        for c, bit in enumerate((bit_x, bit_y)):
            if not i & bit:
                pairs.append([2 * i + c, 2 * (i ^ bit) + c])
    pair_cot = lax.all_gather(cot, everyone, axis=0, tiled=True, axis_index_groups=pairs)

    mid = (pixels, middle)
    whole = (pixels, width)
    pair = (2, middle)
    stat_two, stat_three = (devices, 2, middle), (devices, 3, middle)

    def scalars(*values):
        return jnp.stack(values).astype(jnp.int32)

    def task_half(half, after):
        return kernel_call(
            task_kernel,
            [((tasks, pixels, width), bf16, True)],
            big=(cot, weights),
            scalars=scalars(half),
            scratch=[
                pltpu.VMEM((tasks, rows_half, side, lanes), bf16),
                pltpu.VMEM((2 * tasks, width // 2, lanes), bf16),
                pltpu.VMEM((2 * tasks, pixels, width // 2), bf16),
            ],
            copies=5 * tasks,
            after=after,
            name="task_grad",
        )[0]

    pre_reduce, stats = kernel_call(
        reduce_kernel,
        [(mid, f32, False), (stat_three, f32, False)],
        small=(valid,),
        big=(inputs, reduce_weight),
        scratch=[pltpu.VMEM(whole, bf16), pltpu.VMEM(reduce_weight.shape, bf16)],
        copies=8,
        after=(norms,),
        name="reduce",
    )
    table_one = from_everyone(stats)
    task_mine = task_half(core, (stats,))

    padded = (3, image_count, (side + 2) * side, middle)
    pre_spatial, consts_one, stats, acts = kernel_call(
        functools.partial(spatial_kernel, side),
        [(mid, f32, False), (pair, f32, False), (stat_two, f32, False), (padded, bf16, True)],
        small=(pre_reduce, table_one, norms[0], valid),
        big=(spatial_weight,),
        scratch=[pltpu.VMEM(spatial_weight.shape, bf16), pltpu.VMEM(padded, bf16)],
        copies=10,
        after=(task_mine,),
        name="spatial",
    )
    table_two = from_everyone(stats)
    task_sent = task_half(1 - core, (stats,))
    task_other = swap_core(held_until((table_two,), task_sent)[0])

    act_spatial, consts_two, stats, pre_expand = kernel_call(
        expand_kernel,
        [(mid, bf16, False), (pair, f32, False), ((devices, 2, width), f32, True), (whole, f32, True)],
        small=(pre_spatial, table_two, table_one, norms[1], valid),
        big=(expand_weight,),
        scratch=[
            pltpu.VMEM(expand_weight.shape, bf16),
            pltpu.VMEM(whole, f32),
            pltpu.VMEM((devices, 2, width), f32),
        ],
        copies=12,
        after=(task_sent,),
        name="expand",
    )
    table_three = from_everyone(stats)
    (merged,) = kernel_call(
        drop_kernel,
        [(whole, f32, True)],
        big=(task_mine, task_other, levels_flat),
        scratch=[
            pltpu.VMEM((tasks,) + whole, bf16),
            pltpu.VMEM((tasks,) + whole, bf16),
            pltpu.VMEM(whole, jnp.int32),
            pltpu.VMEM(whole, f32),
        ],
        copies=32,
        after=(stats,),
        name="graddrop",
    )


    pair_blocks = (2, pixels, width // 4)
    x_send, y_send = 2 * (1 - my_x), 1 - my_y
    consts_three, sums, features, same, cross, grad_residual = kernel_call(
        residual_kernel,
        [
            ((2, width), f32, False),
            ((devices, 2, width), f32, True),
            (whole, bf16, True),
            (pair_blocks, bf16, True),
            (pair_blocks, bf16, True),
            (whole, f32, True),
        ],
        scalars=scalars(
            by_core(x_send, y_send),
            by_core(x_send + 1, y_send + 2),
            by_core(y_send, x_send),
            by_core(y_send + 2, x_send + 1),
        ),
        small=(table_three, table_one, gain_row, bias_row, valid),
        big=(pre_expand, inputs, merged),
        scratch=[
            pltpu.VMEM(whole, f32),
            pltpu.VMEM(whole, bf16),
            pltpu.VMEM(whole, f32),
            pltpu.VMEM(whole, bf16),
            pltpu.VMEM((4, pixels, width // 4), bf16),
            pltpu.VMEM(whole, f32),
            pltpu.VMEM((devices, 2, width), f32),
        ],
        copies=28,
        name="residual",
    )
    table_four = from_everyone(sums)
    sibling = swap_core(features)
    far = swap_first(same)
    acts, act_spatial = held_until((features,), acts, act_spatial)
    acts_sib, act_spatial_sib = swap_core(acts), swap_core(act_spatial)

    def heads(first, count, after, fills):
        return kernel_call(
            functools.partial(heads_kernel, first),
            [(cot.shape, bf16, True)],
            big=(features, sibling, weights),
            scalars=scalars(core),
            scratch=[
                pltpu.VMEM(whole, bf16),
                pltpu.VMEM(whole, bf16),
                pltpu.VMEM((count, width, lanes), bf16),
                pltpu.VMEM((count, 2, rows_half, side, lanes), bf16),
            ],
            copies=2 + 6 * count,
            after=after,
            fills=fills,
            name="heads",
        )[0]


    part_shape = (tasks, 2, width // 4, lanes)

    def weight_part(near, cores, sources, cots, added, after):
        n = len(cores)
        return kernel_call(
            functools.partial(weights_kernel, near, cores),
            [(part_shape, bf16, True)],
            big=sources + (cots,) + added,
            scalars=scalars(
                core,
                by_core(my_x, 2 * my_y),
                by_core(my_x + 2, 2 * my_y + 1),
                1 - by_core(my_x, my_y),
            ),
            scratch=[
                pltpu.VMEM((2, n, pixels, width // 4), bf16),
                pltpu.VMEM((2, width // 4, n * pixels), bf16),
                pltpu.VMEM((tasks, n, rows_half, side, lanes), bf16),
                pltpu.VMEM(part_shape, bf16),
            ],
            copies=4 * blocks + 10 * tasks,
            after=after,
            name="heads_grad",
        )[0]

    index = by_core(my_y, my_x)
    near_part = weight_part(True, (0, 1), (features, sibling), cot, (), (sums, same))
    (cross,) = held_until((near_part,), cross)
    far_cross = swap_cross(cross)
    half_part = weight_part(False, (0,), (far,), pair_cot, (near_part,), (cross,))
    heads_part = weight_part(False, (1,), (far_cross,), pair_cot, (half_part,), ())
    (heads_part,) = held_until((table_four,), heads_part)
    heads_half = lax.psum_scatter(
        heads_part.reshape(tasks, width // 2, lanes),
        everyone,
        scatter_dimension=1,
        axis_index_groups=twos,
        tiled=True,
    )

    expand_half, spatial_half = (pixels, width // 2), (pixels, middle // 2)
    out_totals, shifted_two, sums, expand_mine, expand_sent = kernel_call(
        expand_back_kernel,
        [
            ((2, width), f32, False),
            (mid, f32, False),
            (stat_two, f32, False),
            (expand_half, bf16, True),
            (expand_half, bf16, True),
        ],
        scalars=scalars(core),
        small=(consts_three, table_four, gain_row, valid, table_one, pre_spatial, consts_two, norms[1]),
        big=(grad_residual, pre_expand, expand_weight),
        scratch=[
            pltpu.VMEM(whole, f32),
            pltpu.VMEM(whole, f32),
            pltpu.VMEM(expand_weight.shape, bf16),
            pltpu.VMEM(whole, bf16),
        ],
        copies=14,
        after=(heads_part,),
        name="expand_back",
    )
    table_five = from_everyone(sums)
    expand_sib = swap_core(expand_sent)
    totals_two, shifted_one, sums, spatial_mine, spatial_sent = kernel_call(
        functools.partial(spatial_back_kernel, side),
        [
            (pair, f32, False),
            (mid, f32, False),
            (stat_two, f32, False),
            (spatial_half, bf16, True),
            (spatial_half, bf16, True),
        ],
        scalars=scalars(core),
        small=(
            shifted_two, pre_spatial, consts_two, table_five, norms[1], valid, table_one,
            pre_reduce, consts_one, norms[0],
        ),
        big=(spatial_weight,),
        scratch=[
            pltpu.VMEM(spatial_weight.shape, bf16),
            pltpu.VMEM(padded, bf16),
            pltpu.VMEM(mid, bf16),
        ],
        copies=11,
        name="spatial_back",
    )
    table_six = from_everyone(sums)
    spatial_sib = swap_core(spatial_sent)
    x_out, y_out, x_in, y_in = 1 - my_x, 2 * (1 - my_y), my_x, 2 * my_y
    pair_parts = (
        by_core(x_out, y_out),
        by_core(x_out + 2, y_out + 1),
        by_core(x_in, y_in),
        by_core(x_in + 2, y_in + 1),
    )
    high, rows_of_pair = peers >> (low + 2), (1 << low) * (middle // peers)
    early_shape = (2, blocks + 9, high, rows_of_pair, middle // 2)
    early_sent, early_kept = kernel_call(
        functools.partial(trunk_weights_kernel, side),
        [(early_shape, bf16, True), (early_shape, bf16, True)],
        scalars=scalars(*pair_parts),
        small=(act_spatial, act_spatial_sib, spatial_mine, spatial_sib),
        big=(acts, acts_sib, expand_mine, expand_sib),
        scratch=[
            pltpu.VMEM((2,) + padded, bf16),
            pltpu.VMEM((2,) + expand_half, bf16),
            pltpu.VMEM((blocks + 9, high, 4, rows_of_pair, middle // 2), bf16),
        ],
        copies=4 + 4 * (blocks + 9),
        after=(sums,),
        name="trunk_weights",
    )
    (early_sent,) = held_until((table_six,), early_sent)
    early_came = swap_first(early_sent)
    dp_rows = (peers, width // devices, middle)
    totals_one, images_grad, reduce_sent, reduce_kept = kernel_call(
        reduce_back_kernel,
        [(pair, f32, False), (whole, f32, True), (dp_rows, bf16, True), (dp_rows, bf16, True)],
        scalars=scalars(core),
        small=(shifted_one, pre_reduce, consts_one, table_six, norms[0], valid, table_one),
        big=(reduce_weight, grad_residual, inputs),
        scratch=[
            pltpu.VMEM(mid, bf16),
            pltpu.VMEM(reduce_weight.shape, bf16),
            pltpu.VMEM(whole, f32),
            pltpu.VMEM(whole, bf16),
            pltpu.VMEM((peers, 2, width // devices, middle), bf16),
        ],
        copies=24,
        after=(early_kept,),
        name="reduce_back",
    )
    reduce_came = swap_core(reduce_sent)
    (heads_half,) = held_until((reduce_kept,), heads_half)
    heads_grad = lax.psum_scatter(
        heads_half, "dp", scatter_dimension=1, axis_index_groups=rests, tiled=True
    )
    heads_grad = heads_grad.astype(f32)
    quarters = (high, 4, (1 << low) * dp_rows[1], middle)
    reduce_sent, reduce_kept = halved(
        [(reduce_kept.reshape(quarters), reduce_came.reshape(quarters), 1, pair_parts)]
    )
    reduce_came = swap_first(reduce_sent)
    head_values = heads(0, 2, (reduce_kept,), False)
    early_sent, early_kept, reduce_sent, reduce_kept = halved(
        [
            (early_kept, early_came, 0, (1 - index, index)),
            (reduce_kept, reduce_came, 1, (1 - index, index)),
        ],
        (head_values,),
    )
    early_came, reduce_came = swap_second(early_sent), swap_second(reduce_sent)
    head_values = heads(2, tasks - 2, (head_values, reduce_kept), True)
    head_output = head_values.reshape(2 * image_count, side, tasks, side, lanes).transpose(0, 1, 3, 2, 4)
    early = (early_kept.astype(f32) + early_came.astype(f32)).astype(bf16)
    early = early.reshape(blocks + 9, peers // 4, -1, middle // 2).transpose(1, 0, 2, 3)
    late = (reduce_kept.astype(f32) + reduce_came.astype(f32)).astype(bf16)
    both = jnp.concatenate(
        [early.reshape(peers // 4, -1, middle // 2), late.reshape(peers // 4, -1, middle // 2)], axis=1
    )
    came = lax.all_to_all(both, "dp", 0, 0, axis_index_groups=rests, tiled=True)
    (came,) = held_until((head_values, heads_grad), came)
    both = jnp.sum(came.astype(f32), axis=0)
    heads_grad = heads_grad.transpose(1, 0, 2)
    split = (blocks + 9) * (middle // peers)
    early = both[:split].reshape(blocks + 9, -1, middle // 2)
    reduce_grad = both[split:].reshape(-1, middle)

    own_rows = early.reshape(early.shape[0], 2, -1, early.shape[2])
    came_rows = swap_core(pick(own_rows, 1, 1 - core))
    own_rows = pick(own_rows, 1, core)
    halves = jnp.stack(
        [jnp.where(core == 0, own_rows, came_rows), jnp.where(core == 0, came_rows, own_rows)]
    ).astype(f32)
    expand_grad = halves[:, :blocks].transpose(2, 0, 1, 3).reshape(middle // devices, width)
    spatial_grad = halves[:, blocks:].transpose(1, 2, 0, 3).reshape(9, middle // devices, middle)
    gains_grad = jnp.stack([totals_one[1], totals_two[1]], axis=0)
    biases_grad = jnp.stack([totals_one[0], totals_two[0]], axis=0)
    return (
        head_output,
        images_grad.reshape(images.shape),
        reduce_grad,
        spatial_grad,
        expand_grad,
        gains_grad,
        biases_grad,
        out_totals[1],
        out_totals[0],
        heads_grad,
    )


def solution(mesh):
    placed = (
        P(("dp", "task"), None, None, None),
        P(("dp", "task"), None),
        P(("dp", "task"), None, None),
        P(("dp", "task"), None, None, None),
        P(),
        P(),
        P(),
        P(),
        P(),
        P(),
        P(),
        P(None, None, "task"),
        P("dp", None, None, None, "task"),
    )
    return jax.shard_map(
        on_device,
        mesh=mesh,
        in_specs=placed,
        out_specs=(
            P("dp", None, None, None, "task"),
            P(("dp", "task"), None, None, None),
            P(("dp", "task"), None),
            P(None, ("dp", "task"), None),
            P(("dp", "task"), None),
            P(),
            P(),
            P(),
            P(),
            P("dp", None, "task"),
        ),
        check_vma=False,
    )
```

```python
import functools

import jax
import jax.numpy as jnp
from jax import lax
from jax.experimental import pallas as pl
from jax.experimental.pallas import tpu as pltpu
from jax.sharding import PartitionSpec as P

epsilon = 1e-05
steepness = 6.0
levels = 4096.0
everyone = ("dp", "task")
f32 = jnp.float32
bf16 = jnp.bfloat16
lane = 128
MIB = 1 << 20


def dot(left, right, contract):
    return lax.dot_general(
        left, right, ((contract[0:1], contract[1:2]), ((), ())), preferred_element_type=f32
    )


def kernel_call(body, outs, small=(), big=(), scalars=None, scratch=(), copies=0, after=(), fills=False, name=None):
    skipped = len(after)

    def ordered(*refs):
        body(*refs[skipped:])

    big = [pltpu.with_memory_space_constraint(array, pltpu.HBM) for array in big]
    there = pl.BlockSpec(memory_space=pl.ANY)
    here = pl.BlockSpec(memory_space=pltpu.VMEM)
    given = [] if scalars is None else [scalars]
    return pl.pallas_call(
        ordered,
        in_specs=[there] * skipped
        + [pl.BlockSpec(memory_space=pltpu.SMEM)] * len(given)
        + [here] * len(small)
        + [there] * len(big),
        out_specs=[there if streamed else here for _, _, streamed in outs],
        out_shape=[
            pltpu.HBM(shape, dtype) if streamed else jax.ShapeDtypeStruct(shape, dtype)
            for shape, dtype, streamed in outs
        ],
        scratch_shapes=list(scratch) + ([pltpu.SemaphoreType.DMA((copies,))] if copies else []),
        input_output_aliases={0: 0} if fills else {},
        compiler_params=pltpu.CompilerParams(vmem_limit_bytes=48 * MIB),
        name=name,
    )(*after, *given, *small, *big)


def held_until(after, *values):
    def body(*refs):
        pass

    there = pl.BlockSpec(memory_space=pl.ANY)
    return pl.pallas_call(
        body,
        in_specs=[there] * (len(values) + len(after)),
        out_specs=[there] * len(values),
        out_shape=[jax.ShapeDtypeStruct(v.shape, v.dtype) for v in values],
        input_output_aliases={i: i for i in range(len(values))},
        name="held",
    )(*values, *after)


class Copies:
    def __init__(self, sems):
        self.sems = sems
        self.used = 0
        self.open = []

    def start(self, source, target):
        copy = pltpu.make_async_copy(source, target, self.sems.at[self.used])
        self.used += 1
        copy.start()
        return copy

    def out(self, source, target):
        self.open.append(self.start(source, target))

    def finish(self):
        for copy in self.open:
            copy.wait()


def columns(ref, index, size):
    return ref.at[:, index * size : (index + 1) * size]


def sigmoid(value):
    return 0.5 + 0.5 * jnp.tanh(0.5 * value)


def combined(table, counts):
    counts = counts[:, 0:1]
    total = jnp.sum(counts)
    center = jnp.sum(table[:, 0, :], axis=0, keepdims=True) / total
    shift = table[:, 0, :] / jnp.maximum(counts, 1.0) - center
    variance = (
        jnp.sum(table[:, 1, :] + counts * shift * shift, axis=0, keepdims=True) / total
    )
    return center, lax.rsqrt(variance + epsilon)


def store_rows(stats_ref, rows, at=slice(None)):
    table = jnp.concatenate(rows, axis=0)
    stats_ref[:, :, at] = jnp.broadcast_to(table[None], (stats_ref.shape[0],) + table.shape)


def store_moments(stats_ref, values_ref, valid_ref, at=slice(None)):
    valid, values = valid_ref[...], values_ref[...]
    count = jnp.sum(valid)
    first = jnp.sum(values * valid, axis=0, keepdims=True)
    deviation = (values - first / jnp.maximum(count, 1.0)) * valid
    rows = [first, jnp.sum(deviation * deviation, axis=0, keepdims=True)]
    if stats_ref.shape[1] > 2:
        rows.append(jnp.broadcast_to(count, first.shape))
    store_rows(stats_ref, rows, at)


def store_sums(stats_ref, grad, normed, at=slice(None)):
    rows = [jnp.sum(grad, axis=0, keepdims=True), jnp.sum(grad * normed, axis=0, keepdims=True)]
    store_rows(stats_ref, rows, at)


def reduce_kernel(valid_ref, x_ref, w_ref, out_ref, stats_ref, x_buf, w_buf, sems):
    copies = Copies(sems)
    parts = 4
    size = x_ref.shape[1] // parts
    arriving = []
    for k in range(parts):
        arriving.append(
            (
                copies.start(columns(x_ref, k, size), columns(x_buf, k, size)),
                copies.start(w_ref.at[k * size : (k + 1) * size], w_buf.at[k * size : (k + 1) * size]),
            )
        )
    total = None
    for k, pair in enumerate(arriving):
        for copy in pair:
            copy.wait()
        part = dot(x_buf[:, k * size : (k + 1) * size], w_buf[k * size : (k + 1) * size, :], (1, 0))
        total = part if total is None else total + part
    out_ref[...] = total * valid_ref[...]
    store_moments(stats_ref, out_ref, valid_ref)


def pad_edges(acts_ref, side):
    images = acts_ref.shape[1]
    zeros = jnp.zeros((side, acts_ref.shape[3]), bf16)
    for shift in range(3):
        for image in range(images):
            acts_ref[shift, image, 0:side, :] = zeros
            acts_ref[shift, image, (side + 1) * side : (side + 2) * side, :] = zeros


def store_shifted(acts_ref, values, side):
    pixels = values.shape[0]
    column = lax.broadcasted_iota(jnp.int32, (pixels, 1), 0) % side
    before = jnp.where(column == 0, 0.0, pltpu.roll(values, 1, 0))
    after = jnp.where(column == side - 1, 0.0, pltpu.roll(values, pixels - 1, 0))
    for shift, moved in enumerate((before, values, after)):
        for image in range(acts_ref.shape[1]):
            rows = slice(image * side * side, (image + 1) * side * side)
            acts_ref[shift, image, side : side + side * side, :] = moved[rows].astype(bf16)


def window(acts_ref, row_shift, col_shift, side):
    images = acts_ref.shape[1]
    tile = acts_ref[col_shift, :, row_shift * side : row_shift * side + side * side, :]
    return tile.reshape(images * side * side, acts_ref.shape[3])


def spatial_kernel(
    side, pre_ref, table_ref, norm_ref, valid_ref, w_ref, out_ref, consts_ref, stats_ref, acts_out, w_buf, acts_ref, sems
):
    copies = Copies(sems)
    arriving = [copies.start(w_ref.at[k], w_buf.at[k]) for k in range(9)]
    center, inverse = combined(table_ref, table_ref[:, 2, :])
    consts_ref[0:1, :] = center
    consts_ref[1:2, :] = inverse
    gain, bias = norm_ref[0:1, :], norm_ref[1:2, :]
    pad_edges(acts_ref, side)

    shifted = gain * ((pre_ref[...] - center) * inverse) + bias
    store_shifted(acts_ref, valid_ref[...] * shifted * sigmoid(shifted), side)
    copies.out(acts_ref, acts_out)
    total = None
    for tap in range(9):
        arriving[tap].wait()
        part = dot(window(acts_ref, tap // 3, tap % 3, side), w_buf[tap], (1, 0))
        total = part if total is None else total + part
    out_ref[...] = total
    store_moments(stats_ref, out_ref, valid_ref)
    copies.finish()


def expand_kernel(
    pre_ref, table_ref, first_ref, norm_ref, valid_ref, w_ref, act_ref, consts_ref, stats_out, out,
    w_buf, out_buf, stats_ref, sems,
):
    copies = Copies(sems)
    parts = 4
    size = w_ref.shape[1] // parts
    arriving = [copies.start(columns(w_ref, k, size), columns(w_buf, k, size)) for k in range(parts)]
    center, inverse = combined(table_ref, first_ref[:, 2, :])
    consts_ref[0:1, :] = center
    consts_ref[1:2, :] = inverse
    gain, bias = norm_ref[0:1, :], norm_ref[1:2, :]

    shifted = gain * ((pre_ref[...] - center) * inverse) + bias
    act_ref[...] = (valid_ref[...] * shifted * sigmoid(shifted)).astype(bf16)
    for k in range(parts):
        at = slice(k * size, (k + 1) * size)
        arriving[k].wait()
        out_buf[:, at] = dot(act_ref[...], w_buf[:, at], (1, 0))
        copies.out(columns(out_buf, k, size), columns(out, k, size))
        store_moments(stats_ref, columns(out_buf, k, size), valid_ref, at)
        copies.out(stats_ref.at[:, :, at], stats_out.at[:, :, at])
    copies.finish()


def residual_kernel(
    which_ref, table_ref, first_ref, gain_ref, bias_ref, valid_ref, pre_ref, x_ref, merged_ref,
    consts_ref, sums_out, feat_out, same_out, cross_out, grad_out,
    pre_buf, x_buf, merged_buf, feat_buf, block_buf, grad_buf, sums_ref, sems,
):
    copies = Copies(sems)
    parts = 4
    size = pre_ref.shape[1] // parts
    arriving = []
    for k in range(parts):
        arriving.append(
            [
                copies.start(columns(ref, k, size), columns(buf, k, size))
                for ref, buf in ((pre_ref, pre_buf), (x_ref, x_buf), (merged_ref, merged_buf))
            ]
        )
    for k in range(parts):
        at = slice(k * size, (k + 1) * size)
        center, inverse = combined(table_ref[:, :, at], first_ref[:, 2, :])
        consts_ref[0:1, at] = center
        consts_ref[1:2, at] = inverse
        gain, bias = gain_ref[:, at], bias_ref[:, at]
        for copy in arriving[k]:
            copy.wait()

        valid = valid_ref[...]
        normed = (pre_buf[:, at] - center) * inverse
        value = x_buf[:, at].astype(f32) + gain * normed + bias
        sigma = sigmoid(value)
        features = (valid * (value * sigma)).astype(bf16)
        feat_buf[:, at] = features
        for piece in range(4):
            block_buf[2 * (piece % 2) + piece // 2, :, k * lane : (k + 1) * lane] = features[
                :, piece * lane : (piece + 1) * lane
            ]
        grad = merged_buf[:, at] * valid * (sigma * (1.0 + value * (1.0 - sigma)))
        grad_buf[:, at] = grad
        store_sums(sums_ref, grad, normed, at)
        copies.out(sums_ref.at[:, :, at], sums_out.at[:, :, at])
        copies.out(columns(grad_buf, k, size), columns(grad_out, k, size))
        copies.out(columns(feat_buf, k, size), columns(feat_out, k, size))
    for j in range(2):
        copies.out(block_buf.at[which_ref[j]], same_out.at[j])
        copies.out(block_buf.at[which_ref[2 + j]], cross_out.at[j])
    copies.finish()


def slope_rows(grad, pre_ref, consts_ref, norm_ref, valid_ref, out_ref, sums_ref):
    center, inverse = consts_ref[0:1, :], consts_ref[1:2, :]
    gain, bias = norm_ref[0:1, :], norm_ref[1:2, :]
    normed = (pre_ref[...] - center) * inverse
    value = gain * normed + bias
    sigma = sigmoid(value)
    grad = grad * valid_ref[...] * (sigma * (1.0 + value * (1.0 - sigma)))
    out_ref[...] = grad
    store_sums(sums_ref, grad, normed)


def expand_back_kernel(
    which_ref, consts_ref, table_ref, gain_ref, valid_ref, first_ref, mid_pre_ref, mid_consts_ref, mid_norm_ref,
    grad_ref, pre_ref, w_ref,
    totals_ref, shifted_ref, sums_ref, mine_out, sent_out,
    grad_buf, pre_buf, w_buf, out_buf, sems,
):
    copies = Copies(sems)
    parts = 4
    size = pre_ref.shape[1] // parts
    arriving = []
    for k in range(parts):
        arriving.append(
            [
                copies.start(columns(ref, k, size), columns(buf, k, size))
                for ref, buf in ((grad_ref, grad_buf), (pre_ref, pre_buf), (w_ref, w_buf))
            ]
        )
    count = jnp.sum(first_ref[:, 2, 0:1])
    total = None
    for k in range(parts):
        at = slice(k * size, (k + 1) * size)
        totals = jnp.sum(table_ref[:, :, at], axis=0)
        totals_ref[:, at] = totals
        center, inverse = consts_ref[0:1, at], consts_ref[1:2, at]
        plain, scaled = totals[0:1, :] / count, totals[1:2, :] / count
        scale = gain_ref[:, at] * inverse
        for copy in arriving[k]:
            copy.wait()

        normed = (pre_buf[:, at] - center) * inverse
        grad = scale * (grad_buf[:, at] - valid_ref[...] * (plain + normed * scaled))
        out_buf[:, at] = grad.astype(bf16)
        part = dot(out_buf[:, at], w_buf[:, at], (1, 1))
        total = part if total is None else total + part
    half = out_buf.shape[1] // 2
    for place, out in ((which_ref[0], mine_out), (1 - which_ref[0], sent_out)):
        copies.out(out_buf.at[:, pl.ds(pl.multiple_of(place * half, half), half)], out)
    slope_rows(total, mid_pre_ref, mid_consts_ref, mid_norm_ref, valid_ref, shifted_ref, sums_ref)
    copies.finish()


def spatial_back_kernel(
    side, which_ref, grad_ref, pre_ref, consts_ref, table_ref, norm_ref, valid_ref, first_ref,
    low_pre_ref, low_consts_ref, low_norm_ref, w_ref,
    totals_ref, shifted_ref, sums_ref, mine_out, sent_out,
    w_buf, acts_ref, out_ref, sems,
):
    copies = Copies(sems)
    arriving = [copies.start(w_ref.at[k], w_buf.at[k]) for k in range(9)]
    count = jnp.sum(first_ref[:, 2, 0:1])
    totals = jnp.sum(table_ref[...], axis=0)
    totals_ref[...] = totals
    center, inverse = consts_ref[0:1, :], consts_ref[1:2, :]
    plain, scaled = totals[0:1, :] / count, totals[1:2, :] / count
    scale = norm_ref[0:1, :] * inverse
    pad_edges(acts_ref, side)

    normed = (pre_ref[...] - center) * inverse
    grad = scale * (grad_ref[...] - valid_ref[...] * (plain + normed * scaled))
    out_ref[...] = grad.astype(bf16)
    half = out_ref.shape[1] // 2
    for place, out in ((which_ref[0], mine_out), (1 - which_ref[0], sent_out)):
        copies.out(out_ref.at[:, pl.ds(pl.multiple_of(place * half, half), half)], out)
    store_shifted(acts_ref, grad, side)
    total = None
    for tap in range(9):
        arriving[tap].wait()
        part = dot(window(acts_ref, 2 - tap // 3, 2 - tap % 3, side), w_buf[tap], (1, 1))
        total = part if total is None else total + part
    slope_rows(total, low_pre_ref, low_consts_ref, low_norm_ref, valid_ref, shifted_ref, sums_ref)
    copies.finish()


def reduce_back_kernel(
    which_ref, grad_ref, pre_ref, consts_ref, table_ref, norm_ref, valid_ref, first_ref, w_ref, res_ref, x_ref,
    totals_ref, images_out, sent_out, kept_out,
    low_buf, w_buf, res_buf, x_buf, part_buf, sems,
):
    copies = Copies(sems)
    parts = 4
    size = res_ref.shape[1] // parts
    arriving = []
    for k in range(parts):
        at = slice(k * size, (k + 1) * size)
        arriving.append(
            [
                copies.start(columns(x_ref, k, size), columns(x_buf, k, size)),
                copies.start(w_ref.at[at], w_buf.at[at]),
                copies.start(columns(res_ref, k, size), columns(res_buf, k, size)),
            ]
        )
    count = jnp.sum(first_ref[:, 2, 0:1])
    totals = jnp.sum(table_ref[...], axis=0)
    totals_ref[...] = totals
    center, inverse = consts_ref[0:1, :], consts_ref[1:2, :]
    plain, scaled = totals[0:1, :] / count, totals[1:2, :] / count
    scale = norm_ref[0:1, :] * inverse

    normed = (pre_ref[...] - center) * inverse
    grad = scale * (grad_ref[...] - valid_ref[...] * (plain + normed * scaled))
    low_buf[...] = grad.astype(bf16)
    for k in range(parts):
        at = slice(k * size, (k + 1) * size)
        arriving[k][0].wait()
        value = dot(x_buf[:, at], low_buf[...], (0, 0)).astype(bf16)
        peers = part_buf.shape[0] // parts
        dp = slice(k * peers, (k + 1) * peers)
        part_buf[dp] = value.reshape((peers,) + part_buf.shape[1:])
        copies.out(part_buf.at[dp, 1 - which_ref[0]], sent_out.at[dp])
        copies.out(part_buf.at[dp, which_ref[0]], kept_out.at[dp])
    for k in range(parts):
        at = slice(k * size, (k + 1) * size)
        arriving[k][1].wait()
        arriving[k][2].wait()
        res_buf[:, at] = res_buf[:, at] + valid_ref[...] * dot(low_buf[...], w_buf[at, :], (1, 1))
        copies.out(columns(res_buf, k, size), columns(images_out, k, size))
    copies.finish()


def trunk_weights_kernel(
    side, which_ref, act_ref, act_sib, right_ref, right_sib, acts_ref, acts_sib, grad_ref, grad_sib,
    sent_out, kept_out, acts_buf, grad_buf, out_buf, sems,
):
    copies = Copies(sems)
    size = right_ref.shape[1]
    blocks = grad_ref.shape[1] // size
    grads = [copies.start(ref, grad_buf.at[c]) for c, ref in enumerate((grad_ref, grad_sib))]
    acts = [copies.start(ref, acts_buf.at[c]) for c, ref in enumerate((acts_ref, acts_sib))]

    def store(place, value):
        out_buf[place] = value.astype(bf16).reshape(out_buf.shape[1:])
        for q in range(2):
            copies.out(out_buf.at[place, :, which_ref[q]], sent_out.at[q, place])
            copies.out(out_buf.at[place, :, which_ref[2 + q]], kept_out.at[q, place])

    for copy in grads:
        copy.wait()
    for b in range(blocks):
        at = slice(b * size, (b + 1) * size)
        store(b, dot(act_ref[...], grad_buf[0, :, at], (0, 0)) + dot(act_sib[...], grad_buf[1, :, at], (0, 0)))
    for copy in acts:
        copy.wait()
    for tap in range(9):
        tiles = [window(acts_buf.at[c], tap // 3, tap % 3, side) for c in range(2)]
        store(blocks + tap, dot(tiles[0], right_ref[...], (0, 0)) + dot(tiles[1], right_sib[...], (0, 0)))
    copies.finish()


def halve_kernel(axes, which_ref, *refs):
    n = len(axes)
    ins, outs, bufs, sems = refs[: 2 * n], refs[2 * n : 4 * n], refs[4 * n : 6 * n], refs[6 * n]
    copies = Copies(sems)
    arriving = [copies.start(ref, buf) for ref, buf in zip(ins, bufs)]
    first = 0
    for p, axis in enumerate(axes):
        kept_buf, came_buf = bufs[2 * p : 2 * p + 2]
        arriving[2 * p].wait()
        arriving[2 * p + 1].wait()
        kept_buf[...] = (kept_buf[...].astype(f32) + came_buf[...].astype(f32)).astype(bf16)
        count = kept_buf.shape[axis] // 2
        lead = (slice(None),) * axis
        for out in outs[2 * p : 2 * p + 2]:
            for i in range(count):
                target = lead + ((i,) if count > 1 else ())
                copies.out(kept_buf.at[lead + (which_ref[first],)], out.at[target] if target else out)
                first = first + 1
    copies.finish()


def task_kernel(half_ref, cot_ref, w_ref, out, cot_buf, w_buf, out_buf, sems):
    copies = Copies(sems)
    tasks, pixels = out.shape[:2]
    size = w_buf.shape[1]
    parts = w_ref.shape[1] // size
    rows = cot_buf.shape[1]
    start = pl.multiple_of(half_ref[0] * rows, rows)
    cots, arriving = [], []
    for t in range(tasks):
        cots.append(copies.start(cot_ref.at[pl.ds(start, rows), t], cot_buf.at[t]))
        for j in range(parts):
            arriving.append(copies.start(w_ref.at[t, j * size : (j + 1) * size], w_buf.at[t * parts + j]))
    for t in range(tasks):
        cots[t].wait()
        for j in range(parts):
            slot = t * parts + j
            arriving[slot].wait()
            cot = cot_buf[t].reshape(pixels, cot_buf.shape[3])
            out_buf[slot] = dot(cot, w_buf[slot], (1, 1)).astype(bf16)
            copies.out(out_buf.at[slot], out.at[t, :, j * size : (j + 1) * size])
    copies.finish()


def drop_kernel(mine_ref, other_ref, level_ref, out, mine_buf, other_buf, level_buf, out_buf, sems):
    copies = Copies(sems)
    tasks, pixels, _ = mine_ref.shape
    parts = 8
    size = pixels // parts
    arriving = []
    for k in range(parts):
        at = slice(k * size, (k + 1) * size)
        arriving.append(
            [
                copies.start(mine_ref.at[:, at], mine_buf.at[:, at]),
                copies.start(other_ref.at[:, at], other_buf.at[:, at]),
                copies.start(level_ref.at[at], level_buf.at[at]),
            ]
        )
    for k in range(parts):
        for copy in arriving[k]:
            copy.wait()

        rows = slice(k * size, (k + 1) * size)
        grads = [mine_buf[t, rows].astype(f32) + other_buf[t, rows].astype(f32) for t in range(tasks)]
        total, spread = None, None
        for grad in grads:
            squared = grad * grad + 1.0
            root = squared * lax.rsqrt(squared)
            spread = root if spread is None else spread + root
            total = grad if total is None else total + grad
        margin = (0.25 * steepness) * (total / spread) + (
            0.25 * steepness * (1.0 - 1.0 / levels)
            - level_buf[rows].astype(f32) * (0.5 * steepness / levels)
        )
        merged = total
        for grad in grads:
            merged = merged + grad * jnp.tanh(jnp.tanh(grad) * margin)
        out_buf[rows] = 0.5 * merged
        at = slice(k * size, (k + 1) * size)
        copies.out(out_buf.at[at], out.at[at])
    copies.finish()


def heads_kernel(first, which_ref, own_ref, sib_ref, w_ref, out, own_buf, sib_buf, w_buf, out_buf, sems):
    copies = Copies(sems)
    core = which_ref[0]
    tasks = w_buf.shape[0]
    lanes = w_ref.shape[2]
    size = lanes // 2
    rows = out.shape[0] // 2
    arriving = []
    features = []
    for t in range(tasks):
        for j in range(2):
            at = slice(j * size, (j + 1) * size)
            arriving.append(copies.start(w_ref.at[first + t, :, at], w_buf.at[t, :, at]))
            if not features:
                features = [copies.start(own_ref, own_buf), copies.start(sib_ref, sib_buf)]
    for t in range(tasks):
        for j in range(2):
            at = slice(j * size, (j + 1) * size)
            arriving[2 * t + j].wait()
            for s, (source, place) in enumerate(((own_buf, core), (sib_buf, 1 - core))):
                if t + j == 0:
                    features[s].wait()
                value = dot(source[...], w_buf[t, :, at], (1, 0)).astype(bf16)
                out_buf[t, s, :, :, at] = value.reshape(rows, out.shape[2], size)
                copies.out(
                    out_buf.at[t, s, :, :, at],
                    out.at[pl.ds(pl.multiple_of(place * rows, rows), rows), first + t, :, at],
                )
    copies.finish()


def weights_kernel(near, cores, which_ref, *refs):
    sources, cot_ref, refs = refs[: len(cores)], refs[len(cores)], refs[len(cores) + 1 :]
    added_ref, refs = (None, refs) if near else (refs[0], refs[1:])
    out, feat_buf, flip_buf, cot_buf, out_buf, sems = refs
    copies = Copies(sems)
    core = which_ref[0]
    tasks = out.shape[0]
    pixels, channels = feat_buf.shape[2:]
    pieces = channels // lane
    lanes = cot_buf.shape[4]
    rows = cot_buf.shape[2]
    features = []
    for j in range(2):
        for s, ref in enumerate(sources):
            if near:
                features.append(
                    [
                        copies.start(
                            ref.at[:, pl.ds(pl.multiple_of((4 * piece + which_ref[1 + j]) * lane, lane), lane)],
                            feat_buf.at[j, s, :, piece * lane : (piece + 1) * lane],
                        )
                        for piece in range(pieces)
                    ]
                )
            else:
                features.append([copies.start(ref.at[j], feat_buf.at[j, s])])
    start = 0 if near else which_ref[3] * (2 * rows)
    cots, more = [], []
    for t in range(tasks):
        cots.append(
            [
                copies.start(
                    cot_ref.at[pl.ds(pl.multiple_of(start + place * rows, rows), rows), t], cot_buf.at[t, s]
                )
                for s, place in enumerate([core if c == 0 else 1 - core for c in cores])
            ]
        )
        if not near:
            more.append([copies.start(added_ref.at[t, j], out_buf.at[t, j]) for j in range(2)])
    for t in range(tasks):
        for j in range(2):
            if t == 0:
                for s in range(len(cores)):
                    for copy in features[len(cores) * j + s]:
                        copy.wait()
                    flip_buf[j, :, s * pixels : (s + 1) * pixels] = feat_buf[j, s].T
            if j == 0:
                for copy in cots[t]:
                    copy.wait()
            value = dot(flip_buf[j], cot_buf[t].reshape(len(cores) * pixels, lanes), (1, 0))
            if not near:
                more[t][j].wait()
                value = value + out_buf[t, j].astype(f32)
            out_buf[t, j] = value.astype(bf16)
            copies.out(out_buf.at[t, j], out.at[t, j])
    copies.finish()


def validity(bucket_shape, pixel_mask):
    row_index = lax.broadcasted_iota(jnp.int32, pixel_mask.shape, 1)
    col_index = lax.broadcasted_iota(jnp.int32, pixel_mask.shape, 2)
    inside = (row_index < bucket_shape[:, 0][:, None, None]) & (
        col_index < bucket_shape[:, 1][:, None, None]
    )
    return jnp.where(inside, pixel_mask, 0).astype(f32)


def from_everyone(rows):
    return lax.all_to_all(rows, everyone, 0, 0, tiled=True)


def swap_core(value):
    return lax.ppermute(value, "task", [(0, 1), (1, 0)])


def pick(value, axis, index):
    return lax.dynamic_index_in_dim(value, index, axis, keepdims=False)


def two(value, axis, first, second):
    return jnp.stack([pick(value, axis, first), pick(value, axis, second)], axis)


def on_device(
    images,
    bucket_shape,
    pixel_mask,
    thresholds,
    reduce_weight,
    spatial_weight,
    expand_weight,
    mid_gains,
    mid_biases,
    out_gain,
    out_bias,
    head_weights,
    head_cotangent,
):
    image_count = images.shape[0]
    side = images.shape[1]
    width = images.shape[3]
    middle = reduce_weight.shape[1]
    tasks = head_weights.shape[1]
    lanes = head_weights.shape[2]
    pixels = image_count * side * side
    peers = lax.axis_size("dp")
    devices = 2 * peers
    core = lax.axis_index("task")
    low = max(0, (lane * peers // width).bit_length() - 1)
    bit_x, bit_y = 1 << low, 2 << low
    position = lax.axis_index("dp")
    my_x, my_y = (position >> low) & 1, (position >> (low + 1)) & 1
    def pairing(bit_of, cross):
        pairs = []
        for i in range(peers):
            for c in range(2):
                if cross:
                    pairs.append((2 * i + c, 2 * (i ^ bit_of[1 - c]) + 1 - c))
                else:
                    pairs.append((2 * i + c, 2 * (i ^ bit_of[c]) + c))
        return pairs

    def swap_first(value):
        return lax.ppermute(value, everyone, pairing((bit_x, bit_y), False))

    def swap_second(value):
        return lax.ppermute(value, everyone, pairing((bit_y, bit_x), False))

    def swap_cross(value):
        return lax.ppermute(value, everyone, pairing((bit_x, bit_y), True))

    def by_core(zero, one):
        return jnp.where(core == 0, zero, one)

    twos = []
    for i in range(peers):
        for c, bit in enumerate((bit_y, bit_x)):
            if not i & bit:
                twos.append([2 * i + c, 2 * (i | bit) + c])
    rest_bits = [b for b in range(peers.bit_length() - 1) if not (1 << b) & (bit_x | bit_y)]

    def swap_rest(value, done):
        bit = rest_bits[done]
        return lax.ppermute(value, "dp", [(i, i ^ (1 << bit)) for i in range(peers)])

    def halved(pairs, after=()):
        outs, scratch, big, which, count = [], [], [], [], 0
        for kept, came, axis, indices in pairs:
            half = kept.shape[axis] // 2
            shape = kept.shape[:axis] + ((half,) if half > 1 else ()) + kept.shape[axis + 1 :]
            outs += [(shape, bf16, True)] * 2
            scratch += [pltpu.VMEM(kept.shape, bf16)] * 2
            big += [kept, came]
            which += list(indices)
            count += 2 + 2 * half
        return kernel_call(
            functools.partial(halve_kernel, tuple(axis for _, _, axis, _ in pairs)),
            outs,
            big=tuple(big),
            scalars=scalars(*which),
            scratch=scratch,
            copies=count,
            after=after,
            name="halve",
        )

    def rest_part(kept, came, dim, done):
        mine = (position >> rest_bits[done]) & 1
        return kept, came, dim + len(rest_bits) - 1 - done, (1 - mine, mine)

    fours, rests = {}, {}
    for i in range(peers):
        fours.setdefault(i & ~(bit_x | bit_y), []).append(i)
        rests.setdefault(i & (bit_x | bit_y), []).append(i)
    fours, rests = list(fours.values()), list(rests.values())

    def exchanged(value, members):
        came = lax.all_to_all(value, "dp", 0, 0, axis_index_groups=members, tiled=True)
        return jnp.sum(came.astype(f32), axis=0)

    inputs = images.reshape(pixels, width)
    valid = validity(bucket_shape, pixel_mask).reshape(pixels, 1)
    norms = jnp.stack([mid_gains, mid_biases], axis=1)
    gain_row, bias_row = out_gain.reshape(1, width), out_bias.reshape(1, width)
    levels_flat = thresholds.reshape(pixels, width)
    cot = head_cotangent.transpose(0, 1, 3, 2, 4).reshape(2 * image_count * side, tasks, side, lanes)
    rows_half = image_count * side
    weights = head_weights.transpose(1, 0, 2)
    half_lanes = lanes // 2
    block = 4 * lane
    blocks = width // block

    pairs = []
    for i in range(peers):
        for c, bit in enumerate((bit_x, bit_y)):
            if not i & bit:
                pairs.append([2 * i + c, 2 * (i ^ bit) + c])
    pair_cot = lax.all_gather(cot, everyone, axis=0, tiled=True, axis_index_groups=pairs)

    mid = (pixels, middle)
    whole = (pixels, width)
    pair = (2, middle)
    stat_two, stat_three = (devices, 2, middle), (devices, 3, middle)

    def scalars(*values):
        return jnp.stack(values).astype(jnp.int32)

    def task_half(half, after):
        return kernel_call(
            task_kernel,
            [((tasks, pixels, width), bf16, True)],
            big=(cot, weights),
            scalars=scalars(half),
            scratch=[
                pltpu.VMEM((tasks, rows_half, side, lanes), bf16),
                pltpu.VMEM((2 * tasks, width // 2, lanes), bf16),
                pltpu.VMEM((2 * tasks, pixels, width // 2), bf16),
            ],
            copies=5 * tasks,
            after=after,
            name="task_grad",
        )[0]

    pre_reduce, stats = kernel_call(
        reduce_kernel,
        [(mid, f32, False), (stat_three, f32, False)],
        small=(valid,),
        big=(inputs, reduce_weight),
        scratch=[pltpu.VMEM(whole, bf16), pltpu.VMEM(reduce_weight.shape, bf16)],
        copies=8,
        after=(norms,),
        name="reduce",
    )
    table_one = from_everyone(stats)
    task_mine = task_half(core, (stats,))

    padded = (3, image_count, (side + 2) * side, middle)
    pre_spatial, consts_one, stats, acts = kernel_call(
        functools.partial(spatial_kernel, side),
        [(mid, f32, False), (pair, f32, False), (stat_two, f32, False), (padded, bf16, True)],
        small=(pre_reduce, table_one, norms[0], valid),
        big=(spatial_weight,),
        scratch=[pltpu.VMEM(spatial_weight.shape, bf16), pltpu.VMEM(padded, bf16)],
        copies=10,
        after=(task_mine,),
        name="spatial",
    )
    table_two = from_everyone(stats)
    task_sent = task_half(1 - core, (stats,))
    task_other = swap_core(held_until((table_two,), task_sent)[0])

    act_spatial, consts_two, stats, pre_expand = kernel_call(
        expand_kernel,
        [(mid, bf16, False), (pair, f32, False), ((devices, 2, width), f32, True), (whole, f32, True)],
        small=(pre_spatial, table_two, table_one, norms[1], valid),
        big=(expand_weight,),
        scratch=[
            pltpu.VMEM(expand_weight.shape, bf16),
            pltpu.VMEM(whole, f32),
            pltpu.VMEM((devices, 2, width), f32),
        ],
        copies=12,
        after=(task_sent,),
        name="expand",
    )
    table_three = from_everyone(stats)
    (merged,) = kernel_call(
        drop_kernel,
        [(whole, f32, True)],
        big=(task_mine, task_other, levels_flat),
        scratch=[
            pltpu.VMEM((tasks,) + whole, bf16),
            pltpu.VMEM((tasks,) + whole, bf16),
            pltpu.VMEM(whole, jnp.int32),
            pltpu.VMEM(whole, f32),
        ],
        copies=32,
        after=(stats,),
        name="graddrop",
    )


    pair_blocks = (2, pixels, width // 4)
    x_send, y_send = 2 * (1 - my_x), 1 - my_y
    consts_three, sums, features, same, cross, grad_residual = kernel_call(
        residual_kernel,
        [
            ((2, width), f32, False),
            ((devices, 2, width), f32, True),
            (whole, bf16, True),
            (pair_blocks, bf16, True),
            (pair_blocks, bf16, True),
            (whole, f32, True),
        ],
        scalars=scalars(
            by_core(x_send, y_send),
            by_core(x_send + 1, y_send + 2),
            by_core(y_send, x_send),
            by_core(y_send + 2, x_send + 1),
        ),
        small=(table_three, table_one, gain_row, bias_row, valid),
        big=(pre_expand, inputs, merged),
        scratch=[
            pltpu.VMEM(whole, f32),
            pltpu.VMEM(whole, bf16),
            pltpu.VMEM(whole, f32),
            pltpu.VMEM(whole, bf16),
            pltpu.VMEM((4, pixels, width // 4), bf16),
            pltpu.VMEM(whole, f32),
            pltpu.VMEM((devices, 2, width), f32),
        ],
        copies=28,
        name="residual",
    )
    table_four = from_everyone(sums)
    sibling = swap_core(features)
    far = swap_first(same)
    acts, act_spatial = held_until((features,), acts, act_spatial)
    acts_sib, act_spatial_sib = swap_core(acts), swap_core(act_spatial)

    def heads(first, count, after, fills):
        return kernel_call(
            functools.partial(heads_kernel, first),
            [(cot.shape, bf16, True)],
            big=(features, sibling, weights),
            scalars=scalars(core),
            scratch=[
                pltpu.VMEM(whole, bf16),
                pltpu.VMEM(whole, bf16),
                pltpu.VMEM((count, width, lanes), bf16),
                pltpu.VMEM((count, 2, rows_half, side, lanes), bf16),
            ],
            copies=2 + 6 * count,
            after=after,
            fills=fills,
            name="heads",
        )[0]


    part_shape = (tasks, 2, width // 4, lanes)

    def weight_part(near, cores, sources, cots, added, after):
        n = len(cores)
        return kernel_call(
            functools.partial(weights_kernel, near, cores),
            [(part_shape, bf16, True)],
            big=sources + (cots,) + added,
            scalars=scalars(
                core,
                by_core(my_x, 2 * my_y),
                by_core(my_x + 2, 2 * my_y + 1),
                1 - by_core(my_x, my_y),
            ),
            scratch=[
                pltpu.VMEM((2, n, pixels, width // 4), bf16),
                pltpu.VMEM((2, width // 4, n * pixels), bf16),
                pltpu.VMEM((tasks, n, rows_half, side, lanes), bf16),
                pltpu.VMEM(part_shape, bf16),
            ],
            copies=4 * blocks + 10 * tasks,
            after=after,
            name="heads_grad",
        )[0]

    index = by_core(my_y, my_x)
    near_part = weight_part(True, (0, 1), (features, sibling), cot, (), (sums, same))
    (cross,) = held_until((near_part,), cross)
    far_cross = swap_cross(cross)
    half_part = weight_part(False, (0,), (far,), pair_cot, (near_part,), (cross,))
    heads_part = weight_part(False, (1,), (far_cross,), pair_cot, (half_part,), ())
    (heads_part,) = held_until((table_four,), heads_part)
    heads_half = lax.psum_scatter(
        heads_part.reshape(tasks, width // 2, lanes),
        everyone,
        scatter_dimension=1,
        axis_index_groups=twos,
        tiled=True,
    )

    expand_half, spatial_half = (pixels, width // 2), (pixels, middle // 2)
    out_totals, shifted_two, sums, expand_mine, expand_sent = kernel_call(
        expand_back_kernel,
        [
            ((2, width), f32, False),
            (mid, f32, False),
            (stat_two, f32, False),
            (expand_half, bf16, True),
            (expand_half, bf16, True),
        ],
        scalars=scalars(core),
        small=(consts_three, table_four, gain_row, valid, table_one, pre_spatial, consts_two, norms[1]),
        big=(grad_residual, pre_expand, expand_weight),
        scratch=[
            pltpu.VMEM(whole, f32),
            pltpu.VMEM(whole, f32),
            pltpu.VMEM(expand_weight.shape, bf16),
            pltpu.VMEM(whole, bf16),
        ],
        copies=14,
        after=(heads_part,),
        name="expand_back",
    )
    table_five = from_everyone(sums)
    expand_sib = swap_core(expand_sent)
    totals_two, shifted_one, sums, spatial_mine, spatial_sent = kernel_call(
        functools.partial(spatial_back_kernel, side),
        [
            (pair, f32, False),
            (mid, f32, False),
            (stat_two, f32, False),
            (spatial_half, bf16, True),
            (spatial_half, bf16, True),
        ],
        scalars=scalars(core),
        small=(
            shifted_two, pre_spatial, consts_two, table_five, norms[1], valid, table_one,
            pre_reduce, consts_one, norms[0],
        ),
        big=(spatial_weight,),
        scratch=[
            pltpu.VMEM(spatial_weight.shape, bf16),
            pltpu.VMEM(padded, bf16),
            pltpu.VMEM(mid, bf16),
        ],
        copies=11,
        name="spatial_back",
    )
    table_six = from_everyone(sums)
    spatial_sib = swap_core(spatial_sent)
    x_out, y_out, x_in, y_in = 1 - my_x, 2 * (1 - my_y), my_x, 2 * my_y
    pair_parts = (
        by_core(x_out, y_out),
        by_core(x_out + 2, y_out + 1),
        by_core(x_in, y_in),
        by_core(x_in + 2, y_in + 1),
    )
    high, rows_of_pair = peers >> (low + 2), (1 << low) * (middle // peers)
    early_shape = (2, blocks + 9, high, rows_of_pair, middle // 2)
    early_sent, early_kept = kernel_call(
        functools.partial(trunk_weights_kernel, side),
        [(early_shape, bf16, True), (early_shape, bf16, True)],
        scalars=scalars(*pair_parts),
        small=(act_spatial, act_spatial_sib, spatial_mine, spatial_sib),
        big=(acts, acts_sib, expand_mine, expand_sib),
        scratch=[
            pltpu.VMEM((2,) + padded, bf16),
            pltpu.VMEM((2,) + expand_half, bf16),
            pltpu.VMEM((blocks + 9, high, 4, rows_of_pair, middle // 2), bf16),
        ],
        copies=4 + 4 * (blocks + 9),
        after=(sums,),
        name="trunk_weights",
    )
    (early_sent,) = held_until((table_six,), early_sent)
    early_came = swap_first(early_sent)
    dp_rows = (peers, width // devices, middle)
    totals_one, images_grad, reduce_sent, reduce_kept = kernel_call(
        reduce_back_kernel,
        [(pair, f32, False), (whole, f32, True), (dp_rows, bf16, True), (dp_rows, bf16, True)],
        scalars=scalars(core),
        small=(shifted_one, pre_reduce, consts_one, table_six, norms[0], valid, table_one),
        big=(reduce_weight, grad_residual, inputs),
        scratch=[
            pltpu.VMEM(mid, bf16),
            pltpu.VMEM(reduce_weight.shape, bf16),
            pltpu.VMEM(whole, f32),
            pltpu.VMEM(whole, bf16),
            pltpu.VMEM((peers, 2, width // devices, middle), bf16),
        ],
        copies=24,
        after=(early_kept,),
        name="reduce_back",
    )
    reduce_came = swap_core(reduce_sent)
    (heads_half,) = held_until((reduce_kept,), heads_half)
    heads_grad = lax.psum_scatter(
        heads_half, "dp", scatter_dimension=1, axis_index_groups=rests, tiled=True
    )
    heads_grad = heads_grad.astype(f32)
    quarters = (high, 4, (1 << low) * dp_rows[1], middle)
    reduce_sent, reduce_kept = halved(
        [(reduce_kept.reshape(quarters), reduce_came.reshape(quarters), 1, pair_parts)]
    )
    reduce_came = swap_first(reduce_sent)
    head_values = heads(0, 2, (reduce_kept,), False)
    early_sent, early_kept, reduce_sent, reduce_kept = halved(
        [
            (early_kept, early_came, 0, (1 - index, index)),
            (reduce_kept, reduce_came, 1, (1 - index, index)),
        ],
        (head_values,),
    )
    early_came, reduce_came = swap_second(early_sent), swap_second(reduce_sent)
    head_values = heads(2, tasks - 2, (head_values, reduce_kept), True)
    head_output = head_values.reshape(2 * image_count, side, tasks, side, lanes).transpose(0, 1, 3, 2, 4)
    early = (early_kept.astype(f32) + early_came.astype(f32)).astype(bf16)
    early = early.reshape(blocks + 9, peers // 4, -1, middle // 2).transpose(1, 0, 2, 3)
    late = (reduce_kept.astype(f32) + reduce_came.astype(f32)).astype(bf16)
    late = late.reshape(peers // 4, -1, 2, middle // 2).transpose(0, 2, 1, 3)
    both = jnp.concatenate(
        [early.reshape(peers // 4, -1, middle // 2), late.reshape(peers // 4, -1, middle // 2)], axis=1
    )
    came = lax.all_to_all(both, "dp", 0, 0, axis_index_groups=rests, tiled=True)
    (came,) = held_until((head_values, heads_grad), came)
    both = jnp.sum(came.astype(f32), axis=0)
    heads_grad = heads_grad.transpose(1, 0, 2)
    split = (blocks + 9) * (middle // peers)
    early = both[:split].reshape(blocks + 9, -1, middle // 2)
    reduce_grad = both[split:].reshape(2, -1, middle // 2).transpose(1, 0, 2).reshape(-1, middle)

    own_rows = early.reshape(early.shape[0], 2, -1, early.shape[2])
    came_rows = swap_core(pick(own_rows, 1, 1 - core))
    own_rows = pick(own_rows, 1, core)
    halves = jnp.stack(
        [jnp.where(core == 0, own_rows, came_rows), jnp.where(core == 0, came_rows, own_rows)]
    ).astype(f32)
    expand_grad = halves[:, :blocks].transpose(2, 0, 1, 3).reshape(middle // devices, width)
    spatial_grad = halves[:, blocks:].transpose(1, 2, 0, 3).reshape(9, middle // devices, middle)
    gains_grad = jnp.stack([totals_one[1], totals_two[1]], axis=0)
    biases_grad = jnp.stack([totals_one[0], totals_two[0]], axis=0)
    return (
        head_output,
        images_grad.reshape(images.shape),
        reduce_grad,
        spatial_grad,
        expand_grad,
        gains_grad,
        biases_grad,
        out_totals[1],
        out_totals[0],
        heads_grad,
    )


def solution(mesh):
    placed = (
        P(("dp", "task"), None, None, None),
        P(("dp", "task"), None),
        P(("dp", "task"), None, None),
        P(("dp", "task"), None, None, None),
        P(),
        P(),
        P(),
        P(),
        P(),
        P(),
        P(),
        P(None, None, "task"),
        P("dp", None, None, None, "task"),
    )
    return jax.shard_map(
        on_device,
        mesh=mesh,
        in_specs=placed,
        out_specs=(
            P("dp", None, None, None, "task"),
            P(("dp", "task"), None, None, None),
            P(("dp", "task"), None),
            P(None, ("dp", "task"), None),
            P(("dp", "task"), None),
            P(),
            P(),
            P(),
            P(),
            P("dp", None, "task"),
        ),
        check_vma=False,
    )
```

```python
import functools

import jax
import jax.numpy as jnp
from jax import lax
from jax.experimental import pallas as pl
from jax.experimental.pallas import tpu as pltpu
from jax.sharding import PartitionSpec as P

epsilon = 1e-05
steepness = 6.0
levels = 4096.0
everyone = ("dp", "task")
f32 = jnp.float32
bf16 = jnp.bfloat16
lane = 128
MIB = 1 << 20


def dot(left, right, contract):
    return lax.dot_general(
        left, right, ((contract[0:1], contract[1:2]), ((), ())), preferred_element_type=f32
    )


def kernel_call(body, outs, small=(), big=(), scalars=None, scratch=(), copies=0, after=(), fills=False, name=None):
    skipped = len(after)

    def ordered(*refs):
        body(*refs[skipped:])

    big = [pltpu.with_memory_space_constraint(array, pltpu.HBM) for array in big]
    there = pl.BlockSpec(memory_space=pl.ANY)
    here = pl.BlockSpec(memory_space=pltpu.VMEM)
    given = [] if scalars is None else [scalars]
    return pl.pallas_call(
        ordered,
        in_specs=[there] * skipped
        + [pl.BlockSpec(memory_space=pltpu.SMEM)] * len(given)
        + [here] * len(small)
        + [there] * len(big),
        out_specs=[there if streamed else here for _, _, streamed in outs],
        out_shape=[
            pltpu.HBM(shape, dtype) if streamed else jax.ShapeDtypeStruct(shape, dtype)
            for shape, dtype, streamed in outs
        ],
        scratch_shapes=list(scratch) + ([pltpu.SemaphoreType.DMA((copies,))] if copies else []),
        input_output_aliases={0: 0} if fills else {},
        compiler_params=pltpu.CompilerParams(vmem_limit_bytes=48 * MIB),
        name=name,
    )(*after, *given, *small, *big)


def held_until(after, *values):
    def body(*refs):
        pass

    there = pl.BlockSpec(memory_space=pl.ANY)
    return pl.pallas_call(
        body,
        in_specs=[there] * (len(values) + len(after)),
        out_specs=[there] * len(values),
        out_shape=[jax.ShapeDtypeStruct(v.shape, v.dtype) for v in values],
        input_output_aliases={i: i for i in range(len(values))},
        name="held",
    )(*values, *after)


class Copies:
    def __init__(self, sems):
        self.sems = sems
        self.used = 0
        self.open = []

    def start(self, source, target):
        copy = pltpu.make_async_copy(source, target, self.sems.at[self.used])
        self.used += 1
        copy.start()
        return copy

    def out(self, source, target):
        self.open.append(self.start(source, target))

    def finish(self):
        for copy in self.open:
            copy.wait()


def columns(ref, index, size):
    return ref.at[:, index * size : (index + 1) * size]


def sigmoid(value):
    return 0.5 + 0.5 * jnp.tanh(0.5 * value)


def combined(table, counts):
    counts = counts[:, 0:1]
    total = jnp.sum(counts)
    center = jnp.sum(table[:, 0, :], axis=0, keepdims=True) / total
    shift = table[:, 0, :] / jnp.maximum(counts, 1.0) - center
    variance = (
        jnp.sum(table[:, 1, :] + counts * shift * shift, axis=0, keepdims=True) / total
    )
    return center, lax.rsqrt(variance + epsilon)


def store_rows(stats_ref, rows, at=slice(None)):
    table = jnp.concatenate(rows, axis=0)
    stats_ref[:, :, at] = jnp.broadcast_to(table[None], (stats_ref.shape[0],) + table.shape)


def store_moments(stats_ref, values_ref, valid_ref, at=slice(None)):
    valid, values = valid_ref[...], values_ref[...]
    count = jnp.sum(valid)
    first = jnp.sum(values * valid, axis=0, keepdims=True)
    deviation = (values - first / jnp.maximum(count, 1.0)) * valid
    rows = [first, jnp.sum(deviation * deviation, axis=0, keepdims=True)]
    if stats_ref.shape[1] > 2:
        rows.append(jnp.broadcast_to(count, first.shape))
    store_rows(stats_ref, rows, at)


def store_sums(stats_ref, grad, normed, at=slice(None)):
    rows = [jnp.sum(grad, axis=0, keepdims=True), jnp.sum(grad * normed, axis=0, keepdims=True)]
    store_rows(stats_ref, rows, at)


def reduce_kernel(valid_ref, x_ref, w_ref, out_ref, stats_ref, x_buf, w_buf, sems):
    copies = Copies(sems)
    parts = 4
    size = x_ref.shape[1] // parts
    arriving = []
    for k in range(parts):
        arriving.append(
            (
                copies.start(columns(x_ref, k, size), columns(x_buf, k, size)),
                copies.start(w_ref.at[k * size : (k + 1) * size], w_buf.at[k * size : (k + 1) * size]),
            )
        )
    total = None
    for k, pair in enumerate(arriving):
        for copy in pair:
            copy.wait()
        part = dot(x_buf[:, k * size : (k + 1) * size], w_buf[k * size : (k + 1) * size, :], (1, 0))
        total = part if total is None else total + part
    out_ref[...] = total * valid_ref[...]
    store_moments(stats_ref, out_ref, valid_ref)


def pad_edges(acts_ref, side):
    images = acts_ref.shape[1]
    zeros = jnp.zeros((side, acts_ref.shape[3]), bf16)
    for shift in range(3):
        for image in range(images):
            acts_ref[shift, image, 0:side, :] = zeros
            acts_ref[shift, image, (side + 1) * side : (side + 2) * side, :] = zeros


def store_shifted(acts_ref, values, side):
    pixels = values.shape[0]
    column = lax.broadcasted_iota(jnp.int32, (pixels, 1), 0) % side
    before = jnp.where(column == 0, 0.0, pltpu.roll(values, 1, 0))
    after = jnp.where(column == side - 1, 0.0, pltpu.roll(values, pixels - 1, 0))
    for shift, moved in enumerate((before, values, after)):
        for image in range(acts_ref.shape[1]):
            rows = slice(image * side * side, (image + 1) * side * side)
            acts_ref[shift, image, side : side + side * side, :] = moved[rows].astype(bf16)


def window(acts_ref, row_shift, col_shift, side):
    images = acts_ref.shape[1]
    tile = acts_ref[col_shift, :, row_shift * side : row_shift * side + side * side, :]
    return tile.reshape(images * side * side, acts_ref.shape[3])


def spatial_kernel(
    side, pre_ref, table_ref, norm_ref, valid_ref, w_ref, out_ref, consts_ref, stats_ref, acts_out, w_buf, acts_ref, sems
):
    copies = Copies(sems)
    arriving = [copies.start(w_ref.at[k], w_buf.at[k]) for k in range(9)]
    center, inverse = combined(table_ref, table_ref[:, 2, :])
    consts_ref[0:1, :] = center
    consts_ref[1:2, :] = inverse
    gain, bias = norm_ref[0:1, :], norm_ref[1:2, :]
    pad_edges(acts_ref, side)

    shifted = gain * ((pre_ref[...] - center) * inverse) + bias
    store_shifted(acts_ref, valid_ref[...] * shifted * sigmoid(shifted), side)
    copies.out(acts_ref, acts_out)
    total = None
    for tap in range(9):
        arriving[tap].wait()
        part = dot(window(acts_ref, tap // 3, tap % 3, side), w_buf[tap], (1, 0))
        total = part if total is None else total + part
    out_ref[...] = total
    store_moments(stats_ref, out_ref, valid_ref)
    copies.finish()


def expand_kernel(
    pre_ref, table_ref, first_ref, norm_ref, valid_ref, w_ref, act_ref, consts_ref, stats_out, out,
    w_buf, out_buf, stats_ref, sems,
):
    copies = Copies(sems)
    parts = 4
    size = w_ref.shape[1] // parts
    arriving = [copies.start(columns(w_ref, k, size), columns(w_buf, k, size)) for k in range(parts)]
    center, inverse = combined(table_ref, first_ref[:, 2, :])
    consts_ref[0:1, :] = center
    consts_ref[1:2, :] = inverse
    gain, bias = norm_ref[0:1, :], norm_ref[1:2, :]

    shifted = gain * ((pre_ref[...] - center) * inverse) + bias
    act_ref[...] = (valid_ref[...] * shifted * sigmoid(shifted)).astype(bf16)
    for k in range(parts):
        at = slice(k * size, (k + 1) * size)
        arriving[k].wait()
        out_buf[:, at] = dot(act_ref[...], w_buf[:, at], (1, 0))
        copies.out(columns(out_buf, k, size), columns(out, k, size))
        store_moments(stats_ref, columns(out_buf, k, size), valid_ref, at)
        copies.out(stats_ref.at[:, :, at], stats_out.at[:, :, at])
    copies.finish()


def residual_kernel(
    which_ref, table_ref, first_ref, gain_ref, bias_ref, valid_ref, pre_ref, x_ref, merged_ref,
    consts_ref, sums_out, feat_out, same_out, cross_out, grad_out,
    pre_buf, x_buf, merged_buf, feat_buf, block_buf, grad_buf, sums_ref, sems,
):
    copies = Copies(sems)
    parts = 4
    size = pre_ref.shape[1] // parts
    arriving = []
    for k in range(parts):
        arriving.append(
            [
                copies.start(columns(ref, k, size), columns(buf, k, size))
                for ref, buf in ((pre_ref, pre_buf), (x_ref, x_buf), (merged_ref, merged_buf))
            ]
        )
    for k in range(parts):
        at = slice(k * size, (k + 1) * size)
        center, inverse = combined(table_ref[:, :, at], first_ref[:, 2, :])
        consts_ref[0:1, at] = center
        consts_ref[1:2, at] = inverse
        gain, bias = gain_ref[:, at], bias_ref[:, at]
        for copy in arriving[k]:
            copy.wait()

        valid = valid_ref[...]
        normed = (pre_buf[:, at] - center) * inverse
        value = x_buf[:, at].astype(f32) + gain * normed + bias
        sigma = sigmoid(value)
        features = (valid * (value * sigma)).astype(bf16)
        feat_buf[:, at] = features
        for piece in range(4):
            block_buf[2 * (piece % 2) + piece // 2, :, k * lane : (k + 1) * lane] = features[
                :, piece * lane : (piece + 1) * lane
            ]
        grad = merged_buf[:, at] * valid * (sigma * (1.0 + value * (1.0 - sigma)))
        grad_buf[:, at] = grad
        store_sums(sums_ref, grad, normed, at)
        copies.out(sums_ref.at[:, :, at], sums_out.at[:, :, at])
        copies.out(columns(grad_buf, k, size), columns(grad_out, k, size))
        copies.out(columns(feat_buf, k, size), columns(feat_out, k, size))
    for j in range(2):
        copies.out(block_buf.at[which_ref[j]], same_out.at[j])
        copies.out(block_buf.at[which_ref[2 + j]], cross_out.at[j])
    copies.finish()


def slope_rows(grad, pre_ref, consts_ref, norm_ref, valid_ref, out_ref, sums_ref):
    center, inverse = consts_ref[0:1, :], consts_ref[1:2, :]
    gain, bias = norm_ref[0:1, :], norm_ref[1:2, :]
    normed = (pre_ref[...] - center) * inverse
    value = gain * normed + bias
    sigma = sigmoid(value)
    grad = grad * valid_ref[...] * (sigma * (1.0 + value * (1.0 - sigma)))
    out_ref[...] = grad
    store_sums(sums_ref, grad, normed)


def expand_back_kernel(
    which_ref, consts_ref, table_ref, gain_ref, valid_ref, first_ref, mid_pre_ref, mid_consts_ref, mid_norm_ref,
    grad_ref, pre_ref, w_ref,
    totals_ref, shifted_ref, sums_ref, mine_out, sent_out,
    grad_buf, pre_buf, w_buf, out_buf, sems,
):
    copies = Copies(sems)
    parts = 4
    size = pre_ref.shape[1] // parts
    arriving = []
    for k in range(parts):
        arriving.append(
            [
                copies.start(columns(ref, k, size), columns(buf, k, size))
                for ref, buf in ((grad_ref, grad_buf), (pre_ref, pre_buf), (w_ref, w_buf))
            ]
        )
    count = jnp.sum(first_ref[:, 2, 0:1])
    total = None
    for k in range(parts):
        at = slice(k * size, (k + 1) * size)
        totals = jnp.sum(table_ref[:, :, at], axis=0)
        totals_ref[:, at] = totals
        center, inverse = consts_ref[0:1, at], consts_ref[1:2, at]
        plain, scaled = totals[0:1, :] / count, totals[1:2, :] / count
        scale = gain_ref[:, at] * inverse
        for copy in arriving[k]:
            copy.wait()

        normed = (pre_buf[:, at] - center) * inverse
        grad = scale * (grad_buf[:, at] - valid_ref[...] * (plain + normed * scaled))
        out_buf[:, at] = grad.astype(bf16)
        part = dot(out_buf[:, at], w_buf[:, at], (1, 1))
        total = part if total is None else total + part
    half = out_buf.shape[1] // 2
    for place, out in ((which_ref[0], mine_out), (1 - which_ref[0], sent_out)):
        copies.out(out_buf.at[:, pl.ds(pl.multiple_of(place * half, half), half)], out)
    slope_rows(total, mid_pre_ref, mid_consts_ref, mid_norm_ref, valid_ref, shifted_ref, sums_ref)
    copies.finish()


def spatial_back_kernel(
    side, which_ref, grad_ref, pre_ref, consts_ref, table_ref, norm_ref, valid_ref, first_ref,
    low_pre_ref, low_consts_ref, low_norm_ref, w_ref,
    totals_ref, shifted_ref, sums_ref, mine_out, sent_out,
    w_buf, acts_ref, out_ref, sems,
):
    copies = Copies(sems)
    arriving = [copies.start(w_ref.at[k], w_buf.at[k]) for k in range(9)]
    count = jnp.sum(first_ref[:, 2, 0:1])
    totals = jnp.sum(table_ref[...], axis=0)
    totals_ref[...] = totals
    center, inverse = consts_ref[0:1, :], consts_ref[1:2, :]
    plain, scaled = totals[0:1, :] / count, totals[1:2, :] / count
    scale = norm_ref[0:1, :] * inverse
    pad_edges(acts_ref, side)

    normed = (pre_ref[...] - center) * inverse
    grad = scale * (grad_ref[...] - valid_ref[...] * (plain + normed * scaled))
    out_ref[...] = grad.astype(bf16)
    half = out_ref.shape[1] // 2
    for place, out in ((which_ref[0], mine_out), (1 - which_ref[0], sent_out)):
        copies.out(out_ref.at[:, pl.ds(pl.multiple_of(place * half, half), half)], out)
    store_shifted(acts_ref, grad, side)
    total = None
    for tap in range(9):
        arriving[tap].wait()
        part = dot(window(acts_ref, 2 - tap // 3, 2 - tap % 3, side), w_buf[tap], (1, 1))
        total = part if total is None else total + part
    slope_rows(total, low_pre_ref, low_consts_ref, low_norm_ref, valid_ref, shifted_ref, sums_ref)
    copies.finish()


def reduce_back_kernel(
    which_ref, grad_ref, pre_ref, consts_ref, table_ref, norm_ref, valid_ref, first_ref, w_ref, res_ref, x_ref,
    totals_ref, images_out, sent_out, kept_out,
    low_buf, w_buf, res_buf, x_buf, part_buf, sems,
):
    copies = Copies(sems)
    parts = 4
    size = res_ref.shape[1] // parts
    arriving = []
    for k in range(parts):
        at = slice(k * size, (k + 1) * size)
        arriving.append(
            [
                copies.start(columns(x_ref, k, size), columns(x_buf, k, size)),
                copies.start(w_ref.at[at], w_buf.at[at]),
                copies.start(columns(res_ref, k, size), columns(res_buf, k, size)),
            ]
        )
    count = jnp.sum(first_ref[:, 2, 0:1])
    totals = jnp.sum(table_ref[...], axis=0)
    totals_ref[...] = totals
    center, inverse = consts_ref[0:1, :], consts_ref[1:2, :]
    plain, scaled = totals[0:1, :] / count, totals[1:2, :] / count
    scale = norm_ref[0:1, :] * inverse

    normed = (pre_ref[...] - center) * inverse
    grad = scale * (grad_ref[...] - valid_ref[...] * (plain + normed * scaled))
    low_buf[...] = grad.astype(bf16)
    for k in range(parts):
        at = slice(k * size, (k + 1) * size)
        arriving[k][0].wait()
        value = dot(x_buf[:, at], low_buf[...], (0, 0)).astype(bf16)
        peers = part_buf.shape[0] // parts
        dp = slice(k * peers, (k + 1) * peers)
        part_buf[dp] = value.reshape((peers,) + part_buf.shape[1:])
        copies.out(part_buf.at[dp, 1 - which_ref[0]], sent_out.at[dp])
        copies.out(part_buf.at[dp, which_ref[0]], kept_out.at[dp])
    for k in range(parts):
        at = slice(k * size, (k + 1) * size)
        arriving[k][1].wait()
        arriving[k][2].wait()
        res_buf[:, at] = res_buf[:, at] + valid_ref[...] * dot(low_buf[...], w_buf[at, :], (1, 1))
        copies.out(columns(res_buf, k, size), columns(images_out, k, size))
    copies.finish()


def trunk_weights_kernel(
    side, which_ref, act_ref, act_sib, right_ref, right_sib, acts_ref, acts_sib, grad_ref, grad_sib,
    sent_out, kept_out, acts_buf, grad_buf, out_buf, sems,
):
    copies = Copies(sems)
    size = right_ref.shape[1]
    blocks = grad_ref.shape[1] // size
    grads = [copies.start(ref, grad_buf.at[c]) for c, ref in enumerate((grad_ref, grad_sib))]
    acts = [copies.start(ref, acts_buf.at[c]) for c, ref in enumerate((acts_ref, acts_sib))]

    def store(place, value):
        out_buf[place] = value.astype(bf16).reshape(out_buf.shape[1:])
        for q in range(2):
            copies.out(out_buf.at[place, :, which_ref[q]], sent_out.at[q, place])
            copies.out(out_buf.at[place, :, which_ref[2 + q]], kept_out.at[q, place])

    for copy in grads:
        copy.wait()
    for b in range(blocks):
        at = slice(b * size, (b + 1) * size)
        store(b, dot(act_ref[...], grad_buf[0, :, at], (0, 0)) + dot(act_sib[...], grad_buf[1, :, at], (0, 0)))
    for copy in acts:
        copy.wait()
    for tap in range(9):
        tiles = [window(acts_buf.at[c], tap // 3, tap % 3, side) for c in range(2)]
        store(blocks + tap, dot(tiles[0], right_ref[...], (0, 0)) + dot(tiles[1], right_sib[...], (0, 0)))
    copies.finish()


def halve_kernel(axes, which_ref, *refs):
    n = len(axes)
    ins, outs, bufs, sems = refs[: 2 * n], refs[2 * n : 4 * n], refs[4 * n : 6 * n], refs[6 * n]
    copies = Copies(sems)
    arriving = [copies.start(ref, buf) for ref, buf in zip(ins, bufs)]
    first = 0
    for p, axis in enumerate(axes):
        kept_buf, came_buf = bufs[2 * p : 2 * p + 2]
        arriving[2 * p].wait()
        arriving[2 * p + 1].wait()
        kept_buf[...] = (kept_buf[...].astype(f32) + came_buf[...].astype(f32)).astype(bf16)
        count = kept_buf.shape[axis] // 2
        lead = (slice(None),) * axis
        for out in outs[2 * p : 2 * p + 2]:
            for i in range(count):
                target = lead + ((i,) if count > 1 else ())
                copies.out(kept_buf.at[lead + (which_ref[first],)], out.at[target] if target else out)
                first = first + 1
    copies.finish()


def task_kernel(half_ref, cot_ref, w_ref, out, cot_buf, w_buf, out_buf, sems):
    copies = Copies(sems)
    tasks, pixels = out.shape[:2]
    size = w_buf.shape[1]
    parts = w_ref.shape[1] // size
    rows = cot_buf.shape[1]
    start = pl.multiple_of(half_ref[0] * rows, rows)
    cots, arriving = [], []
    for t in range(tasks):
        cots.append(copies.start(cot_ref.at[pl.ds(start, rows), t], cot_buf.at[t]))
        for j in range(parts):
            arriving.append(copies.start(w_ref.at[t, j * size : (j + 1) * size], w_buf.at[t * parts + j]))
    for t in range(tasks):
        cots[t].wait()
        for j in range(parts):
            slot = t * parts + j
            arriving[slot].wait()
            cot = cot_buf[t].reshape(pixels, cot_buf.shape[3])
            out_buf[slot] = dot(cot, w_buf[slot], (1, 1)).astype(bf16)
            copies.out(out_buf.at[slot], out.at[t, :, j * size : (j + 1) * size])
    copies.finish()


def drop_kernel(mine_ref, other_ref, level_ref, out, mine_buf, other_buf, level_buf, out_buf, sems):
    copies = Copies(sems)
    tasks, pixels, _ = mine_ref.shape
    parts = 8
    size = pixels // parts
    arriving = []
    for k in range(parts):
        at = slice(k * size, (k + 1) * size)
        arriving.append(
            [
                copies.start(mine_ref.at[:, at], mine_buf.at[:, at]),
                copies.start(other_ref.at[:, at], other_buf.at[:, at]),
                copies.start(level_ref.at[at], level_buf.at[at]),
            ]
        )
    for k in range(parts):
        for copy in arriving[k]:
            copy.wait()

        rows = slice(k * size, (k + 1) * size)
        grads = [mine_buf[t, rows].astype(f32) + other_buf[t, rows].astype(f32) for t in range(tasks)]
        total, spread = None, None
        for grad in grads:
            squared = grad * grad + 1.0
            root = squared * lax.rsqrt(squared)
            spread = root if spread is None else spread + root
            total = grad if total is None else total + grad
        margin = (0.25 * steepness) * (total / spread) + (
            0.25 * steepness * (1.0 - 1.0 / levels)
            - level_buf[rows].astype(f32) * (0.5 * steepness / levels)
        )
        merged = total
        for grad in grads:
            merged = merged + grad * jnp.tanh(jnp.tanh(grad) * margin)
        out_buf[rows] = 0.5 * merged
        at = slice(k * size, (k + 1) * size)
        copies.out(out_buf.at[at], out.at[at])
    copies.finish()


def heads_kernel(first, which_ref, own_ref, sib_ref, w_ref, out, own_buf, sib_buf, w_buf, out_buf, sems):
    copies = Copies(sems)
    core = which_ref[0]
    tasks = w_buf.shape[0]
    lanes = w_ref.shape[2]
    size = lanes // 2
    rows = out.shape[0] // 2
    arriving = []
    features = []
    for t in range(tasks):
        for j in range(2):
            at = slice(j * size, (j + 1) * size)
            arriving.append(copies.start(w_ref.at[first + t, :, at], w_buf.at[t, :, at]))
            if not features:
                features = [copies.start(own_ref, own_buf), copies.start(sib_ref, sib_buf)]
    for t in range(tasks):
        for j in range(2):
            at = slice(j * size, (j + 1) * size)
            arriving[2 * t + j].wait()
            for s, (source, place) in enumerate(((own_buf, core), (sib_buf, 1 - core))):
                if t + j == 0:
                    features[s].wait()
                value = dot(source[...], w_buf[t, :, at], (1, 0)).astype(bf16)
                out_buf[t, s, :, :, at] = value.reshape(rows, out.shape[2], size)
                copies.out(
                    out_buf.at[t, s, :, :, at],
                    out.at[pl.ds(pl.multiple_of(place * rows, rows), rows), first + t, :, at],
                )
    copies.finish()


def weights_kernel(near, cores, which_ref, *refs):
    sources, cot_ref, refs = refs[: len(cores)], refs[len(cores)], refs[len(cores) + 1 :]
    added_ref, refs = (None, refs) if near else (refs[0], refs[1:])
    out, feat_buf, flip_buf, cot_buf, out_buf, sems = refs
    copies = Copies(sems)
    core = which_ref[0]
    tasks = out.shape[0]
    pixels, channels = feat_buf.shape[2:]
    pieces = channels // lane
    lanes = cot_buf.shape[4]
    rows = cot_buf.shape[2]
    features = []
    for j in range(2):
        for s, ref in enumerate(sources):
            if near:
                features.append(
                    [
                        copies.start(
                            ref.at[:, pl.ds(pl.multiple_of((4 * piece + which_ref[1 + j]) * lane, lane), lane)],
                            feat_buf.at[j, s, :, piece * lane : (piece + 1) * lane],
                        )
                        for piece in range(pieces)
                    ]
                )
            else:
                features.append([copies.start(ref.at[j], feat_buf.at[j, s])])
    start = 0 if near else which_ref[3] * (2 * rows)
    cots, more = [], []
    for t in range(tasks):
        cots.append(
            [
                copies.start(
                    cot_ref.at[pl.ds(pl.multiple_of(start + place * rows, rows), rows), t], cot_buf.at[t, s]
                )
                for s, place in enumerate([core if c == 0 else 1 - core for c in cores])
            ]
        )
        if not near:
            more.append([copies.start(added_ref.at[t, j], out_buf.at[t, j]) for j in range(2)])
    for t in range(tasks):
        for j in range(2):
            if t == 0:
                for s in range(len(cores)):
                    for copy in features[len(cores) * j + s]:
                        copy.wait()
                    flip_buf[j, :, s * pixels : (s + 1) * pixels] = feat_buf[j, s].T
            if j == 0:
                for copy in cots[t]:
                    copy.wait()
            value = dot(flip_buf[j], cot_buf[t].reshape(len(cores) * pixels, lanes), (1, 0))
            if not near:
                more[t][j].wait()
                value = value + out_buf[t, j].astype(f32)
            out_buf[t, j] = value.astype(bf16)
            copies.out(out_buf.at[t, j], out.at[t, j])
    copies.finish()


def validity(bucket_shape, pixel_mask):
    row_index = lax.broadcasted_iota(jnp.int32, pixel_mask.shape, 1)
    col_index = lax.broadcasted_iota(jnp.int32, pixel_mask.shape, 2)
    inside = (row_index < bucket_shape[:, 0][:, None, None]) & (
        col_index < bucket_shape[:, 1][:, None, None]
    )
    return jnp.where(inside, pixel_mask, 0).astype(f32)


def from_everyone(rows):
    return lax.all_to_all(rows, everyone, 0, 0, tiled=True)


def swap_core(value):
    return lax.ppermute(value, "task", [(0, 1), (1, 0)])


def pick(value, axis, index):
    return lax.dynamic_index_in_dim(value, index, axis, keepdims=False)


def two(value, axis, first, second):
    return jnp.stack([pick(value, axis, first), pick(value, axis, second)], axis)


def on_device(
    images,
    bucket_shape,
    pixel_mask,
    thresholds,
    reduce_weight,
    spatial_weight,
    expand_weight,
    mid_gains,
    mid_biases,
    out_gain,
    out_bias,
    head_weights,
    head_cotangent,
):
    image_count = images.shape[0]
    side = images.shape[1]
    width = images.shape[3]
    middle = reduce_weight.shape[1]
    tasks = head_weights.shape[1]
    lanes = head_weights.shape[2]
    pixels = image_count * side * side
    peers = lax.axis_size("dp")
    devices = 2 * peers
    core = lax.axis_index("task")
    low = max(0, (lane * peers // width).bit_length() - 1)
    bit_x, bit_y = 1 << low, 2 << low
    position = lax.axis_index("dp")
    my_x, my_y = (position >> low) & 1, (position >> (low + 1)) & 1
    def pairing(bit_of, cross):
        pairs = []
        for i in range(peers):
            for c in range(2):
                if cross:
                    pairs.append((2 * i + c, 2 * (i ^ bit_of[1 - c]) + 1 - c))
                else:
                    pairs.append((2 * i + c, 2 * (i ^ bit_of[c]) + c))
        return pairs

    def swap_first(value):
        return lax.ppermute(value, everyone, pairing((bit_x, bit_y), False))

    def swap_second(value):
        return lax.ppermute(value, everyone, pairing((bit_y, bit_x), False))

    def swap_cross(value):
        return lax.ppermute(value, everyone, pairing((bit_x, bit_y), True))

    def by_core(zero, one):
        return jnp.where(core == 0, zero, one)

    twos = []
    for i in range(peers):
        for c, bit in enumerate((bit_y, bit_x)):
            if not i & bit:
                twos.append([2 * i + c, 2 * (i | bit) + c])
    rest_bits = [b for b in range(peers.bit_length() - 1) if not (1 << b) & (bit_x | bit_y)]

    def swap_rest(value, done):
        bit = rest_bits[done]
        return lax.ppermute(value, "dp", [(i, i ^ (1 << bit)) for i in range(peers)])

    def halved(pairs, after=()):
        outs, scratch, big, which, count = [], [], [], [], 0
        for kept, came, axis, indices in pairs:
            half = kept.shape[axis] // 2
            shape = kept.shape[:axis] + ((half,) if half > 1 else ()) + kept.shape[axis + 1 :]
            outs += [(shape, bf16, True)] * 2
            scratch += [pltpu.VMEM(kept.shape, bf16)] * 2
            big += [kept, came]
            which += list(indices)
            count += 2 + 2 * half
        return kernel_call(
            functools.partial(halve_kernel, tuple(axis for _, _, axis, _ in pairs)),
            outs,
            big=tuple(big),
            scalars=scalars(*which),
            scratch=scratch,
            copies=count,
            after=after,
            name="halve",
        )

    def rest_part(kept, came, dim, done):
        mine = (position >> rest_bits[done]) & 1
        return kept, came, dim + len(rest_bits) - 1 - done, (1 - mine, mine)

    fours, rests = {}, {}
    for i in range(peers):
        fours.setdefault(i & ~(bit_x | bit_y), []).append(i)
        rests.setdefault(i & (bit_x | bit_y), []).append(i)
    fours, rests = list(fours.values()), list(rests.values())

    def exchanged(value, members):
        came = lax.all_to_all(value, "dp", 0, 0, axis_index_groups=members, tiled=True)
        return jnp.sum(came.astype(f32), axis=0)

    inputs = images.reshape(pixels, width)
    valid = validity(bucket_shape, pixel_mask).reshape(pixels, 1)
    norms = jnp.stack([mid_gains, mid_biases], axis=1)
    gain_row, bias_row = out_gain.reshape(1, width), out_bias.reshape(1, width)
    levels_flat = thresholds.reshape(pixels, width)
    cot = head_cotangent.transpose(0, 1, 3, 2, 4).reshape(2 * image_count * side, tasks, side, lanes)
    rows_half = image_count * side
    weights = head_weights.transpose(1, 0, 2)
    half_lanes = lanes // 2
    block = 4 * lane
    blocks = width // block

    pairs = []
    for i in range(peers):
        for c, bit in enumerate((bit_x, bit_y)):
            if not i & bit:
                pairs.append([2 * i + c, 2 * (i ^ bit) + c])
    pair_cot = lax.all_gather(cot, everyone, axis=0, tiled=True, axis_index_groups=pairs)

    mid = (pixels, middle)
    whole = (pixels, width)
    pair = (2, middle)
    stat_two, stat_three = (devices, 2, middle), (devices, 3, middle)

    def scalars(*values):
        return jnp.stack(values).astype(jnp.int32)

    def task_half(half, after):
        return kernel_call(
            task_kernel,
            [((tasks, pixels, width), bf16, True)],
            big=(cot, weights),
            scalars=scalars(half),
            scratch=[
                pltpu.VMEM((tasks, rows_half, side, lanes), bf16),
                pltpu.VMEM((2 * tasks, width // 2, lanes), bf16),
                pltpu.VMEM((2 * tasks, pixels, width // 2), bf16),
            ],
            copies=5 * tasks,
            after=after,
            name="task_grad",
        )[0]

    pre_reduce, stats = kernel_call(
        reduce_kernel,
        [(mid, f32, False), (stat_three, f32, False)],
        small=(valid,),
        big=(inputs, reduce_weight),
        scratch=[pltpu.VMEM(whole, bf16), pltpu.VMEM(reduce_weight.shape, bf16)],
        copies=8,
        name="reduce",
    )
    table_one = from_everyone(stats)
    task_mine = task_half(core, (stats,))

    padded = (3, image_count, (side + 2) * side, middle)
    pre_spatial, consts_one, stats, acts = kernel_call(
        functools.partial(spatial_kernel, side),
        [(mid, f32, False), (pair, f32, False), (stat_two, f32, False), (padded, bf16, True)],
        small=(pre_reduce, table_one, norms[0], valid),
        big=(spatial_weight,),
        scratch=[pltpu.VMEM(spatial_weight.shape, bf16), pltpu.VMEM(padded, bf16)],
        copies=10,
        after=(task_mine,),
        name="spatial",
    )
    table_two = from_everyone(stats)
    task_sent = task_half(1 - core, (stats,))
    task_other = swap_core(held_until((table_two,), task_sent)[0])

    act_spatial, consts_two, stats, pre_expand = kernel_call(
        expand_kernel,
        [(mid, bf16, False), (pair, f32, False), ((devices, 2, width), f32, True), (whole, f32, True)],
        small=(pre_spatial, table_two, table_one, norms[1], valid),
        big=(expand_weight,),
        scratch=[
            pltpu.VMEM(expand_weight.shape, bf16),
            pltpu.VMEM(whole, f32),
            pltpu.VMEM((devices, 2, width), f32),
        ],
        copies=12,
        after=(task_sent,),
        name="expand",
    )
    table_three = from_everyone(stats)
    (merged,) = kernel_call(
        drop_kernel,
        [(whole, f32, True)],
        big=(task_mine, task_other, levels_flat),
        scratch=[
            pltpu.VMEM((tasks,) + whole, bf16),
            pltpu.VMEM((tasks,) + whole, bf16),
            pltpu.VMEM(whole, jnp.int32),
            pltpu.VMEM(whole, f32),
        ],
        copies=32,
        after=(stats,),
        name="graddrop",
    )


    pair_blocks = (2, pixels, width // 4)
    x_send, y_send = 2 * (1 - my_x), 1 - my_y
    consts_three, sums, features, same, cross, grad_residual = kernel_call(
        residual_kernel,
        [
            ((2, width), f32, False),
            ((devices, 2, width), f32, True),
            (whole, bf16, True),
            (pair_blocks, bf16, True),
            (pair_blocks, bf16, True),
            (whole, f32, True),
        ],
        scalars=scalars(
            by_core(x_send, y_send),
            by_core(x_send + 1, y_send + 2),
            by_core(y_send, x_send),
            by_core(y_send + 2, x_send + 1),
        ),
        small=(table_three, table_one, gain_row, bias_row, valid),
        big=(pre_expand, inputs, merged),
        scratch=[
            pltpu.VMEM(whole, f32),
            pltpu.VMEM(whole, bf16),
            pltpu.VMEM(whole, f32),
            pltpu.VMEM(whole, bf16),
            pltpu.VMEM((4, pixels, width // 4), bf16),
            pltpu.VMEM(whole, f32),
            pltpu.VMEM((devices, 2, width), f32),
        ],
        copies=28,
        name="residual",
    )
    table_four = from_everyone(sums)
    sibling = swap_core(features)
    far = swap_first(same)
    acts, act_spatial = held_until((features,), acts, act_spatial)
    acts_sib, act_spatial_sib = swap_core(acts), swap_core(act_spatial)

    def heads(first, count, after, fills):
        return kernel_call(
            functools.partial(heads_kernel, first),
            [(cot.shape, bf16, True)],
            big=(features, sibling, weights),
            scalars=scalars(core),
            scratch=[
                pltpu.VMEM(whole, bf16),
                pltpu.VMEM(whole, bf16),
                pltpu.VMEM((count, width, lanes), bf16),
                pltpu.VMEM((count, 2, rows_half, side, lanes), bf16),
            ],
            copies=2 + 6 * count,
            after=after,
            fills=fills,
            name="heads",
        )[0]


    part_shape = (tasks, 2, width // 4, lanes)

    def weight_part(near, cores, sources, cots, added, after):
        n = len(cores)
        return kernel_call(
            functools.partial(weights_kernel, near, cores),
            [(part_shape, bf16, True)],
            big=sources + (cots,) + added,
            scalars=scalars(
                core,
                by_core(my_x, 2 * my_y),
                by_core(my_x + 2, 2 * my_y + 1),
                1 - by_core(my_x, my_y),
            ),
            scratch=[
                pltpu.VMEM((2, n, pixels, width // 4), bf16),
                pltpu.VMEM((2, width // 4, n * pixels), bf16),
                pltpu.VMEM((tasks, n, rows_half, side, lanes), bf16),
                pltpu.VMEM(part_shape, bf16),
            ],
            copies=4 * blocks + 10 * tasks,
            after=after,
            name="heads_grad",
        )[0]

    index = by_core(my_y, my_x)
    near_part = weight_part(True, (0, 1), (features, sibling), cot, (), (sums, same))
    (cross,) = held_until((near_part,), cross)
    far_cross = swap_cross(cross)
    half_part = weight_part(False, (0,), (far,), pair_cot, (near_part,), (cross,))
    heads_part = weight_part(False, (1,), (far_cross,), pair_cot, (half_part,), ())
    (heads_part,) = held_until((table_four,), heads_part)
    heads_half = lax.psum_scatter(
        heads_part.reshape(tasks, width // 2, lanes),
        everyone,
        scatter_dimension=1,
        axis_index_groups=twos,
        tiled=True,
    )

    expand_half, spatial_half = (pixels, width // 2), (pixels, middle // 2)
    out_totals, shifted_two, sums, expand_mine, expand_sent = kernel_call(
        expand_back_kernel,
        [
            ((2, width), f32, False),
            (mid, f32, False),
            (stat_two, f32, False),
            (expand_half, bf16, True),
            (expand_half, bf16, True),
        ],
        scalars=scalars(core),
        small=(consts_three, table_four, gain_row, valid, table_one, pre_spatial, consts_two, norms[1]),
        big=(grad_residual, pre_expand, expand_weight),
        scratch=[
            pltpu.VMEM(whole, f32),
            pltpu.VMEM(whole, f32),
            pltpu.VMEM(expand_weight.shape, bf16),
            pltpu.VMEM(whole, bf16),
        ],
        copies=14,
        after=(heads_part,),
        name="expand_back",
    )
    table_five = from_everyone(sums)
    expand_sib = swap_core(expand_sent)
    totals_two, shifted_one, sums, spatial_mine, spatial_sent = kernel_call(
        functools.partial(spatial_back_kernel, side),
        [
            (pair, f32, False),
            (mid, f32, False),
            (stat_two, f32, False),
            (spatial_half, bf16, True),
            (spatial_half, bf16, True),
        ],
        scalars=scalars(core),
        small=(
            shifted_two, pre_spatial, consts_two, table_five, norms[1], valid, table_one,
            pre_reduce, consts_one, norms[0],
        ),
        big=(spatial_weight,),
        scratch=[
            pltpu.VMEM(spatial_weight.shape, bf16),
            pltpu.VMEM(padded, bf16),
            pltpu.VMEM(mid, bf16),
        ],
        copies=11,
        name="spatial_back",
    )
    table_six = from_everyone(sums)
    spatial_sib = swap_core(spatial_sent)
    x_out, y_out, x_in, y_in = 1 - my_x, 2 * (1 - my_y), my_x, 2 * my_y
    pair_parts = (
        by_core(x_out, y_out),
        by_core(x_out + 2, y_out + 1),
        by_core(x_in, y_in),
        by_core(x_in + 2, y_in + 1),
    )
    high, rows_of_pair = peers >> (low + 2), (1 << low) * (middle // peers)
    early_shape = (2, blocks + 9, high, rows_of_pair, middle // 2)
    early_sent, early_kept = kernel_call(
        functools.partial(trunk_weights_kernel, side),
        [(early_shape, bf16, True), (early_shape, bf16, True)],
        scalars=scalars(*pair_parts),
        small=(act_spatial, act_spatial_sib, spatial_mine, spatial_sib),
        big=(acts, acts_sib, expand_mine, expand_sib),
        scratch=[
            pltpu.VMEM((2,) + padded, bf16),
            pltpu.VMEM((2,) + expand_half, bf16),
            pltpu.VMEM((blocks + 9, high, 4, rows_of_pair, middle // 2), bf16),
        ],
        copies=4 + 4 * (blocks + 9),
        after=(sums,),
        name="trunk_weights",
    )
    (early_sent,) = held_until((table_six,), early_sent)
    early_came = swap_first(early_sent)
    dp_rows = (peers, width // devices, middle)
    totals_one, images_grad, reduce_sent, reduce_kept = kernel_call(
        reduce_back_kernel,
        [(pair, f32, False), (whole, f32, True), (dp_rows, bf16, True), (dp_rows, bf16, True)],
        scalars=scalars(core),
        small=(shifted_one, pre_reduce, consts_one, table_six, norms[0], valid, table_one),
        big=(reduce_weight, grad_residual, inputs),
        scratch=[
            pltpu.VMEM(mid, bf16),
            pltpu.VMEM(reduce_weight.shape, bf16),
            pltpu.VMEM(whole, f32),
            pltpu.VMEM(whole, bf16),
            pltpu.VMEM((peers, 2, width // devices, middle), bf16),
        ],
        copies=24,
        after=(early_kept,),
        name="reduce_back",
    )
    reduce_came = swap_core(reduce_sent)
    (heads_half,) = held_until((reduce_kept,), heads_half)
    heads_grad = lax.psum_scatter(
        heads_half, "dp", scatter_dimension=1, axis_index_groups=rests, tiled=True
    )
    heads_grad = heads_grad.astype(f32)
    quarters = (high, 4, (1 << low) * dp_rows[1], middle)
    reduce_sent, reduce_kept = halved(
        [(reduce_kept.reshape(quarters), reduce_came.reshape(quarters), 1, pair_parts)]
    )
    reduce_came = swap_first(reduce_sent)
    head_values = heads(0, 2, (reduce_kept,), False)
    early_sent, early_kept, reduce_sent, reduce_kept = halved(
        [
            (early_kept, early_came, 0, (1 - index, index)),
            (reduce_kept, reduce_came, 1, (1 - index, index)),
        ],
        (head_values,),
    )
    early_came, reduce_came = swap_second(early_sent), swap_second(reduce_sent)
    head_values = heads(2, tasks - 2, (head_values, reduce_kept), True)
    head_output = head_values.reshape(2 * image_count, side, tasks, side, lanes).transpose(0, 1, 3, 2, 4)
    early = (early_kept.astype(f32) + early_came.astype(f32)).astype(bf16)
    early = early.reshape(blocks + 9, peers // 4, -1, middle // 2).transpose(1, 0, 2, 3)
    late = (reduce_kept.astype(f32) + reduce_came.astype(f32)).astype(bf16)
    late = late.reshape(peers // 4, -1, 2, middle // 2).transpose(0, 2, 1, 3)
    both = jnp.concatenate(
        [early.reshape(peers // 4, -1, middle // 2), late.reshape(peers // 4, -1, middle // 2)], axis=1
    )
    came = lax.all_to_all(both, "dp", 0, 0, axis_index_groups=rests, tiled=True)
    (came,) = held_until((head_values, heads_grad), came)
    both = jnp.sum(came.astype(f32), axis=0)
    heads_grad = heads_grad.transpose(1, 0, 2)
    split = (blocks + 9) * (middle // peers)
    early = both[:split].reshape(blocks + 9, -1, middle // 2)
    reduce_grad = both[split:].reshape(2, -1, middle // 2).transpose(1, 0, 2).reshape(-1, middle)

    own_rows = early.reshape(early.shape[0], 2, -1, early.shape[2])
    came_rows = swap_core(pick(own_rows, 1, 1 - core))
    own_rows = pick(own_rows, 1, core)
    halves = jnp.stack(
        [jnp.where(core == 0, own_rows, came_rows), jnp.where(core == 0, came_rows, own_rows)]
    ).astype(f32)
    expand_grad = halves[:, :blocks].transpose(2, 0, 1, 3).reshape(middle // devices, width)
    spatial_grad = halves[:, blocks:].transpose(1, 2, 0, 3).reshape(9, middle // devices, middle)
    gains_grad = jnp.stack([totals_one[1], totals_two[1]], axis=0)
    biases_grad = jnp.stack([totals_one[0], totals_two[0]], axis=0)
    return (
        head_output,
        images_grad.reshape(images.shape),
        reduce_grad,
        spatial_grad,
        expand_grad,
        gains_grad,
        biases_grad,
        out_totals[1],
        out_totals[0],
        heads_grad,
    )


def solution(mesh):
    placed = (
        P(("dp", "task"), None, None, None),
        P(("dp", "task"), None),
        P(("dp", "task"), None, None),
        P(("dp", "task"), None, None, None),
        P(),
        P(),
        P(),
        P(),
        P(),
        P(),
        P(),
        P(None, None, "task"),
        P("dp", None, None, None, "task"),
    )
    return jax.shard_map(
        on_device,
        mesh=mesh,
        in_specs=placed,
        out_specs=(
            P("dp", None, None, None, "task"),
            P(("dp", "task"), None, None, None),
            P(("dp", "task"), None),
            P(None, ("dp", "task"), None),
            P(("dp", "task"), None),
            P(),
            P(),
            P(),
            P(),
            P("dp", None, "task"),
        ),
        check_vma=False,
    )
```
